32 devices in a mesh: dp: 8 (over z, x), tensor: 4 (over y, core).
Axes of the slice: x: 2, y: 2, z: 4, core: 2. Of those that a mesh axis runs over, the one named last changes fastest.
Arguments:
- inputs: bfloat16 [8192, 768], P('dp'), may hold values from -6 to 6
- encoded: bfloat16 [32768, 768], P('dp'), may hold values from -6 to 6
- example_counts: int32 [8], P('dp'), may hold values from 4 to 8, as said below
- lengths: int32 [64], P('dp'), may hold values from 57 to 114, as said below
- buckets: int32 [128], replicated, may hold values from 0 to 31, as said below
- gain_self: float32 [768], replicated, may hold values from 0.1 to 1.9
- gain_cross: float32 [768], replicated, may hold values from 0.1 to 1.9
- gain_ffn: float32 [768], replicated, may hold values from 0.1 to 1.9
- bias_table: float32 [32, 12], P(None, 'tensor'), may hold values from -4 to 4
- query_self: bfloat16 [768, 768], P(None, 'tensor'), may hold values from -0.0546875 to 0.0546875
- key_self: bfloat16 [768, 768], P(None, 'tensor'), may hold values from -0.21875 to 0.21875
- value_self: bfloat16 [768, 768], P(None, 'tensor'), may hold values from -0.21875 to 0.21875
- output_self: bfloat16 [768, 768], P(None, 'tensor'), may hold values from -0.625 to 0.625
- query_cross: bfloat16 [768, 768], P(None, 'tensor'), may hold values from -0.0546875 to 0.0546875
- key_cross: bfloat16 [768, 768], P(None, 'tensor'), may hold values from -0.21875 to 0.21875
- value_cross: bfloat16 [768, 768], P(None, 'tensor'), may hold values from -0.21875 to 0.21875
- output_cross: bfloat16 [768, 768], P(None, 'tensor'), may hold values from -0.875 to 0.875
- hidden_in: bfloat16 [768, 3072], P(None, 'tensor'), may hold values from -0.21875 to 0.21875
- hidden_out: bfloat16 [768, 3072], P(None, 'tensor'), may hold values from -0.15625 to 0.15625
- out_grad: bfloat16 [8192, 768], P('dp'), may hold values from -6 to 6
Outputs:
- layer_out: bfloat16 [8192, 768], P('dp', 'tensor')
- input_grad: bfloat16 [8192, 768], P('dp', 'tensor')
- encoded_grad: bfloat16 [32768, 768], P(('dp', 'tensor'))
- grad_gain_self: float32 [768], replicated
- grad_gain_cross: float32 [768], replicated
- grad_gain_ffn: float32 [768], replicated
- grad_bias_table: float32 [32, 12], P(None, 'tensor')
- grad_query_self: float32 [768, 768], P('dp', 'tensor')
- grad_key_self: float32 [768, 768], P('dp', 'tensor')
- grad_value_self: float32 [768, 768], P('dp', 'tensor')
- grad_output_self: float32 [768, 768], P('dp', 'tensor')
- grad_query_cross: float32 [768, 768], P('dp', 'tensor')
- grad_key_cross: float32 [768, 768], P('dp', 'tensor')
- grad_value_cross: float32 [768, 768], P('dp', 'tensor')
- grad_output_cross: float32 [768, 768], P('dp', 'tensor')
- grad_hidden_in: float32 [768, 3072], P('dp', 'tensor')
- grad_hidden_out: float32 [768, 3072], P('dp', 'tensor')
The draws below stay inside these ranges and needn't reach their ends.
Inputs may be any that keep to these rules, and one draw needn't show every extreme that they name: `example_counts`: every shard of dp has at least 4 live slots, its lowest ones; some shard has all 8. `lengths`: some slot has length 114. buckets[0] = 0 and the buckets never fall with distance; the largest is 31.
All inputs are finite; a program needn't handle non-finite values.
Results may differ from the reference program's by a relative error of at most 0.028.
The reference program's roundings to bfloat16 on the way count: a program that leaves them out, or rounds other values in their place, can miss the bound.
Values may be sent and summed in bfloat16 or wider, within the bound.
A program may use at most 192 MiB of HBM per device.

```python
import jax
import jax.numpy as jnp
from jax import lax

D = 768
H = 12
HD = 64
FF = 3072
NB = 32
SEQ = 128
MAXLEN = 114
ENC = 512
EX_DEV = 8
GROUP = 4
INNER = 768
EXAMPLES = 64
TOKENS = 8192
ENC_TOKENS = 32768
N_DP = 8


def draw_example_counts(key, part):
    key = jax.random.fold_in(key, 11)
    first_key, second_key = jax.random.split(key)
    base = jax.random.randint(first_key, (N_DP,), EX_DEV // 2, EX_DEV + 1)
    chosen = jax.random.randint(second_key, (), 0, N_DP)
    return jnp.where(jnp.arange(N_DP) == chosen, EX_DEV, base).astype(jnp.int32)


def draw_lengths(key, part):
    key = jax.random.fold_in(key, 12)
    first_key, second_key = jax.random.split(key)
    base = jax.random.randint(first_key, (EXAMPLES,), MAXLEN // 2, MAXLEN + 1)
    chosen = jax.random.randint(second_key, (), 0, EXAMPLES)
    return jnp.where(jnp.arange(EXAMPLES) == chosen, MAXLEN, base).astype(jnp.int32)


def draw_buckets(key, part):
    key = jax.random.fold_in(key, 13)
    half_count = NB // 2
    order = jax.random.permutation(key, SEQ - half_count)
    rise_tail = (order < half_count).astype(jnp.int32)
    distance = jnp.arange(half_count)
    rise_head = (distance >= 1).astype(jnp.int32)
    rise = jnp.concatenate([rise_head, rise_tail])
    return jnp.cumsum(rise).astype(jnp.int32)


def shard_levels(rng, dims, cuts, least, top_value):
    level = 1.0
    for dim, shards_of in cuts:
        draws = jax.random.uniform(jax.random.fold_in(jax.random.fold_in(rng, 6), dim), (shards_of,), jnp.float32, least / len(cuts), top_value / len(cuts))
        level = level * jnp.repeat(jnp.exp(draws), dims[dim] // shards_of).reshape((-1,) + (1,) * (len(dims) - 1 - dim))
    return level


def normal_values(stream_key, shape, scale, reach, cuts=(), kind=jnp.bfloat16):
    entries = jax.random.normal(stream_key, shape, jnp.float32) * scale
    if len(cuts) > 0:
        entries = shard_levels(stream_key, shape, cuts, -0.22, 0.18) * entries
    return jnp.clip(entries, min=-reach, max=reach).astype(kind)


def setup_inputs(seed: int = 0) -> dict:
    key_of = jax.random.split(jax.random.key(seed), 21)
    inputs = normal_values(key_of[0], (TOKENS, D), 1.0, 6.0, ((0, 8),))
    encoded = normal_values(key_of[1], (ENC_TOKENS, D), 1.0, 6.0, ((0, 8),))
    example_counts = draw_example_counts(jax.random.fold_in(key_of[20], 71), 0)
    lengths = draw_lengths(jax.random.fold_in(key_of[20], 71), 0)
    buckets = draw_buckets(jax.random.fold_in(key_of[20], 71), 0)
    gain_self = jnp.clip(1.0 + 0.18 * jax.random.normal(key_of[5], (D,), jnp.float32), 0.1, 1.9)
    gain_cross = jnp.clip(1.0 + 0.18 * jax.random.normal(key_of[6], (D,), jnp.float32), 0.1, 1.9)
    gain_ffn = jnp.clip(1.0 + 0.18 * jax.random.normal(key_of[7], (D,), jnp.float32), 0.1, 1.9)
    bias_table = normal_values(key_of[8], (NB, H), 1.0, 4.0, ((1, 4),), jnp.float32)
    query_self = normal_values(key_of[9], (D, INNER), (D * 16) ** -0.5, 0.0546875, ((1, 4),))
    key_self = normal_values(key_of[10], (D, INNER), D ** -0.5, 0.21875, ((1, 4),))
    value_self = normal_values(key_of[11], (D, INNER), D ** -0.5, 0.21875, ((1, 4),))
    output_self = normal_values(key_of[12], (D, INNER), (INNER // 8) ** -0.5, 0.625, ((1, 4),))
    query_cross = normal_values(key_of[13], (D, INNER), (D * 16) ** -0.5, 0.0546875, ((1, 4),))
    key_cross = normal_values(key_of[14], (D, INNER), D ** -0.5, 0.21875, ((1, 4),))
    value_cross = normal_values(key_of[15], (D, INNER), D ** -0.5, 0.21875, ((1, 4),))
    output_cross = normal_values(key_of[16], (D, INNER), (INNER // 16) ** -0.5, 0.875, ((1, 4),))
    hidden_in = normal_values(key_of[17], (D, FF), D ** -0.5, 0.21875, ((1, 4),))
    hidden_out = normal_values(key_of[18], (D, FF), (FF // 2) ** -0.5, 0.15625, ((1, 4),))
    out_grad = normal_values(key_of[19], (TOKENS, D), 1.0, 6.0, ((0, 8),))
    return {"inputs": inputs, "encoded": encoded, "example_counts": example_counts, "lengths": lengths, "buckets": buckets, "gain_self": gain_self, "gain_cross": gain_cross, "gain_ffn": gain_ffn, "bias_table": bias_table, "query_self": query_self, "key_self": key_self, "value_self": value_self, "output_self": output_self, "query_cross": query_cross, "key_cross": key_cross, "value_cross": value_cross, "output_cross": output_cross, "hidden_in": hidden_in, "hidden_out": hidden_out, "out_grad": out_grad}


@jax.custom_vjp
def low(v):
    return lax.optimization_barrier(v.astype(jnp.bfloat16)).astype(jnp.float32)

@jax.custom_vjp
def low_back(v):
    return v

def low_keep(v):
    return (low(v), None)

def low_pass(kept, grad):
    return (grad,)

def back_keep(v):
    return (v, None)

def back_low(kept, grad):
    return (low(grad),)
low.defvjp(low_keep, low_pass)
low_back.defvjp(back_keep, back_low)
norm_epsilon = 1e-06
masked_score = -1e+30
highest = lax.Precision.HIGHEST

def dense(left, right):
    return jnp.dot(left, right, precision=highest)

def rms_norm(row_data, gain):
    return row_data * lax.rsqrt(lax.optimization_barrier(jnp.mean(row_data * row_data, axis=-1, keepdims=True)) + norm_epsilon) * gain

def build_bias(bias_table, buckets):
    positions = jnp.arange(SEQ)
    distance = jnp.maximum(positions[:, None] - positions[None, :], 0)
    dist_table = (distance[:, :, None] == positions[None, None, :]).astype(jnp.float32)
    bucket_table = (buckets[:, None] == jnp.arange(NB)[None, :]).astype(jnp.float32)
    per_dist = jnp.dot(bucket_table, bias_table, precision=highest)
    return jnp.einsum('ijd,dh->hij', dist_table, per_dist, precision=highest)

def attention(query, key_rows, value_rows, score_bias, causal):
    scores = low_back(jnp.einsum('gihd,gjhd->ghij', query, key_rows, precision=highest) + score_bias)
    if causal is not None:
        scores = jnp.where(causal, scores, masked_score)
    row_max = lax.optimization_barrier(jnp.max(scores, axis=-1, keepdims=True))
    exp_terms = jnp.exp(scores - row_max)
    soft = low(exp_terms / lax.optimization_barrier(jnp.sum(exp_terms, axis=-1, keepdims=True)))
    mixed = jnp.einsum('ghij,gjhd->gihd', soft, value_rows, precision=highest)
    return low_back(low(mixed))

def decoder_group(params, self_bias, causal, row_data, enc_rows):
    gain_self, gain_cross, gain_ffn, bias_table, query_self, key_self, value_self, output_self, query_cross, key_cross, value_cross, output_cross, hidden_in, hidden_out = params
    group_size = row_data.shape[0] // SEQ
    normed_self = low(rms_norm(row_data, gain_self))
    query = low_back(low(dense(normed_self, query_self))).reshape(group_size, SEQ, H, HD)
    key_rows = low_back(low(dense(normed_self, key_self))).reshape(group_size, SEQ, H, HD)
    value_rows = low_back(low(dense(normed_self, value_self))).reshape(group_size, SEQ, H, HD)
    mixed_self = attention(query, key_rows, value_rows, self_bias, causal).reshape(group_size * SEQ, INNER)
    hidden_one = row_data + low_back(dense(mixed_self, output_self.T))
    normed_cross = low(rms_norm(hidden_one, gain_cross))
    cross_query = low_back(low(dense(normed_cross, query_cross))).reshape(group_size, SEQ, H, HD)
    cross_key = low_back(low(dense(enc_rows, key_cross))).reshape(group_size, ENC, H, HD)
    cross_value = low_back(low(dense(enc_rows, value_cross))).reshape(group_size, ENC, H, HD)
    mixed_cross = attention(cross_query, cross_key, cross_value, 0.0, None).reshape(group_size * SEQ, INNER)
    hidden_two = hidden_one + low_back(dense(mixed_cross, output_cross.T))
    normed_ffn = low(rms_norm(hidden_two, gain_ffn))
    pre_act = low_back(dense(normed_ffn, hidden_in))
    activ = low(jax.nn.gelu(pre_act))
    return hidden_two + low_back(dense(activ, hidden_out.T))

def reference(inputs, encoded, example_counts, lengths, buckets, gain_self, gain_cross, gain_ffn, bias_table, query_self, key_self, value_self, output_self, query_cross, key_cross, value_cross, output_cross, hidden_in, hidden_out, out_grad):
    positions = jnp.arange(SEQ)
    slot_index = jnp.arange(EXAMPLES)
    live = slot_index % EX_DEV < example_counts[slot_index // EX_DEV]
    valid_rows = ((positions[None, :] < lengths[:, None]) & live[:, None]).astype(jnp.float32).reshape(TOKENS, 1)
    causal = positions[:, None] >= positions[None, :]
    params = (gain_self, gain_cross, gain_ffn, bias_table, query_self.astype(jnp.float32), key_self.astype(jnp.float32), value_self.astype(jnp.float32), output_self.astype(jnp.float32), query_cross.astype(jnp.float32), key_cross.astype(jnp.float32), value_cross.astype(jnp.float32), output_cross.astype(jnp.float32), hidden_in.astype(jnp.float32), hidden_out.astype(jnp.float32))
    step_fn = jax.checkpoint(decoder_group)

    def layer(param_set, row_data, enc_data):
        self_bias = build_bias(param_set[3], buckets)
        row_blocks = row_data.reshape(EXAMPLES // GROUP, GROUP * SEQ, D)
        enc_blocks = enc_data.reshape(EXAMPLES // GROUP, GROUP * ENC, D)
        result = lax.map(lambda packed: step_fn(param_set, self_bias, causal, packed[0], packed[1]), (row_blocks, enc_blocks))
        return result.reshape(TOKENS, D) * valid_rows
    output, pullback = jax.vjp(layer, params, inputs.astype(jnp.float32), encoded.astype(jnp.float32))
    grad_params, grad_rows, grad_enc = pullback(out_grad.astype(jnp.float32))
    return (output.astype(jnp.bfloat16), grad_rows.astype(jnp.bfloat16), grad_enc.astype(jnp.bfloat16), grad_params[0], grad_params[1], grad_params[2], grad_params[3], grad_params[4], grad_params[5], grad_params[6], grad_params[7], grad_params[8], grad_params[9], grad_params[10], grad_params[11], grad_params[12], grad_params[13])
```

```python
import functools

import jax
import jax.numpy as jnp
from jax import lax
from jax.experimental import pallas as pl
from jax.experimental.pallas import tpu as pltpu
from jax.sharding import PartitionSpec as P

HD = 64
GROUP = 4


norm_epsilon = 1e-06
masked_score = -1e30
highest = lax.Precision.HIGHEST


def dot_plain(left, right):
    return jnp.dot(left, right, preferred_element_type=jnp.float32)


def dot_trans(left, right):
    return lax.dot_general(
        left, right, (((1,), (1,)), ((), ())), preferred_element_type=jnp.float32
    )


def trans_dot(left, right):
    return lax.dot_general(
        left, right, (((0,), (0,)), ((), ())), preferred_element_type=jnp.float32
    )


def rms_forward(row_data, gain):
    inverse = lax.rsqrt(jnp.mean(row_data * row_data, axis=-1, keepdims=True) + norm_epsilon)
    return (inverse, (row_data * inverse * gain).astype(jnp.bfloat16))


def rms_backward(row_data, inverse, gain, grad_normed):
    scaled = gain * grad_normed
    inner = jnp.mean(scaled * row_data, axis=-1, keepdims=True)
    grad_rows = inverse * scaled - row_data * (inverse * inverse * inverse) * inner
    grad_gain = jnp.sum(grad_normed * row_data * inverse, axis=0)
    return (grad_rows, grad_gain)


def attend_forward(query, key_rows, value_rows, score_bias):
    scores = (
        jnp.einsum("gihd,gjhd->ghij", query, key_rows, preferred_element_type=jnp.float32)
        + score_bias
    )
    row_max = jnp.max(scores, axis=-1, keepdims=True)
    exp_terms = jnp.exp(scores - row_max)
    row_total = jnp.sum(exp_terms, axis=-1, keepdims=True)
    soft = (exp_terms / row_total).astype(jnp.bfloat16)
    mixed = jnp.einsum("ghij,gjhd->gihd", soft, value_rows, preferred_element_type=jnp.float32)
    return (mixed.astype(jnp.bfloat16), (row_max + jnp.log(row_total))[..., 0])


def attend_backward(query, key_rows, value_rows, score_bias, log_total, grad_mixed, keep_table):
    scores = (
        jnp.einsum("gihd,gjhd->ghij", query, key_rows, preferred_element_type=jnp.float32)
        + score_bias
    )
    soft = jnp.exp(scores - log_total[..., None])
    grad_soft = jnp.einsum(
        "gihd,gjhd->ghij", grad_mixed, value_rows, preferred_element_type=jnp.float32
    )
    grad_value = jnp.einsum(
        "ghij,gihd->gjhd", soft.astype(jnp.bfloat16), grad_mixed, preferred_element_type=jnp.float32
    ).astype(jnp.bfloat16)
    inner = jnp.sum(soft * grad_soft, axis=-1, keepdims=True)
    grad_scores = (soft * (grad_soft - inner)).astype(jnp.bfloat16)
    grad_query = jnp.einsum(
        "ghij,gjhd->gihd", grad_scores, key_rows, preferred_element_type=jnp.float32
    ).astype(jnp.bfloat16)
    grad_key = jnp.einsum(
        "ghij,gihd->gjhd", grad_scores, query, preferred_element_type=jnp.float32
    ).astype(jnp.bfloat16)
    if keep_table:
        return (grad_query, grad_key, grad_value, jnp.sum(grad_scores.astype(jnp.float32), axis=0))
    return (grad_query, grad_key, grad_value)


MESH = pl.DeviceIdType.MESH
VM = pl.BlockSpec(memory_space=pltpu.VMEM)


def tensor_peer(bit):
    return (lax.axis_index("dp"), lax.axis_index("tensor") ^ bit)


def dp_peer(bit):
    return (lax.axis_index("dp") ^ bit, lax.axis_index("tensor"))


def greet(peers):
    barrier = pltpu.get_barrier_semaphore()
    for peer in peers:
        pl.semaphore_signal(barrier, inc=1, device_id=peer, device_id_type=MESH)
    pl.semaphore_wait(barrier, len(peers))


def send(src, dst, sems, index, peer):
    copy = pltpu.make_async_remote_copy(
        src_ref=src,
        dst_ref=dst,
        send_sem=sems.at[0, index],
        recv_sem=sems.at[1, index],
        device_id=peer,
        device_id_type=MESH,
    )
    copy.start()
    return copy


def total_kernel(term, out, near, mine, far, sems):
    rows = term.shape[0] // 2
    core = lax.rem(lax.axis_index("tensor"), 2)
    greet([tensor_peer(1), tensor_peer(2)])
    own = pl.multiple_of(core * rows, rows)
    other = pl.multiple_of((1 - core) * rows, rows)
    first = send(term.at[pl.ds(other, rows)], near, sems, 0, tensor_peer(1))
    first.wait()
    mine[...] = (
        term[pl.ds(own, rows)].astype(jnp.float32) + near[...].astype(jnp.float32)
    ).astype(jnp.bfloat16)
    second = send(mine, far, sems, 1, tensor_peer(2))
    second.wait()
    out[pl.ds(own, rows)] = (
        mine[...].astype(jnp.float32) + far[...].astype(jnp.float32)
    ).astype(jnp.bfloat16)
    third = send(out.at[pl.ds(own, rows)], out.at[pl.ds(own, rows)], sems, 2, tensor_peer(1))
    third.wait()


def tensor_total(term, ident):
    rows, width = term.shape
    half = pltpu.VMEM((rows // 2, width), jnp.bfloat16)
    return pl.pallas_call(
        total_kernel,
        out_shape=jax.ShapeDtypeStruct(term.shape, jnp.bfloat16),
        in_specs=[VM],
        out_specs=VM,
        scratch_shapes=[half, half, half, pltpu.SemaphoreType.DMA((2, 3))],
        compiler_params=pltpu.CompilerParams(
            collective_id=ident, has_side_effects=True, vmem_limit_bytes=24 * 2**20
        ),
    )(term)


def scatter_kernel(term, out, near, mine, far, sems):
    rows = term.shape[1]
    me = lax.axis_index("tensor")
    core = lax.rem(me, 2)
    greet([tensor_peer(1), tensor_peer(2)])
    y = me // 2
    first = send(term.at[(1 - core) + 2 * (1 - y)], near.at[0], sems, 0, tensor_peer(1))
    second = send(term.at[(1 - core) + 2 * y], near.at[1], sems, 1, tensor_peer(1))
    first.wait()
    mine[...] = (
        term[core + 2 * (1 - y)].astype(jnp.float32) + near[0].astype(jnp.float32)
    ).astype(jnp.bfloat16)
    third = send(mine, far, sems, 2, tensor_peer(2))
    second.wait()
    third.wait()
    out[...] = (
        term[core + 2 * y].astype(jnp.float32)
        + near[1].astype(jnp.float32)
        + far[...].astype(jnp.float32)
    ).astype(jnp.bfloat16)


def tensor_scatter(term, ident):
    rows, width = term.shape
    quarter = pltpu.VMEM((rows // 4, width), jnp.bfloat16)
    return pl.pallas_call(
        scatter_kernel,
        out_shape=jax.ShapeDtypeStruct((rows // 4, width), jnp.bfloat16),
        in_specs=[VM],
        out_specs=VM,
        scratch_shapes=[
            pltpu.VMEM((2, rows // 4, width), jnp.bfloat16),
            quarter,
            quarter,
            pltpu.SemaphoreType.DMA((2, 3)),
        ],
        compiler_params=pltpu.CompilerParams(
            collective_id=ident, has_side_effects=True, vmem_limit_bytes=40 * 2**20
        ),
    )(term.reshape(4, rows // 4, width))


def halving_kernel(chunks, levels, term, out, *rest):
    lands, holds, sems = rest[:levels], rest[levels:-1], rest[-1]
    me = lax.axis_index("dp")
    greet([dp_peer(1 << k) for k in range(levels)])

    def part(ref, chunk, count, bit):
        return ref.at[chunk, bit, :]

    pending = []
    for chunk in range(chunks):
        pending.append(None)

    def start(level, chunk):
        bit = lax.rem(me // (1 << level), 2)
        source = term if level == 0 else holds[level - 1]
        return send(
            source.at[chunk, 1 - bit],
            lands[level].at[chunk],
            sems,
            level * chunks + chunk,
            dp_peer(1 << level),
        )

    def finish(level, chunk, copy):
        bit = lax.rem(me // (1 << level), 2)
        source = term if level == 0 else holds[level - 1]
        copy.wait_recv()
        total = source[chunk, bit].astype(jnp.float32) + lands[level][chunk].astype(jnp.float32)
        if level == levels - 1:
            out[chunk] = total.reshape(out.shape[1:])
        else:
            holds[level][chunk] = total.reshape(holds[level].shape[1:]).astype(jnp.bfloat16)

    copies = {}
    for chunk in range(chunks):
        copies[0, chunk] = start(0, chunk)
    for step in range(chunks + levels - 1):
        for level in range(levels):
            chunk = step - level
            if 0 <= chunk < chunks:
                finish(level, chunk, copies[level, chunk])
                if level + 1 < levels:
                    copies[level + 1, chunk] = start(level + 1, chunk)
    for copy in copies.values():
        copy.wait_send()


def dp_scatter(term, chunks, ident):
    n, rows, columns = term.shape
    width = columns // chunks
    levels = n.bit_length() - 1
    shape = term.reshape((2,) * levels + (rows, chunks, width))
    order = (levels + 1,) + tuple(range(levels - 1, -1, -1)) + (levels, levels + 2)
    pieces = shape.transpose(order)
    lands, holds = [], []
    for level in range(levels):
        left = (2,) * (levels - 1 - level)
        lands.append(pltpu.VMEM((chunks,) + left + (rows, width), jnp.bfloat16))
        if level + 1 < levels:
            holds.append(pltpu.VMEM((chunks,) + left + (rows, width), jnp.bfloat16))
    return pl.pallas_call(
        functools.partial(halving_kernel, chunks, levels),
        out_shape=jax.ShapeDtypeStruct((chunks, rows, width), jnp.float32),
        in_specs=[VM],
        out_specs=VM,
        scratch_shapes=lands + holds + [pltpu.SemaphoreType.DMA((2, levels * chunks))],
        compiler_params=pltpu.CompilerParams(
            collective_id=ident, has_side_effects=True, vmem_limit_bytes=48 * 2**20
        ),
    )(pieces)


def per_device(
    inputs,
    encoded,
    example_counts,
    lengths,
    buckets,
    gain_self,
    gain_cross,
    gain_ffn,
    bias_table,
    query_self,
    key_self,
    value_self,
    output_self,
    query_cross,
    key_cross,
    value_cross,
    output_cross,
    hidden_in,
    hidden_out,
    out_grad,
):
    model_width = inputs.shape[1]
    seq_len = buckets.shape[0]
    slot_count = lengths.shape[0]
    enc_len = encoded.shape[0] // slot_count
    heads_local = query_self.shape[1] // HD
    block_count = slot_count // GROUP
    positions = jnp.arange(seq_len)
    live = jnp.arange(slot_count) < example_counts[0]
    valid_rows = (
        ((positions[None, :] < lengths[:, None]) & live[:, None]).astype(jnp.float32).reshape(-1, 1)
    )
    row_data = inputs.astype(jnp.float32)
    group_count = lax.axis_size("tensor")

    idents = iter(range(1, 20))

    def forward_sum(term):
        return tensor_total(term.astype(jnp.bfloat16), next(idents)).astype(jnp.float32)

    backward_sum = forward_sum

    distance = jnp.maximum(positions[:, None] - positions[None, :], 0)
    dist_table = (distance[:, :, None] == positions[None, None, :]).astype(jnp.float32)
    bucket_table = (buckets[:, None] == jnp.arange(bias_table.shape[0])[None, :]).astype(
        jnp.float32
    )
    per_dist = jnp.dot(bucket_table, bias_table, precision=highest)
    causal = positions[:, None] >= positions[None, :]
    self_bias = jnp.where(
        causal[None],
        jnp.einsum("ijd,dh->hij", dist_table, per_dist, precision=highest),
        masked_score,
    )

    def to_blocks(flat, length):
        return flat.reshape(block_count, GROUP, length, heads_local, HD)

    def run_forward(query, key_rows, value_rows, score_bias, key_len):
        shaped = (
            to_blocks(query, seq_len),
            to_blocks(key_rows, key_len),
            to_blocks(value_rows, key_len),
        )
        mixed, log_total = lax.map(
            lambda packed: attend_forward(packed[0], packed[1], packed[2], score_bias), shaped
        )
        return (mixed.reshape(query.shape), log_total)

    def run_backward(
        query, key_rows, value_rows, score_bias, key_len, log_total, grad_mixed, keep_table
    ):
        shaped = (
            to_blocks(query, seq_len),
            to_blocks(key_rows, key_len),
            to_blocks(value_rows, key_len),
            log_total,
            to_blocks(grad_mixed, seq_len),
        )
        results = lax.map(
            lambda packed: attend_backward(
                packed[0], packed[1], packed[2], score_bias, packed[3], packed[4], keep_table
            ),
            shaped,
        )
        grads = (
            results[0].reshape(query.shape),
            results[1].reshape(key_rows.shape),
            results[2].reshape(value_rows.shape),
        )
        if keep_table:
            return grads + (jnp.sum(results[3], axis=0),)
        return grads

    scale_one, normed_self = rms_forward(row_data, gain_self)
    query = dot_plain(normed_self, query_self).astype(jnp.bfloat16)
    key_rows = dot_plain(normed_self, key_self).astype(jnp.bfloat16)
    value_rows = dot_plain(normed_self, value_self).astype(jnp.bfloat16)
    mixed_self, log_self = run_forward(query, key_rows, value_rows, self_bias, seq_len)
    hidden_one = row_data + forward_sum(dot_trans(mixed_self, output_self))
    scale_two, normed_share_two = rms_forward(hidden_one, gain_cross)
    cross_query = dot_plain(normed_share_two, query_cross).astype(jnp.bfloat16)
    cross_key = dot_plain(encoded, key_cross).astype(jnp.bfloat16)
    cross_value = dot_plain(encoded, value_cross).astype(jnp.bfloat16)
    mixed_cross, log_cross = run_forward(cross_query, cross_key, cross_value, 0.0, enc_len)
    hidden_two = hidden_one + forward_sum(dot_trans(mixed_cross, output_cross))
    scale_three, normed_share_three = rms_forward(hidden_two, gain_ffn)
    pre_act = dot_plain(normed_share_three, hidden_in)
    activ = jax.nn.gelu(pre_act).astype(jnp.bfloat16)
    part_width = model_width // group_count
    column_start = lax.axis_index("tensor") * part_width
    ffn_share = lax.dynamic_slice_in_dim(
        forward_sum(dot_trans(activ, hidden_out)), column_start, part_width, 1
    )
    layer_out = (
        valid_rows * (lax.dynamic_slice_in_dim(hidden_two, column_start, part_width, 1) + ffn_share)
    ).astype(jnp.bfloat16)
    grad_top = out_grad.astype(jnp.float32) * valid_rows
    grad_top_low = grad_top.astype(jnp.bfloat16)
    grad_hidden_out = trans_dot(grad_top_low, activ)
    grad_act = dot_plain(grad_top_low, hidden_out)
    gelu_value, gelu_pull = jax.vjp(jax.nn.gelu, pre_act)
    grad_pre = gelu_pull(grad_act)[0].astype(jnp.bfloat16)
    grad_hidden_in = trans_dot(normed_share_three, grad_pre)
    grad_rows_three, grad_gain_three = rms_backward(
        hidden_two, scale_three, gain_ffn, backward_sum(dot_trans(grad_pre, hidden_in))
    )
    grad_hidden_two = grad_top + grad_rows_three
    grad_two_low = grad_hidden_two.astype(jnp.bfloat16)
    grad_output_cross = trans_dot(grad_two_low, mixed_cross)
    grad_mixed_cross = dot_plain(grad_two_low, output_cross).astype(jnp.bfloat16)
    grad_cq, grad_ck, grad_cv = run_backward(
        cross_query, cross_key, cross_value, 0.0, enc_len, log_cross, grad_mixed_cross, False
    )
    grad_query_cross = trans_dot(normed_share_two, grad_cq)
    grad_key_cross = trans_dot(encoded, grad_ck)
    grad_value_cross = trans_dot(encoded, grad_cv)
    encoded_grad = tensor_scatter(
        (dot_trans(grad_ck, key_cross) + dot_trans(grad_cv, value_cross)).astype(jnp.bfloat16),
        next(idents),
    )
    grad_rows_two, grad_gain_two = rms_backward(
        hidden_one, scale_two, gain_cross, backward_sum(dot_trans(grad_cq, query_cross))
    )
    grad_hidden_one = grad_hidden_two + grad_rows_two
    grad_one_low = grad_hidden_one.astype(jnp.bfloat16)
    grad_output_self = trans_dot(grad_one_low, mixed_self)
    grad_mixed_self = dot_plain(grad_one_low, output_self).astype(jnp.bfloat16)
    grad_q, grad_k, grad_v, score_sums = run_backward(
        query, key_rows, value_rows, self_bias, seq_len, log_self, grad_mixed_self, True
    )
    dist_sums = jnp.einsum("hij,ijd->dh", score_sums, dist_table, precision=highest)
    table_grad = jnp.dot(bucket_table.T, dist_sums, precision=highest)
    grad_query_self = trans_dot(normed_self, grad_q)
    grad_key_self = trans_dot(normed_self, grad_k)
    grad_value_self = trans_dot(normed_self, grad_v)
    grad_normed_self = backward_sum(
        dot_trans(grad_q, query_self) + dot_trans(grad_k, key_self) + dot_trans(grad_v, value_self)
    )
    grad_rows_one, grad_gain_one = rms_backward(row_data, scale_one, gain_self, grad_normed_self)
    total_grad = grad_hidden_one + grad_rows_one
    input_grad = lax.dynamic_slice_in_dim(total_grad, column_start, part_width, 1).astype(
        jnp.bfloat16
    )
    weight_grads = (
        grad_query_self,
        grad_key_self,
        grad_value_self,
        grad_output_self,
        grad_query_cross,
        grad_key_cross,
        grad_value_cross,
        grad_output_cross,
        grad_hidden_in,
        grad_hidden_out,
    )
    dp_count = lax.axis_size("dp")
    piece_rows = model_width // dp_count
    if piece_rows % 16 == 0:
        merged = jnp.concatenate([grad.astype(jnp.bfloat16) for grad in weight_grads], axis=1)
        chunks = 4
        summed = dp_scatter(
            merged.reshape(dp_count, piece_rows, merged.shape[1]), chunks, next(idents)
        )
        summed = summed.transpose(1, 0, 2).reshape(piece_rows, merged.shape[1])
        weight_sums = []
        column = 0
        for grad in weight_grads:
            weight_sums.append(summed[:, column : column + grad.shape[1]])
            column += grad.shape[1]
    else:
        weight_sums = [
            lax.psum_scatter(grad, "dp", scatter_dimension=0, tiled=True) for grad in weight_grads
        ]
    small_sums = lax.psum((grad_gain_one, grad_gain_two, grad_gain_three, table_grad), "dp")
    return (
        layer_out,
        input_grad,
        encoded_grad,
        small_sums[0],
        small_sums[1],
        small_sums[2],
        small_sums[3],
        weight_sums[0],
        weight_sums[1],
        weight_sums[2],
        weight_sums[3],
        weight_sums[4],
        weight_sums[5],
        weight_sums[6],
        weight_sums[7],
        weight_sums[8],
        weight_sums[9],
    )


def solution(mesh):
    placed = (
        P("dp", None),
        P("dp", None),
        P("dp"),
        P("dp"),
        P(),
        P(),
        P(),
        P(),
        P(None, "tensor"),
        P(None, "tensor"),
        P(None, "tensor"),
        P(None, "tensor"),
        P(None, "tensor"),
        P(None, "tensor"),
        P(None, "tensor"),
        P(None, "tensor"),
        P(None, "tensor"),
        P(None, "tensor"),
        P(None, "tensor"),
        P("dp", None),
    )
    return jax.shard_map(
        per_device,
        mesh=mesh,
        in_specs=placed,
        out_specs=(
            P("dp", "tensor"),
            P("dp", "tensor"),
            P(("dp", "tensor"), None),
            P(),
            P(),
            P(),
            P(None, "tensor"),
            P("dp", "tensor"),
            P("dp", "tensor"),
            P("dp", "tensor"),
            P("dp", "tensor"),
            P("dp", "tensor"),
            P("dp", "tensor"),
            P("dp", "tensor"),
            P("dp", "tensor"),
            P("dp", "tensor"),
            P("dp", "tensor"),
        ),
        check_vma=False,
    )
```

```python
import functools
from types import SimpleNamespace
from typing import NamedTuple

import jax
import jax.numpy as jnp
from jax import lax
from jax.experimental import pallas as pl
from jax.experimental.pallas import tpu as pltpu
from jax.sharding import PartitionSpec as P

HD = 64
CHUNK_SLOTS = 2
GELU_ROWS = 32

norm_epsilon = 1e-06
masked_score = -1e30
highest = lax.Precision.HIGHEST
MESH = pl.DeviceIdType.MESH
VM = pl.BlockSpec(memory_space=pltpu.VMEM)
SM = pl.BlockSpec(memory_space=pltpu.SMEM)
HBM = pl.BlockSpec(memory_space=pl.ANY)
low = jnp.bfloat16
wide = jnp.float32


def dot(left, right):
    return lax.dot_general(left, right, (((1,), (0,)), ((), ())), preferred_element_type=wide)


def dot_t(left, right):
    return lax.dot_general(left, right, (((1,), (1,)), ((), ())), preferred_element_type=wide)


def t_dot(left, right):
    return lax.dot_general(left, right, (((0,), (0,)), ((), ())), preferred_element_type=wide)


def inverse_rms(rows):
    return lax.rsqrt(jnp.mean(rows * rows, axis=-1, keepdims=True) + norm_epsilon)


def norm_back(rows, gain, grad):
    inverse = inverse_rms(rows)
    scaled = gain * grad
    inner = jnp.mean(scaled * rows, axis=-1, keepdims=True)
    grad_rows = inverse * scaled - rows * (inverse * inverse * inverse) * inner
    return grad_rows, jnp.sum(grad * rows * inverse, axis=0, keepdims=True)


def tensor_peer(bit):
    return (lax.axis_index("dp"), lax.axis_index("tensor") ^ bit)


def dp_peer(bit):
    return (lax.axis_index("dp") ^ bit, lax.axis_index("tensor"))


def reversed_bits(value, levels):
    return sum(((value >> k) & 1) << (levels - 1 - k) for k in range(levels))


class Weights(NamedTuple):
    query_self: object
    key_self: object
    value_self: object
    output_self: object
    query_cross: object
    key_cross: object
    value_cross: object
    output_cross: object
    hidden_in: object
    hidden_out: object


def layer_kernel(cfg, names, *refs):
    a = SimpleNamespace(**dict(zip(names, refs, strict=True)))
    seq, enc_len, slots, width = cfg.seq, cfg.enc_len, cfg.slots, cfg.width
    heads, levels, in_kernel = cfg.heads, cfg.levels, cfg.in_kernel
    inner = heads * HD
    if in_kernel:
        a.lands = [getattr(a, "land%d" % i) for i in range(levels)]
        a.holds = [getattr(a, "hold%d" % i) for i in range(levels - 1)]
    chunks = slots // CHUNK_SLOTS
    chunk_rows = CHUNK_SLOTS * seq
    half_rows = chunk_rows // 2
    half_width = width // 2
    quarter_width = width // 4
    me = lax.axis_index("tensor")
    core = lax.rem(me, 2)
    y = me // 2
    dp_me = lax.axis_index("dp")
    c_peer, y_peer = tensor_peer(1), tensor_peer(2)

    def rows_of(k, count):
        return pl.ds(pl.multiple_of(k * count, count), count)

    def load(index, src, dst):
        return pltpu.make_async_copy(src, dst, a.load_sem.at[index])

    load_x, load_g = load(0, a.inputs, a.x), load(1, a.out_grad, a.g3)
    loads = Weights(
        *(
            load(2 + i, getattr(a, name), getattr(a, "w_" + name))
            for i, name in enumerate(Weights._fields)
        )
    )
    load_x.start()
    for copy in loads[:4]:
        copy.start()

    def enc_copy(slot, buffer):
        rows = pl.ds(pl.multiple_of(slot * enc_len, enc_len), enc_len)
        return pltpu.make_async_copy(a.encoded.at[rows], a.enc.at[rows_of(buffer, enc_len)], a.enc_sem.at[buffer])

    enc_copy(0, 0).start()
    for copy in loads[4:]:
        copy.start()
    load_g.start()

    barrier = pltpu.get_barrier_semaphore()
    peers = [c_peer, y_peer] + [dp_peer(1 << k) for k in range(levels)]
    for peer in peers:
        pl.semaphore_signal(barrier, inc=1, device_id=peer, device_id_type=MESH)

    lane = lax.broadcasted_iota(jnp.int32, (1, inner), 1)
    masks = [jnp.where(lane // HD == h, 1.0, 0.0).astype(wide) for h in range(heads)]
    masks_low = [m.astype(low) for m in masks]
    row_i = lax.broadcasted_iota(jnp.int32, (seq, seq), 0)
    col_i = lax.broadcasted_iota(jnp.int32, (seq, seq), 1)
    for h in range(heads):
        line = jnp.broadcast_to(a.bias_line[h : h + 1, :], (seq, seq))
        turned = pltpu.roll(line, 0, 1, stride=1, stride_axis=0)
        a.bias[h * seq : (h + 1) * seq, :] = jnp.where(row_i >= col_i, turned, masked_score)
    a.table[...] = jnp.zeros_like(a.table)
    a.small[...] = jnp.zeros_like(a.small)

    def stack(rows):
        return jnp.concatenate([rows * m for m in masks_low], axis=0)

    def unstack(rows):
        return sum(rows[h * seq : (h + 1) * seq] * masks[h] for h in range(heads))

    def softmax(scores):
        peak = jnp.max(scores, axis=-1, keepdims=True)
        terms = jnp.exp(scores - peak)
        return (terms / jnp.sum(terms, axis=-1, keepdims=True)).astype(low)

    def own_rows(k):
        return pl.ds(pl.multiple_of(k * chunk_rows + core * half_rows, half_rows), half_rows)

    def other_rows(k):
        return pl.ds(pl.multiple_of(k * chunk_rows + (1 - core) * half_rows, half_rows), half_rows)

    def remote(src, dst, sems, index, peer):
        return pltpu.make_async_remote_copy(
            src_ref=src,
            dst_ref=dst,
            send_sem=sems.at[(0,) + index],
            recv_sem=sems.at[(1,) + index],
            device_id=peer,
            device_id_type=MESH,
        )

    def near_copy(p, k):
        return remote(a.part.at[other_rows(k)], a.near.at[k], a.near_sem, (p, k), c_peer)

    def far_copy(p, k):
        return remote(a.mine.at[k], a.far.at[p % 2, k], a.far_sem, (p, k), y_peer)

    def y_send(p, k):
        near_copy(p, k).wait()
        a.mine[k] = (a.part[own_rows(k)].astype(wide) + a.near[k].astype(wide)).astype(low)
        far_copy(p, k).start()

    def total(p, k):
        far_copy(p, k).wait()
        return a.mine[k].astype(wide) + a.far[p % 2, k].astype(wide)

    def share_copy(p, k, buffer):
        return remote(buffer.at[own_rows(k)], buffer.at[own_rows(k)], a.share_sem, (p, k), c_peer)

    def each_chunk(body):
        def step(k, carry):
            body(k)
            return carry

        lax.fori_loop(0, chunks, step, 0)

    def phase(p, finish, buffer, compute):
        def body(k):
            finish(k, total(p - 1, k))
            share_copy(p, k, buffer).start()

            @pl.when(k > 0)
            def _():
                y_send(p, k - 1)

            share_copy(p, k, buffer).wait()
            compute(k)
            near_copy(p, k).start()

        each_chunk(body)
        y_send(p, chunks - 1)

    def project(slot, buffer):
        enc_copy(slot, buffer).wait()

        @pl.when(slot + 1 < slots)
        def _():
            enc_copy(slot + 1, 1 - buffer).start()

        rows = rows_of(slot, enc_len)
        a.k2[rows] = dot(a.enc[rows_of(buffer, enc_len)], a.w_key_cross[...]).astype(low)
        a.v2[rows] = dot(a.enc[rows_of(buffer, enc_len)], a.w_value_cross[...]).astype(low)

    def self_forward(k):
        rows = rows_of(k, chunk_rows)
        x = a.x[rows].astype(wide)
        normed = (x * inverse_rms(x) * a.gain_self[...]).astype(low)
        a.n1[rows] = normed
        query = dot(normed, a.w_query_self[...]).astype(low)
        keys = dot(normed, a.w_key_self[...]).astype(low)
        values = dot(normed, a.w_value_self[...]).astype(low)
        a.q1[rows], a.k1[rows], a.v1[rows] = query, keys, values
        mixed = []
        for s in range(CHUNK_SLOTS):
            part = slice(s * seq, (s + 1) * seq)
            weights = softmax(dot_t(stack(query[part]), keys[part]) + a.bias[...])
            a.soft1[k * CHUNK_SLOTS + s] = weights
            mixed.append(unstack(dot(weights, values[part])).astype(low))
        mixed = jnp.concatenate(mixed, axis=0)
        a.o1[rows] = mixed
        a.part[rows] = dot_t(mixed, a.w_output_self[...]).astype(low)

    load_x.wait()
    for copy in loads[:4]:
        copy.wait()

    def phase_zero(k):
        self_forward(k)

        @pl.when(k == 0)
        def _():
            pl.semaphore_wait(barrier, len(peers))
            loads.key_cross.wait()
            loads.value_cross.wait()

        near_copy(0, k).start()
        project(CHUNK_SLOTS * k, 0)
        y_send(0, k)
        project(CHUNK_SLOTS * k + 1, 1)

    each_chunk(phase_zero)
    loads.query_cross.wait()
    loads.output_cross.wait()

    def finish_one(k, term):
        hidden = a.x[own_rows(k)].astype(wide) + term
        a.h1[k] = hidden
        a.n2[own_rows(k)] = (hidden * inverse_rms(hidden) * a.gain_cross[...]).astype(low)

    def cross_forward(k):
        rows = rows_of(k, chunk_rows)
        query = dot(a.n2[rows], a.w_query_cross[...]).astype(low)
        a.q2[rows] = query
        mixed = []
        for s in range(CHUNK_SLOTS):
            slot = k * CHUNK_SLOTS + s
            enc_rows = rows_of(slot, enc_len)
            weights = softmax(dot_t(stack(query[s * seq : (s + 1) * seq]), a.k2[enc_rows]))
            a.soft2[slot] = weights
            mixed.append(unstack(dot(weights, a.v2[enc_rows])).astype(low))
        mixed = jnp.concatenate(mixed, axis=0)
        a.o2[rows] = mixed
        a.part[rows] = dot_t(mixed, a.w_output_cross[...]).astype(low)

    phase(1, finish_one, a.n2, cross_forward)
    for copy in (loads.hidden_in, loads.hidden_out, load_g):
        copy.wait()

    def limit(slot):
        return jnp.where(slot < a.counts[0], a.lengths[slot], 0)

    def keep_rows(slot, rows):
        pos = lax.broadcasted_iota(jnp.int32, (seq, 1), 0)
        return jnp.where(pos < limit(slot), rows, 0.0)

    def finish_two(k, term):
        hidden = a.h1[k] + term
        a.h2[k] = hidden
        a.n3[own_rows(k)] = (hidden * inverse_rms(hidden) * a.gain_ffn[...]).astype(low)

    def out_near_copy(k):
        return remote(a.out_part.at[k % 2, 1 - core], a.out_near.at[k], a.out_near_sem, (k,), c_peer)

    def out_far_copy(k):
        return remote(a.out_mine.at[k, 1 - y], a.out_far.at[k], a.out_far_sem, (k,), y_peer)

    def out_send(k):
        out_near_copy(k).wait()
        term = a.out_part[k % 2, core].astype(wide) + a.out_near[k].astype(wide)
        a.out_mine[k, 0] = term[:, :half_width].astype(low)
        a.out_mine[k, 1] = term[:, half_width:].astype(low)
        out_far_copy(k).start()

    scale = 0.7978845608028654

    def feed_forward(k):
        rows = rows_of(k, chunk_rows)
        grad = jnp.concatenate(
            [
                keep_rows(k * CHUNK_SLOTS + s, a.g3[rows_of(k * CHUNK_SLOTS + s, seq)].astype(wide))
                for s in range(CHUNK_SLOTS)
            ],
            axis=0,
        ).astype(low)
        a.g3[rows] = grad
        a.pre[...] = dot(a.n3[rows], a.w_hidden_in[...])

        def gelu_rows(i, carry):
            part = rows_of(i, GELU_ROWS)
            pre = a.pre[part]
            square = pre * pre
            bend = jnp.tanh(scale * pre * (1.0 + 0.044715 * square))
            half = 0.5 * (1.0 + bend)
            curve = scale * (1.0 + 3 * 0.044715 * square)
            a.pre[part] = half + 0.5 * pre * (1.0 - bend * bend) * curve
            target = pl.ds(pl.multiple_of(k * chunk_rows + i * GELU_ROWS, GELU_ROWS), GELU_ROWS)
            a.act[target] = (pre * half).astype(low)
            return carry

        lax.fori_loop(0, chunk_rows // GELU_ROWS, gelu_rows, 0)
        out = dot_t(a.act[rows], a.w_hidden_out[...]).astype(low)
        a.out_part[k % 2, 0] = out[:half_rows]
        a.out_part[k % 2, 1] = out[half_rows:]
        out_near_copy(k).start()
        grad_pre = (a.pre[...] * dot(grad, a.w_hidden_out[...])).astype(low)
        a.d_pre[rows] = grad_pre
        a.part[rows] = dot_t(grad_pre, a.w_hidden_in[...]).astype(low)

    def feed_forward_sends(k):
        feed_forward(k)
        out_send(k)

    phase(2, finish_two, a.n3, feed_forward_sends)

    def column_copy(which, k):
        return remote(
            a.col_send.at[which, k], a.columns.at[which, own_rows(k)], a.col_sem, (which, k), c_peer
        )

    def emit_columns(which, k, value):
        left, right = value[:, :quarter_width], value[:, quarter_width:]
        first = core == 0
        a.columns[which, own_rows(k)] = jnp.where(first, left, right).astype(low)
        a.col_send[which, k] = jnp.where(first, right, left).astype(low)
        column_copy(which, k).start()

    def my_half(value):
        return jnp.where(y == 0, value[:, :half_width], value[:, half_width:])

    def finish_out(k):
        out_far_copy(k).wait()
        value = my_half(a.h2[k]) + a.out_mine[k, y].astype(wide) + a.out_far[k].astype(wide)
        emit_columns(0, k, keep_rows(k * CHUNK_SLOTS + core, value))

    def dp_rank(level):
        return (dp_me >> level) & 1

    def dp_copy(block, level):
        buffer = block % 2
        count = 1 << (levels - 1 - level)
        source = a.term if level == 0 else a.holds[level - 1]
        part = pl.ds((1 - dp_rank(level)) * count, count)
        return remote(
            source.at[buffer, part],
            a.lands[level].at[buffer],
            a.dp_sem,
            (block, level),
            dp_peer(1 << level),
        )

    def dp_begin(block):
        if in_kernel:
            if block >= 2:
                credit_wait(block, 0)
            dp_copy(block, 0).start()
        else:
            pltpu.make_async_copy(
                a.term.at[block % 2], a.raw_grads.at[block], a.dp_sem.at[0, block, 0]
            ).start()

    def credit_wait(block, level):
        pl.semaphore_wait(a.credit_sem.at[block % 2, level], 1)

    def dp_advance(block, level):
        if not in_kernel:
            return
        buffer = block % 2
        count = 1 << (levels - 1 - level)
        dp_copy(block, level).wait()
        source = a.term if level == 0 else a.holds[level - 1]
        land = a.lands[level]
        part = pl.ds(dp_rank(level) * count, count)
        value = source[buffer, part].astype(wide) + land[buffer].astype(wide)
        if level == levels - 1:
            emit_grads(block, value[0])
        else:
            a.holds[level][buffer] = value.astype(low)
        if block < 2:
            pl.semaphore_signal(
                a.credit_sem.at[buffer, level],
                inc=1,
                device_id=dp_peer(1 << level),
                device_id_type=MESH,
            )
        if level + 1 < levels:
            if block >= 2:
                credit_wait(block, level + 1)
            dp_copy(block, level + 1).start()

    def dp_finish_raw(block):
        if not in_kernel:
            pltpu.make_async_copy(
                a.term.at[block % 2], a.raw_grads.at[block], a.dp_sem.at[0, block, 0]
            ).wait()

    def emit_grads(block, value):
        if block == 0:
            a.grad_hidden_out[...] = value
        elif block == 1:
            a.grad_hidden_in[...] = value
        else:
            names = Weights._fields[4:8] if block == 2 else Weights._fields[:4]
            for i, name in enumerate(names):
                getattr(a, "grad_" + name)[...] = value[:, i * inner : (i + 1) * inner]

    piece = cfg.piece
    groups = 2
    group_rows = width // groups
    pieces_each = max(group_rows // piece, 1) if in_kernel else 1

    def store_pieces(block, g, rows):
        if in_kernel:
            for i in range(pieces_each):
                for gg in range(groups):
                    index = reversed_bits(gg * pieces_each + i, levels)
                    if gg == g:
                        a.term[block % 2, index] = rows[i * piece : (i + 1) * piece]
        else:
            a.term[block % 2, g * group_rows : (g + 1) * group_rows] = rows

    def plain_grads(block, left, right):
        for g in range(groups):
            columns = slice(g * group_rows, (g + 1) * group_rows)
            store_pieces(block, g, t_dot(left[:, columns], right[...]).astype(low))

    def turned_grads(block):
        for g in range(groups):
            columns = slice(g * group_rows, (g + 1) * group_rows)
            store_pieces(block, g, a.enc[all_turned, columns].T)

    def turned_rows(i):
        return slice(i * inner, (i + 1) * inner)

    all_turned = slice(0, 4 * inner)

    plain_grads(0, a.g3, a.act)
    dp_begin(0)
    plain_grads(1, a.n3, a.d_pre)
    dp_begin(1)

    def add_gain(index, value):
        a.small[index : index + 1, :] += value

    def finish_three(k, term):
        grad_rows, grad_gain = norm_back(a.h2[k], a.gain_ffn[...], term)
        add_gain(2, grad_gain)
        grad = a.g3[own_rows(k)].astype(wide) + grad_rows
        a.dh[k] = grad
        a.dh2[own_rows(k)] = grad.astype(low)
        finish_out(k)

    def score_back(soft, grad_soft):
        weights = soft.astype(wide)
        row_inner = jnp.sum(weights * grad_soft, axis=-1, keepdims=True)
        return (weights * (grad_soft - row_inner)).astype(low)

    def cross_backward(k):
        rows = rows_of(k, chunk_rows)
        grad_mixed = dot(a.dh2[rows], a.w_output_cross[...]).astype(low)
        query = a.q2[rows]
        grads = []
        for s in range(CHUNK_SLOTS):
            slot = k * CHUNK_SLOTS + s
            part = slice(s * seq, (s + 1) * seq)
            enc_rows = rows_of(slot, enc_len)
            tall_grad, tall_query = stack(grad_mixed[part]), stack(query[part])
            soft = a.soft2[slot]
            grad_scores = score_back(soft, dot_t(tall_grad, a.v2[enc_rows]))
            a.dkv[slot, :inner] = t_dot(tall_query, grad_scores).astype(low)
            a.dkv[slot, inner:] = t_dot(tall_grad, soft).astype(low)
            grads.append(unstack(dot(grad_scores, a.k2[enc_rows])).astype(low))
        grads = jnp.concatenate(grads, axis=0)
        a.q2[rows] = grads
        a.part[rows] = dot_t(grads, a.w_query_cross[...]).astype(low)

        @pl.when(k == 2)
        def _():
            dp_advance(0, 0)

    phase(3, finish_three, a.dh2, cross_backward)

    kv_blocks = 2 * inner // half_rows
    for i in range(kv_blocks):
        a.h2[i] = jnp.zeros_like(a.h2[i])

    def enc_slots(j, own):
        which = jnp.where(own == 1, core, 1 - core)
        side = jnp.where(j < 2, 1 - y, y)
        return 4 * side + 2 * which + lax.rem(j, 2)

    def enc_partial(slot, buffer):
        key_grad, value_grad = a.dkv[slot, :inner], a.dkv[slot, inner:]
        for i in range(kv_blocks):
            part = slice(i * half_rows, (i + 1) * half_rows)
            a.h2[i] += dot(a.dkv[slot, part], a.enc[rows_of(buffer, enc_len)])
        return dot_t(key_grad.T, a.w_key_cross[...]) + dot_t(value_grad.T, a.w_value_cross[...])

    def enc_half(j):
        return rows_of(lax.rem(j, 2), enc_len)

    def enc_near_copy(j):
        source = a.n3.at[enc_half(j)]
        target = a.act if j < 2 else a.d_pre
        return remote(source, target.at[enc_half(j)], a.enc_near_sem, (j,), c_peer)

    def enc_far_copy(j):
        return remote(a.g3.at[enc_half(j)], a.enc_far.at[j], a.enc_far_sem, (j,), y_peer)

    enc_copy(enc_slots(0, 0), 0).start()
    for j in range(4):
        enc_copy(enc_slots(j, 0), 0).wait()
        enc_copy(enc_slots(j, 1), 1).start()
        if j >= 2:
            enc_near_copy(j - 2).wait_send()
        a.n3[enc_half(j)] = enc_partial(enc_slots(j, 0), 0).astype(low)
        enc_near_copy(j).start()
        enc_copy(enc_slots(j, 1), 1).wait()
        if j < 3:
            enc_copy(enc_slots(j + 1, 0), 0).start()
        partial = enc_partial(enc_slots(j, 1), 1)
        enc_near_copy(j).wait_recv()
        if j < 2:
            a.g3[enc_half(j)] = (partial + a.act[enc_half(j)].astype(wide)).astype(low)
            enc_far_copy(j).start()
        else:
            a.enc_out[rows_of(j - 2, enc_len)] = (
                partial + a.d_pre[enc_half(j)].astype(wide)
            ).astype(low)
    dp_advance(1, 0)
    dp_advance(0, 1)

    a.enc[turned_rows(0)] = t_dot(a.q2[...], a.n2[...]).astype(low)
    for i in range(kv_blocks):
        a.enc[inner + i * half_rows : inner + (i + 1) * half_rows] = a.h2[i].astype(low)
    a.enc[turned_rows(3)] = t_dot(a.o2[...], a.dh2[...]).astype(low)
    dp_finish_raw(0)
    turned_grads(2)
    dp_begin(2)

    def finish_four(k, term):
        grad_rows, grad_gain = norm_back(a.h1[k], a.gain_cross[...], term)
        add_gain(1, grad_gain)
        grad = a.dh[k] + grad_rows
        a.dh[k] = grad
        a.dh1[own_rows(k)] = grad.astype(low)

    def self_backward(k):
        rows = rows_of(k, chunk_rows)
        grad_mixed = dot(a.dh1[rows], a.w_output_self[...]).astype(low)
        query, keys, values = a.q1[rows], a.k1[rows], a.v1[rows]
        grads = [[], [], []]
        for s in range(CHUNK_SLOTS):
            part = slice(s * seq, (s + 1) * seq)
            tall_grad, tall_query = stack(grad_mixed[part]), stack(query[part])
            soft = a.soft1[k * CHUNK_SLOTS + s]
            grad_scores = score_back(soft, dot_t(tall_grad, values[part]))
            a.table[...] += grad_scores.astype(wide)
            grads[0].append(unstack(dot(grad_scores, keys[part])).astype(low))
            grads[1].append(t_dot(grad_scores, tall_query).astype(low))
            grads[2].append(t_dot(soft, tall_grad).astype(low))
        grads = [jnp.concatenate(g, axis=0) for g in grads]
        a.q1[rows], a.k1[rows], a.v1[rows] = grads
        a.part[rows] = (
            dot_t(grads[0], a.w_query_self[...])
            + dot_t(grads[1], a.w_key_self[...])
            + dot_t(grads[2], a.w_value_self[...])
        ).astype(low)

    phase(4, finish_four, a.dh1, self_backward)
    dp_advance(1, 1)
    dp_advance(0, 2)
    dp_advance(1, 2)
    a.enc[turned_rows(0)] = t_dot(a.q1[...], a.n1[...]).astype(low)
    a.enc[turned_rows(1)] = t_dot(a.k1[...], a.n1[...]).astype(low)
    a.enc[turned_rows(2)] = t_dot(a.v1[...], a.n1[...]).astype(low)
    a.enc[turned_rows(3)] = t_dot(a.o1[...], a.dh1[...]).astype(low)
    dp_finish_raw(1)
    turned_grads(3)
    dp_begin(3)
    dp_advance(2, 0)

    def phase_five(k):
        grad_rows, grad_gain = norm_back(
            a.x[own_rows(k)].astype(wide), a.gain_self[...], total(4, k)
        )
        add_gain(0, grad_gain)
        emit_columns(1, k, my_half(a.dh[k] + grad_rows))

    each_chunk(phase_five)

    mirror = jnp.where(row_i + col_i == seq - 1, 1.0, 0.0).astype(wide)
    for h in range(heads):
        flipped = jnp.dot(
            a.table[h * seq : (h + 1) * seq, :],
            mirror,
            precision=highest,
            preferred_element_type=wide,
        )
        turned = pltpu.roll(flipped, 0, 1, stride=1, stride_axis=0)
        a.small[3:4, h * seq : (h + 1) * seq] = jnp.sum(turned, axis=0, keepdims=True)

    def small_copy(i):
        peer = c_peer if i == 0 else dp_peer(1 << (i - 1))
        return remote(a.small, a.small_land.at[i], a.small_sem, (i,), peer)

    small_copy(0).start()
    dp_advance(2, 1)
    small_copy(0).wait()
    row = lax.broadcasted_iota(jnp.int32, a.small.shape, 0)
    a.small[...] += jnp.where(row < 3, a.small_land[0], 0.0)
    for i in range(1, levels + 1):
        small_copy(i).start()
        if i == 1:
            dp_advance(3, 0)
        if i == 2:
            dp_advance(2, 2)
        small_copy(i).wait()
        a.small[...] += a.small_land[i]
    dp_advance(3, 1)
    dp_advance(3, 2)
    dp_finish_raw(2)
    dp_finish_raw(3)

    for j in range(2):
        enc_far_copy(j).wait()
        a.enc_out[rows_of(j, enc_len)] = (
            a.enc_out[rows_of(j, enc_len)].astype(wide) + a.enc_far[j].astype(wide)
        ).astype(low)
        enc_near_copy(2 + j).wait_send()
    for k in range(chunks):
        column_copy(0, k).wait()
        column_copy(1, k).wait()
    stores = [
        load(0, a.columns.at[0], a.layer_out),
        load(1, a.columns.at[1], a.input_grad),
        load(2, a.enc_out, a.encoded_grad),
    ]
    for store in stores:
        store.start()
    a.small_out[...] = a.small[...]
    for store in stores:
        store.wait()


def per_device(*args):
    (
        inputs,
        encoded,
        example_counts,
        lengths,
        buckets,
        gain_self,
        gain_cross,
        gain_ffn,
        bias_table,
    ) = args[:9]
    weights = args[9:19]
    out_grad = args[19]
    rows, width = inputs.shape
    seq = buckets.shape[0]
    slots = lengths.shape[0]
    enc_rows = encoded.shape[0]
    enc_len = enc_rows // slots
    inner = weights[0].shape[1]
    hidden = weights[8].shape[1]
    heads = inner // HD
    dp_count = lax.axis_size("dp")
    levels = dp_count.bit_length() - 1
    piece = width // dp_count
    in_kernel = piece % 16 == 0
    chunks = slots // CHUNK_SLOTS
    half = CHUNK_SLOTS * seq // 2

    bucket_table = (buckets[:, None] == jnp.arange(bias_table.shape[0])[None, :]).astype(wide)
    per_dist = jnp.dot(bucket_table, bias_table, precision=highest)
    bias_line = jnp.roll(per_dist[::-1], 1, axis=0).T

    ins = dict(
        lengths=(lengths, SM),
        counts=(example_counts, SM),
        gain_self=(gain_self[None], VM),
        gain_cross=(gain_cross[None], VM),
        gain_ffn=(gain_ffn[None], VM),
        bias_line=(bias_line, VM),
        inputs=(inputs, HBM),
        encoded=(encoded, HBM),
        out_grad=(out_grad, HBM),
    )
    for name, weight in zip(Weights._fields, weights, strict=True):
        ins[name] = (weight, HBM)
    shape = jax.ShapeDtypeStruct
    outs = dict(
        layer_out=(shape((rows, width // 4), low), HBM),
        input_grad=(shape((rows, width // 4), low), HBM),
        encoded_grad=(shape((enc_rows // 4, width), low), HBM),
        small_out=(shape((8, width), wide), VM),
    )
    if in_kernel:
        for name, weight in zip(Weights._fields, weights, strict=True):
            outs["grad_" + name] = (shape((piece, weight.shape[1]), wide), VM)
    else:
        outs.update(raw_grads=(shape((4, width, width), low), HBM))
    vmem, dma = pltpu.VMEM, pltpu.SemaphoreType.DMA
    quarter = width // 4
    whole_rows = vmem((rows, width), low)
    hidden_rows = vmem((rows, hidden), low)
    inner_rows = vmem((rows, inner), low)
    own_wide = vmem((chunks, half, width), wide)
    own_low = vmem((chunks, half, width), low)
    scratch = {
        "w_" + name: vmem(weight.shape, low)
        for name, weight in zip(Weights._fields, weights, strict=True)
    }
    scratch.update(
        x=whole_rows,
        g3=whole_rows,
        enc=vmem((2 * enc_len, width), low),
        n1=whole_rows,
        n2=whole_rows,
        n3=whole_rows,
        dh1=whole_rows,
        dh2=whole_rows,
        part=whole_rows,
        act=hidden_rows,
        d_pre=hidden_rows,
        q1=inner_rows,
        k1=inner_rows,
        v1=inner_rows,
        o1=inner_rows,
        q2=inner_rows,
        o2=inner_rows,
        k2=vmem((enc_rows, inner), low),
        v2=vmem((enc_rows, inner), low),
        h1=own_wide,
        h2=own_wide,
        dh=own_wide,
        soft1=vmem((slots, heads * seq, seq), low),
        soft2=vmem((slots, heads * seq, enc_len), low),
        dkv=vmem((slots, 2 * inner, enc_len), low),
        near=own_low,
        mine=own_low,
        far=vmem((2, chunks, half, width), low),
        out_part=vmem((2, 2, half, width), low),
        out_near=own_low,
        out_mine=vmem((chunks, 2, half, width // 2), low),
        out_far=vmem((chunks, half, width // 2), low),
        columns=vmem((2, rows, quarter), low),
        col_send=vmem((2, chunks, half, quarter), low),
        enc_far=vmem((2, enc_len, width), low),
        enc_out=vmem((enc_rows // 4, width), low),
        pre=vmem((CHUNK_SLOTS * seq, hidden), wide),
        bias=vmem((heads * seq, seq), wide),
        table=vmem((heads * seq, seq), wide),
        small=vmem((8, width), wide),
        small_land=vmem((levels + 1, 8, width), wide),
        load_sem=dma((2 + len(weights),)),
        enc_sem=dma((2,)),
        near_sem=dma((2, 5, chunks)),
        far_sem=dma((2, 5, chunks)),
        share_sem=dma((2, 5, chunks)),
        out_near_sem=dma((2, chunks)),
        out_far_sem=dma((2, chunks)),
        col_sem=dma((2, 2, chunks)),
        enc_near_sem=dma((2, 4)),
        enc_far_sem=dma((2, 2)),
        dp_sem=dma((2, 4, levels)),
        small_sem=dma((2, levels + 1)),
        credit_sem=pltpu.SemaphoreType.REGULAR((2, levels)),
    )
    if in_kernel:
        scratch.update(term=vmem((2, dp_count, piece, width), low))
        for level in range(levels):
            count = 1 << (levels - 1 - level)
            scratch["land%d" % level] = vmem((2, count, piece, width), low)
            if level + 1 < levels:
                scratch["hold%d" % level] = vmem((2, count, piece, width), low)
    else:
        scratch.update(term=vmem((2, width, width), low))
    cfg = SimpleNamespace(
        seq=seq,
        enc_len=enc_len,
        slots=slots,
        width=width,
        heads=heads,
        levels=levels,
        in_kernel=in_kernel,
        piece=piece,
    )
    results = pl.pallas_call(
        functools.partial(layer_kernel, cfg, tuple(ins) + tuple(outs) + tuple(scratch)),
        out_shape=tuple(o[0] for o in outs.values()),
        in_specs=[i[1] for i in ins.values()],
        out_specs=tuple(o[1] for o in outs.values()),
        scratch_shapes=list(scratch.values()),
        compiler_params=pltpu.CompilerParams(
            collective_id=1, has_side_effects=True, vmem_limit_bytes=63 * 2**20
        ),
    )(*[i[0] for i in ins.values()])
    out = SimpleNamespace(**dict(zip(outs, results, strict=True)))
    small = out.small_out
    dist_sums = jnp.roll(small[3, : heads * seq].reshape(heads, seq), 1, axis=1)
    table_grad = jnp.dot(dist_sums, bucket_table, precision=highest).T
    if in_kernel:
        grads = [getattr(out, "grad_" + name) for name in Weights._fields]
    else:
        raw = out.raw_grads
        parts = [raw[3][:, i * inner : (i + 1) * inner] for i in range(4)]
        parts += [raw[2][:, i * inner : (i + 1) * inner] for i in range(4)]
        grads = [
            lax.psum_scatter(part.astype(wide), "dp", scatter_dimension=0, tiled=True)
            for part in (*parts, raw[1], raw[0])
        ]
    return (
        out.layer_out,
        out.input_grad,
        out.encoded_grad,
        small[0],
        small[1],
        small[2],
        table_grad,
        *grads,
    )


def solution(mesh):
    columns = P(None, "tensor")
    both = P("dp", "tensor")
    placed = (
        (P("dp", None), P("dp", None), P("dp"), P("dp"), P(), P(), P(), P())
        + (columns,) * 11
        + (P("dp", None),)
    )
    return jax.shard_map(
        per_device,
        mesh=mesh,
        in_specs=placed,
        out_specs=(both, both, P(("dp", "tensor"), None), P(), P(), P(), columns) + (both,) * 10,
        check_vma=False,
    )
```

```python
import functools
from types import SimpleNamespace
from typing import NamedTuple

import jax
import jax.numpy as jnp
from jax import lax
from jax.experimental import pallas as pl
from jax.experimental.pallas import tpu as pltpu
from jax.sharding import PartitionSpec as P

HD = 64
CHUNK_SLOTS = 2
GELU_ROWS = 32

norm_epsilon = 1e-06
masked_score = -1e30
highest = lax.Precision.HIGHEST
MESH = pl.DeviceIdType.MESH
VM = pl.BlockSpec(memory_space=pltpu.VMEM)
SM = pl.BlockSpec(memory_space=pltpu.SMEM)
HBM = pl.BlockSpec(memory_space=pl.ANY)
low = jnp.bfloat16
wide = jnp.float32


def dot(left, right):
    return lax.dot_general(left, right, (((1,), (0,)), ((), ())), preferred_element_type=wide)


def dot_t(left, right):
    return lax.dot_general(left, right, (((1,), (1,)), ((), ())), preferred_element_type=wide)


def t_dot(left, right):
    return lax.dot_general(left, right, (((0,), (0,)), ((), ())), preferred_element_type=wide)


def exact_dot(left, right):
    return jnp.dot(left, right, precision=highest, preferred_element_type=wide)


def inverse_rms(rows):
    return lax.rsqrt(jnp.mean(rows * rows, axis=-1, keepdims=True) + norm_epsilon)


def norm_back(rows, gain, grad):
    inverse = inverse_rms(rows)
    scaled = gain * grad
    inner = jnp.mean(scaled * rows, axis=-1, keepdims=True)
    grad_rows = inverse * scaled - rows * (inverse * inverse * inverse) * inner
    return grad_rows, jnp.sum(grad * rows * inverse, axis=0, keepdims=True)


def tensor_peer(bit):
    return (lax.axis_index("dp"), lax.axis_index("tensor") ^ bit)


def dp_peer(bit):
    return (lax.axis_index("dp") ^ bit, lax.axis_index("tensor"))


def reversed_bits(value, levels):
    return sum(((value >> k) & 1) << (levels - 1 - k) for k in range(levels))


class Weights(NamedTuple):
    query_self: object
    key_self: object
    value_self: object
    output_self: object
    query_cross: object
    key_cross: object
    value_cross: object
    output_cross: object
    hidden_in: object
    hidden_out: object


def layer_kernel(cfg, names, *refs):
    a = SimpleNamespace(**dict(zip(names, refs, strict=True)))
    seq, enc_len, slots, width = cfg.seq, cfg.enc_len, cfg.slots, cfg.width
    heads, levels, in_kernel = cfg.heads, cfg.levels, cfg.in_kernel
    inner = heads * HD
    if in_kernel:
        a.lands = [getattr(a, "land%d" % i) for i in range(levels)]
        a.holds = [getattr(a, "hold%d" % i) for i in range(levels - 1)]
    chunks = slots // CHUNK_SLOTS
    chunk_rows = CHUNK_SLOTS * seq
    half_rows = chunk_rows // 2
    half_width = width // 2
    quarter_width = width // 4
    me = lax.axis_index("tensor")
    core = lax.rem(me, 2)
    y = me // 2
    dp_me = lax.axis_index("dp")
    c_peer, y_peer = tensor_peer(1), tensor_peer(2)

    def rows_of(k, count):
        return pl.ds(pl.multiple_of(k * count, count), count)

    def load(index, src, dst):
        return pltpu.make_async_copy(src, dst, a.load_sem.at[index])

    load_x, load_g = load(0, a.inputs, a.x), load(1, a.out_grad, a.g3)
    loads = Weights(
        *(
            load(2 + i, getattr(a, name), getattr(a, "w_" + name))
            for i, name in enumerate(Weights._fields)
        )
    )
    load_x.start()
    for copy in loads[:4]:
        copy.start()

    def enc_copy(slot, buffer):
        rows = pl.ds(pl.multiple_of(slot * enc_len, enc_len), enc_len)
        return pltpu.make_async_copy(a.encoded.at[rows], a.enc.at[rows_of(buffer, enc_len)], a.enc_sem.at[buffer])

    enc_copy(0, 0).start()
    for copy in loads[4:]:
        copy.start()
    load_g.start()

    barrier = pltpu.get_barrier_semaphore()
    peers = [c_peer, y_peer] + [dp_peer(1 << k) for k in range(levels)]
    for peer in peers:
        pl.semaphore_signal(barrier, inc=1, device_id=peer, device_id_type=MESH)

    gain_self, gain_cross, gain_ffn = (
        ref[...].reshape(1, width) for ref in (a.gain_self, a.gain_cross, a.gain_ffn)
    )

    lane = lax.broadcasted_iota(jnp.int32, (1, inner), 1)
    masks = [jnp.where(lane // HD == h, 1.0, 0.0).astype(wide) for h in range(heads)]
    masks_low = [m.astype(low) for m in masks]
    row_i = lax.broadcasted_iota(jnp.int32, (seq, seq), 0)
    col_i = lax.broadcasted_iota(jnp.int32, (seq, seq), 1)
    bucket = lax.broadcasted_iota(jnp.int32, (a.table_in.shape[1], seq), 0)
    chosen = jnp.where(a.buckets[...] == bucket, 1.0, 0.0).astype(wide)
    per_dist = exact_dot(a.table_in[...], chosen)
    backward = jnp.where((row_i + col_i) % seq == 0, 1.0, 0.0).astype(wide)
    lines = exact_dot(per_dist, backward)
    for h in range(heads):
        line = jnp.broadcast_to(lines[h : h + 1, :], (seq, seq))
        turned = pltpu.roll(line, 0, 1, stride=1, stride_axis=0)
        a.bias[h * seq : (h + 1) * seq, :] = jnp.where(row_i >= col_i, turned, masked_score)
    a.table[...] = jnp.zeros_like(a.table)
    a.small[...] = jnp.zeros_like(a.small)

    def stack(rows):
        return jnp.concatenate([rows * m for m in masks_low], axis=0)

    def unstack(rows):
        return sum(rows[h * seq : (h + 1) * seq] * masks[h] for h in range(heads))

    def softmax(scores):
        peak = jnp.max(scores, axis=-1, keepdims=True)
        terms = jnp.exp(scores - peak)
        return (terms / jnp.sum(terms, axis=-1, keepdims=True)).astype(low)

    def own_rows(k):
        return pl.ds(pl.multiple_of(k * chunk_rows + core * half_rows, half_rows), half_rows)

    def other_rows(k):
        return pl.ds(pl.multiple_of(k * chunk_rows + (1 - core) * half_rows, half_rows), half_rows)

    def remote(src, dst, sems, index, peer):
        return pltpu.make_async_remote_copy(
            src_ref=src,
            dst_ref=dst,
            send_sem=sems.at[(0,) + index],
            recv_sem=sems.at[(1,) + index],
            device_id=peer,
            device_id_type=MESH,
        )

    def near_copy(p, k):
        return remote(a.part.at[other_rows(k)], a.near.at[k], a.near_sem, (p, k), c_peer)

    def far_copy(p, k):
        return remote(a.mine.at[k], a.far.at[p % 2, k], a.far_sem, (p, k), y_peer)

    def y_send(p, k):
        near_copy(p, k).wait()
        a.mine[k] = (a.part[own_rows(k)].astype(wide) + a.near[k].astype(wide)).astype(low)
        far_copy(p, k).start()

    def total(p, k):
        far_copy(p, k).wait()
        return a.mine[k].astype(wide) + a.far[p % 2, k].astype(wide)

    def share_copy(p, k, buffer):
        return remote(buffer.at[own_rows(k)], buffer.at[own_rows(k)], a.share_sem, (p, k), c_peer)

    def each_chunk(body):
        def step(k, carry):
            body(k)
            return carry

        lax.fori_loop(0, chunks, step, 0)

    def phase(p, finish, buffer, compute):
        def body(k):
            finish(k, total(p - 1, k))
            share_copy(p, k, buffer).start()

            @pl.when(k > 0)
            def _():
                y_send(p, k - 1)

            share_copy(p, k, buffer).wait()
            compute(k)
            near_copy(p, k).start()

        each_chunk(body)
        y_send(p, chunks - 1)

    def project(slot, buffer):
        enc_copy(slot, buffer).wait()

        @pl.when(slot + 1 < slots)
        def _():
            enc_copy(slot + 1, 1 - buffer).start()

        rows = rows_of(slot, enc_len)
        a.k2[rows] = dot_t(a.enc[rows_of(buffer, enc_len)], a.w_key_cross[...]).astype(low)
        a.v2[rows] = dot_t(a.enc[rows_of(buffer, enc_len)], a.w_value_cross[...]).astype(low)

    def self_forward(k):
        rows = rows_of(k, chunk_rows)
        x = a.x[rows].astype(wide)
        normed = (x * inverse_rms(x) * gain_self).astype(low)
        a.n1[rows] = normed
        query = dot_t(normed, a.w_query_self[...]).astype(low)
        keys = dot_t(normed, a.w_key_self[...]).astype(low)
        values = dot_t(normed, a.w_value_self[...]).astype(low)
        a.q1[rows], a.k1[rows], a.v1[rows] = query, keys, values
        mixed = []
        for s in range(CHUNK_SLOTS):
            part = slice(s * seq, (s + 1) * seq)
            weights = softmax(dot_t(stack(query[part]), keys[part]) + a.bias[...])
            a.soft1[k * CHUNK_SLOTS + s] = weights
            mixed.append(unstack(dot(weights, values[part])).astype(low))
        mixed = jnp.concatenate(mixed, axis=0)
        a.o1[rows] = mixed
        a.part[rows] = dot(mixed, a.w_output_self[...]).astype(low)

    load_x.wait()
    for copy in loads[:4]:
        copy.wait()

    def phase_zero(k):
        self_forward(k)

        @pl.when(k == 0)
        def _():
            pl.semaphore_wait(barrier, len(peers))
            loads.key_cross.wait()
            loads.value_cross.wait()

        near_copy(0, k).start()
        project(CHUNK_SLOTS * k, 0)
        y_send(0, k)
        project(CHUNK_SLOTS * k + 1, 1)

    each_chunk(phase_zero)
    loads.query_cross.wait()
    loads.output_cross.wait()

    def finish_one(k, term):
        hidden = a.x[own_rows(k)].astype(wide) + term
        a.h1[k] = hidden
        a.n2[own_rows(k)] = (hidden * inverse_rms(hidden) * gain_cross).astype(low)

    def cross_forward(k):
        rows = rows_of(k, chunk_rows)
        query = dot_t(a.n2[rows], a.w_query_cross[...]).astype(low)
        a.q2[rows] = query
        mixed = []
        for s in range(CHUNK_SLOTS):
            slot = k * CHUNK_SLOTS + s
            enc_rows = rows_of(slot, enc_len)
            weights = softmax(dot_t(stack(query[s * seq : (s + 1) * seq]), a.k2[enc_rows]))
            a.soft2[slot] = weights
            mixed.append(unstack(dot(weights, a.v2[enc_rows])).astype(low))
        mixed = jnp.concatenate(mixed, axis=0)
        a.o2[rows] = mixed
        a.part[rows] = dot(mixed, a.w_output_cross[...]).astype(low)

    phase(1, finish_one, a.n2, cross_forward)
    for copy in (loads.hidden_in, loads.hidden_out, load_g):
        copy.wait()

    def limit(slot):
        return jnp.where(slot < a.counts[0], a.lengths[slot], 0)

    def keep_rows(slot, rows):
        pos = lax.broadcasted_iota(jnp.int32, (seq, 1), 0)
        return jnp.where(pos < limit(slot), rows, 0.0)

    def finish_two(k, term):
        hidden = a.h1[k] + term
        a.h2[k] = hidden
        a.n3[own_rows(k)] = (hidden * inverse_rms(hidden) * gain_ffn).astype(low)

    def out_near_copy(k):
        return remote(a.out_part.at[k % 2, 1 - core], a.out_near.at[k], a.out_near_sem, (k,), c_peer)

    def out_far_copy(k):
        return remote(a.out_mine.at[k, 1 - y], a.out_far.at[k], a.out_far_sem, (k,), y_peer)

    def out_send(k):
        out_near_copy(k).wait()
        term = a.out_part[k % 2, core].astype(wide) + a.out_near[k].astype(wide)
        a.out_mine[k, 0] = term[:, :half_width].astype(low)
        a.out_mine[k, 1] = term[:, half_width:].astype(low)
        out_far_copy(k).start()

    scale = 0.7978845608028654

    def feed_forward(k):
        rows = rows_of(k, chunk_rows)
        grad = jnp.concatenate(
            [
                keep_rows(k * CHUNK_SLOTS + s, a.g3[rows_of(k * CHUNK_SLOTS + s, seq)].astype(wide))
                for s in range(CHUNK_SLOTS)
            ],
            axis=0,
        ).astype(low)
        a.g3[rows] = grad
        a.pre[...] = dot(a.n3[rows], a.w_hidden_in[...])

        def gelu_rows(i, carry):
            part = rows_of(i, GELU_ROWS)
            pre = a.pre[part]
            square = pre * pre
            bend = jnp.tanh(scale * pre * (1.0 + 0.044715 * square))
            half = 0.5 * (1.0 + bend)
            curve = scale * (1.0 + 3 * 0.044715 * square)
            a.pre[part] = half + 0.5 * pre * (1.0 - bend * bend) * curve
            target = pl.ds(pl.multiple_of(k * chunk_rows + i * GELU_ROWS, GELU_ROWS), GELU_ROWS)
            a.act[target] = (pre * half).astype(low)
            return carry

        lax.fori_loop(0, chunk_rows // GELU_ROWS, gelu_rows, 0)
        out = dot_t(a.act[rows], a.w_hidden_out[...]).astype(low)
        a.out_part[k % 2, 0] = out[:half_rows]
        a.out_part[k % 2, 1] = out[half_rows:]
        out_near_copy(k).start()
        grad_pre = (a.pre[...] * dot(grad, a.w_hidden_out[...])).astype(low)
        a.d_pre[rows] = grad_pre
        a.part[rows] = dot_t(grad_pre, a.w_hidden_in[...]).astype(low)

    def feed_forward_sends(k):
        feed_forward(k)
        out_send(k)

    phase(2, finish_two, a.n3, feed_forward_sends)

    def column_copy(which, k):
        return remote(
            a.col_send.at[which, k],
            a.columns.at[which, :, own_rows(k)],
            a.col_sem,
            (which, k),
            c_peer,
        )

    def emit_columns(which, k, value):
        value = value.T
        left, right = value[:quarter_width], value[quarter_width:]
        first = core == 0
        a.columns[which, :, own_rows(k)] = jnp.where(first, left, right).astype(low)
        a.col_send[which, k] = jnp.where(first, right, left).astype(low)
        column_copy(which, k).start()

    def my_half(value):
        return jnp.where(y == 0, value[:, :half_width], value[:, half_width:])

    def finish_out(k):
        out_far_copy(k).wait()
        value = my_half(a.h2[k]) + a.out_mine[k, y].astype(wide) + a.out_far[k].astype(wide)
        emit_columns(0, k, keep_rows(k * CHUNK_SLOTS + core, value))

    def dp_rank(level):
        return (dp_me >> level) & 1

    def dp_copy(block, level):
        buffer = block % 2
        count = 1 << (levels - 1 - level)
        source = a.term if level == 0 else a.holds[level - 1]
        part = pl.ds((1 - dp_rank(level)) * count, count)
        return remote(
            source.at[buffer, part],
            a.lands[level].at[buffer],
            a.dp_sem,
            (block, level),
            dp_peer(1 << level),
        )

    def dp_begin(block):
        if in_kernel:
            if block >= 2:
                credit_wait(block, 0)
            dp_copy(block, 0).start()
        else:
            pltpu.make_async_copy(
                a.term.at[block % 2], a.raw_grads.at[block], a.dp_sem.at[0, block, 0]
            ).start()

    def credit_wait(block, level):
        pl.semaphore_wait(a.credit_sem.at[block % 2, level], 1)

    def dp_advance(block, level):
        if not in_kernel:
            return
        buffer = block % 2
        count = 1 << (levels - 1 - level)
        dp_copy(block, level).wait()
        source = a.term if level == 0 else a.holds[level - 1]
        land = a.lands[level]
        part = pl.ds(dp_rank(level) * count, count)
        value = source[buffer, part].astype(wide) + land[buffer].astype(wide)
        if level == levels - 1:
            emit_grads(block, value[0])
        else:
            a.holds[level][buffer] = value.astype(low)
        if block < 2:
            pl.semaphore_signal(
                a.credit_sem.at[buffer, level],
                inc=1,
                device_id=dp_peer(1 << level),
                device_id_type=MESH,
            )
        if level + 1 < levels:
            if block >= 2:
                credit_wait(block, level + 1)
            dp_copy(block, level + 1).start()

    def dp_finish_raw(block):
        if not in_kernel:
            pltpu.make_async_copy(
                a.term.at[block % 2], a.raw_grads.at[block], a.dp_sem.at[0, block, 0]
            ).wait()

    def emit_grads(block, value):
        if block == 0:
            a.grad_hidden_out[...] = value
        elif block == 1:
            a.grad_hidden_in[...] = value
        else:
            names = Weights._fields[4:8] if block == 2 else Weights._fields[:4]
            for i, name in enumerate(names):
                getattr(a, "grad_" + name)[...] = value[:, i * inner : (i + 1) * inner]

    piece = cfg.piece
    groups = 2
    group_rows = width // groups
    pieces_each = max(group_rows // piece, 1) if in_kernel else 1

    def store_pieces(block, g, rows):
        if in_kernel:
            for i in range(pieces_each):
                for gg in range(groups):
                    index = reversed_bits(gg * pieces_each + i, levels)
                    if gg == g:
                        a.term[block % 2, index] = rows[i * piece : (i + 1) * piece]
        else:
            a.term[block % 2, g * group_rows : (g + 1) * group_rows] = rows

    def plain_grads(block, left, right):
        for g in range(groups):
            columns = slice(g * group_rows, (g + 1) * group_rows)
            store_pieces(block, g, t_dot(left[:, columns], right[...]).astype(low))

    def turned_grads(block):
        for g in range(groups):
            columns = slice(g * group_rows, (g + 1) * group_rows)
            store_pieces(block, g, a.enc[all_turned, columns].T)

    def turned_rows(i):
        return slice(i * inner, (i + 1) * inner)

    all_turned = slice(0, 4 * inner)

    plain_grads(0, a.g3, a.act)
    dp_begin(0)
    plain_grads(1, a.n3, a.d_pre)
    dp_begin(1)

    def add_gain(index, value):
        a.small[index : index + 1, :] += value

    def finish_three(k, term):
        grad_rows, grad_gain = norm_back(a.h2[k], gain_ffn, term)
        add_gain(2, grad_gain)
        grad = a.g3[own_rows(k)].astype(wide) + grad_rows
        a.dh[k] = grad
        a.dh2[own_rows(k)] = grad.astype(low)
        finish_out(k)

    def score_back(soft, grad_soft):
        weights = soft.astype(wide)
        row_inner = jnp.sum(weights * grad_soft, axis=-1, keepdims=True)
        return (weights * (grad_soft - row_inner)).astype(low)

    def cross_backward(k):
        rows = rows_of(k, chunk_rows)
        grad_mixed = dot_t(a.dh2[rows], a.w_output_cross[...]).astype(low)
        query = a.q2[rows]
        grads = []
        for s in range(CHUNK_SLOTS):
            slot = k * CHUNK_SLOTS + s
            part = slice(s * seq, (s + 1) * seq)
            enc_rows = rows_of(slot, enc_len)
            tall_grad, tall_query = stack(grad_mixed[part]), stack(query[part])
            soft = a.soft2[slot]
            grad_scores = score_back(soft, dot_t(tall_grad, a.v2[enc_rows]))
            a.dkv[slot, :inner] = t_dot(tall_query, grad_scores).astype(low)
            a.dkv[slot, inner:] = t_dot(tall_grad, soft).astype(low)
            grads.append(unstack(dot(grad_scores, a.k2[enc_rows])).astype(low))
        grads = jnp.concatenate(grads, axis=0)
        a.q2[rows] = grads
        a.part[rows] = dot(grads, a.w_query_cross[...]).astype(low)

        @pl.when(k == 2)
        def _():
            dp_advance(0, 0)

    phase(3, finish_three, a.dh2, cross_backward)

    kv_blocks = 2 * inner // half_rows
    for i in range(kv_blocks):
        a.h2[i] = jnp.zeros_like(a.h2[i])

    def enc_slots(j, own):
        which = jnp.where(own == 1, core, 1 - core)
        side = jnp.where(j < 2, 1 - y, y)
        return 4 * side + 2 * which + lax.rem(j, 2)

    def enc_partial(slot, buffer):
        key_grad, value_grad = a.dkv[slot, :inner], a.dkv[slot, inner:]
        for i in range(kv_blocks):
            part = slice(i * half_rows, (i + 1) * half_rows)
            a.h2[i] += dot(a.dkv[slot, part], a.enc[rows_of(buffer, enc_len)])
        return t_dot(key_grad, a.w_key_cross[...]) + t_dot(value_grad, a.w_value_cross[...])

    def enc_half(j):
        return rows_of(lax.rem(j, 2), enc_len)

    def enc_near_copy(j):
        source = a.n3.at[enc_half(j)]
        target = a.act if j < 2 else a.d_pre
        return remote(source, target.at[enc_half(j)], a.enc_near_sem, (j,), c_peer)

    def enc_far_copy(j):
        return remote(a.g3.at[enc_half(j)], a.enc_far.at[j], a.enc_far_sem, (j,), y_peer)

    enc_copy(enc_slots(0, 0), 0).start()
    for j in range(4):
        enc_copy(enc_slots(j, 0), 0).wait()
        enc_copy(enc_slots(j, 1), 1).start()
        if j >= 2:
            enc_near_copy(j - 2).wait_send()
        a.n3[enc_half(j)] = enc_partial(enc_slots(j, 0), 0).astype(low)
        enc_near_copy(j).start()
        enc_copy(enc_slots(j, 1), 1).wait()
        if j < 3:
            enc_copy(enc_slots(j + 1, 0), 0).start()
        partial = enc_partial(enc_slots(j, 1), 1)
        enc_near_copy(j).wait_recv()
        if j < 2:
            a.g3[enc_half(j)] = (partial + a.act[enc_half(j)].astype(wide)).astype(low)
            enc_far_copy(j).start()
        else:
            a.enc_out[rows_of(j - 2, enc_len)] = (
                partial + a.d_pre[enc_half(j)].astype(wide)
            ).astype(low)
    dp_advance(1, 0)
    dp_advance(0, 1)

    a.enc[turned_rows(0)] = t_dot(a.q2[...], a.n2[...]).astype(low)
    for i in range(kv_blocks):
        a.enc[inner + i * half_rows : inner + (i + 1) * half_rows] = a.h2[i].astype(low)
    a.enc[turned_rows(3)] = t_dot(a.o2[...], a.dh2[...]).astype(low)
    dp_finish_raw(0)
    turned_grads(2)
    dp_begin(2)

    def finish_four(k, term):
        grad_rows, grad_gain = norm_back(a.h1[k], gain_cross, term)
        add_gain(1, grad_gain)
        grad = a.dh[k] + grad_rows
        a.dh[k] = grad
        a.dh1[own_rows(k)] = grad.astype(low)

    def self_backward(k):
        rows = rows_of(k, chunk_rows)
        grad_mixed = dot_t(a.dh1[rows], a.w_output_self[...]).astype(low)
        query, keys, values = a.q1[rows], a.k1[rows], a.v1[rows]
        grads = [[], [], []]
        for s in range(CHUNK_SLOTS):
            part = slice(s * seq, (s + 1) * seq)
            tall_grad, tall_query = stack(grad_mixed[part]), stack(query[part])
            soft = a.soft1[k * CHUNK_SLOTS + s]
            grad_scores = score_back(soft, dot_t(tall_grad, values[part]))
            a.table[...] += grad_scores.astype(wide)
            grads[0].append(unstack(dot(grad_scores, keys[part])).astype(low))
            grads[1].append(t_dot(grad_scores, tall_query).astype(low))
            grads[2].append(t_dot(soft, tall_grad).astype(low))
        grads = [jnp.concatenate(g, axis=0) for g in grads]
        a.q1[rows], a.k1[rows], a.v1[rows] = grads
        a.part[rows] = (
            dot(grads[0], a.w_query_self[...])
            + dot(grads[1], a.w_key_self[...])
            + dot(grads[2], a.w_value_self[...])
        ).astype(low)

    phase(4, finish_four, a.dh1, self_backward)
    dp_advance(1, 1)
    dp_advance(0, 2)
    dp_advance(1, 2)
    a.enc[turned_rows(0)] = t_dot(a.q1[...], a.n1[...]).astype(low)
    a.enc[turned_rows(1)] = t_dot(a.k1[...], a.n1[...]).astype(low)
    a.enc[turned_rows(2)] = t_dot(a.v1[...], a.n1[...]).astype(low)
    a.enc[turned_rows(3)] = t_dot(a.o1[...], a.dh1[...]).astype(low)
    dp_finish_raw(1)
    turned_grads(3)
    dp_begin(3)
    dp_advance(2, 0)

    def phase_five(k):
        grad_rows, grad_gain = norm_back(
            a.x[own_rows(k)].astype(wide), gain_self, total(4, k)
        )
        add_gain(0, grad_gain)
        emit_columns(1, k, my_half(a.dh[k] + grad_rows))

    each_chunk(phase_five)

    mirror = jnp.where(row_i + col_i == seq - 1, 1.0, 0.0).astype(wide)
    for h in range(heads):
        flipped = exact_dot(a.table[h * seq : (h + 1) * seq, :], mirror)
        turned = pltpu.roll(flipped, 0, 1, stride=1, stride_axis=0)
        a.small[3:4, h * seq : (h + 1) * seq] = jnp.sum(turned, axis=0, keepdims=True)

    def small_copy(i):
        peer = c_peer if i == 0 else dp_peer(1 << (i - 1))
        return remote(a.small, a.small_land.at[i], a.small_sem, (i,), peer)

    small_copy(0).start()
    dp_advance(2, 1)
    small_copy(0).wait()
    row = lax.broadcasted_iota(jnp.int32, a.small.shape, 0)
    a.small[...] += jnp.where(row < 3, a.small_land[0], 0.0)
    for i in range(1, levels + 1):
        small_copy(i).start()
        if i == 1:
            dp_advance(3, 0)
        if i == 2:
            dp_advance(2, 2)
        small_copy(i).wait()
        a.small[...] += a.small_land[i]
    dp_advance(3, 1)
    dp_advance(3, 2)
    dp_finish_raw(2)
    dp_finish_raw(3)

    for j in range(2):
        enc_far_copy(j).wait()
        a.enc_out[rows_of(j, enc_len)] = (
            a.enc_out[rows_of(j, enc_len)].astype(wide) + a.enc_far[j].astype(wide)
        ).astype(low)
        enc_near_copy(2 + j).wait_send()
    for k in range(chunks):
        column_copy(0, k).wait()
        column_copy(1, k).wait()
    stores = [
        load(0, a.columns.at[0], a.layer_out),
        load(1, a.columns.at[1], a.input_grad),
        load(2, a.enc_out, a.encoded_grad),
    ]
    for store in stores:
        store.start()
    a.small_out[...] = a.small[...]
    for store in stores:
        store.wait()


def finish_kernel(count, heads, seq, *refs):
    small, buckets = refs[count], refs[count + 1]
    targets, held, sems = refs[count + 2 : 2 * count + 6], refs[2 * count + 6 : -1], refs[-1]
    copies = [pltpu.make_async_copy(refs[i], held[i], sems.at[i]) for i in range(count)]
    for copy in copies:
        copy.start()
    for i in range(count):
        copies[i].wait()
        copies[i] = pltpu.make_async_copy(held[i], targets[i], sems.at[i])
        copies[i].start()
    for i in range(3):
        targets[count + i][...] = small[i, :]
    sums = jnp.concatenate([small[3:4, h * seq : (h + 1) * seq] for h in range(heads)], axis=0)
    by_lane = pltpu.roll(jnp.broadcast_to(buckets[...], (8, seq)), seq - 1, 1)[:1]
    kinds = targets[count + 3].shape[1]
    bucket = lax.broadcasted_iota(jnp.int32, (kinds, seq), 0)
    chosen = jnp.where(by_lane == bucket, 1.0, 0.0).astype(wide)
    targets[count + 3][...] = lax.dot_general(
        sums,
        chosen,
        (((1,), (1,)), ((), ())),
        precision=highest,
        preferred_element_type=wide,
    )
    for copy in copies:
        copy.wait()


def per_device(*args):
    (
        inputs,
        encoded,
        example_counts,
        lengths,
        buckets,
        gain_self,
        gain_cross,
        gain_ffn,
        bias_table,
    ) = args[:9]
    weights = args[9:19]
    out_grad = args[19]
    rows, width = inputs.shape
    seq = buckets.shape[0]
    slots = lengths.shape[0]
    enc_rows = encoded.shape[0]
    enc_len = enc_rows // slots
    inner = weights[0].shape[1]
    hidden = weights[8].shape[1]
    heads = inner // HD
    dp_count = lax.axis_size("dp")
    levels = dp_count.bit_length() - 1
    piece = width // dp_count
    in_kernel = piece % 16 == 0
    chunks = slots // CHUNK_SLOTS
    half = CHUNK_SLOTS * seq // 2

    ins = dict(
        lengths=(lengths, SM),
        counts=(example_counts, SM),
        gain_self=(gain_self, VM),
        gain_cross=(gain_cross, VM),
        gain_ffn=(gain_ffn, VM),
        table_in=(bias_table.T, VM),
        buckets=(buckets[None], VM),
        inputs=(inputs, HBM),
        encoded=(encoded, HBM),
        out_grad=(out_grad, HBM),
    )
    for name, weight in zip(Weights._fields, weights, strict=True):
        ins[name] = (weight, HBM)
    for name in Weights._fields[:8]:
        ins[name] = (ins[name][0].T, HBM)
    shape = jax.ShapeDtypeStruct
    outs = dict(
        layer_out=(shape((width // 4, rows), low), HBM),
        input_grad=(shape((width // 4, rows), low), HBM),
        encoded_grad=(shape((enc_rows // 4, width), low), HBM),
        small_out=(shape((8, width), wide), VM),
    )
    if in_kernel:
        for name, weight in zip(Weights._fields, weights, strict=True):
            outs["grad_" + name] = (shape((piece, weight.shape[1]), wide), VM)
    else:
        outs.update(raw_grads=(shape((4, width, width), low), HBM))
    vmem, dma = pltpu.VMEM, pltpu.SemaphoreType.DMA
    quarter = width // 4
    whole_rows = vmem((rows, width), low)
    hidden_rows = vmem((rows, hidden), low)
    inner_rows = vmem((rows, inner), low)
    own_wide = vmem((chunks, half, width), wide)
    own_low = vmem((chunks, half, width), low)
    scratch = {
        "w_" + name: vmem(ins[name][0].shape, low) for name in Weights._fields
    }
    scratch.update(
        x=whole_rows,
        g3=whole_rows,
        enc=vmem((2 * enc_len, width), low),
        n1=whole_rows,
        n2=whole_rows,
        n3=whole_rows,
        dh1=whole_rows,
        dh2=whole_rows,
        part=whole_rows,
        act=hidden_rows,
        d_pre=hidden_rows,
        q1=inner_rows,
        k1=inner_rows,
        v1=inner_rows,
        o1=inner_rows,
        q2=inner_rows,
        o2=inner_rows,
        k2=vmem((enc_rows, inner), low),
        v2=vmem((enc_rows, inner), low),
        h1=own_wide,
        h2=own_wide,
        dh=own_wide,
        soft1=vmem((slots, heads * seq, seq), low),
        soft2=vmem((slots, heads * seq, enc_len), low),
        dkv=vmem((slots, 2 * inner, enc_len), low),
        near=own_low,
        mine=own_low,
        far=vmem((2, chunks, half, width), low),
        out_part=vmem((2, 2, half, width), low),
        out_near=own_low,
        out_mine=vmem((chunks, 2, half, width // 2), low),
        out_far=vmem((chunks, half, width // 2), low),
        columns=vmem((2, quarter, rows), low),
        col_send=vmem((2, chunks, quarter, half), low),
        enc_far=vmem((2, enc_len, width), low),
        enc_out=vmem((enc_rows // 4, width), low),
        pre=vmem((CHUNK_SLOTS * seq, hidden), wide),
        bias=vmem((heads * seq, seq), wide),
        table=vmem((heads * seq, seq), wide),
        small=vmem((8, width), wide),
        small_land=vmem((levels + 1, 8, width), wide),
        load_sem=dma((2 + len(weights),)),
        enc_sem=dma((2,)),
        near_sem=dma((2, 5, chunks)),
        far_sem=dma((2, 5, chunks)),
        share_sem=dma((2, 5, chunks)),
        out_near_sem=dma((2, chunks)),
        out_far_sem=dma((2, chunks)),
        col_sem=dma((2, 2, chunks)),
        enc_near_sem=dma((2, 4)),
        enc_far_sem=dma((2, 2)),
        dp_sem=dma((2, 4, levels)),
        small_sem=dma((2, levels + 1)),
        credit_sem=pltpu.SemaphoreType.REGULAR((2, levels)),
    )
    if in_kernel:
        scratch.update(term=vmem((2, dp_count, piece, width), low))
        for level in range(levels):
            count = 1 << (levels - 1 - level)
            scratch["land%d" % level] = vmem((2, count, piece, width), low)
            if level + 1 < levels:
                scratch["hold%d" % level] = vmem((2, count, piece, width), low)
    else:
        scratch.update(term=vmem((2, width, width), low))
    cfg = SimpleNamespace(
        seq=seq,
        enc_len=enc_len,
        slots=slots,
        width=width,
        heads=heads,
        levels=levels,
        in_kernel=in_kernel,
        piece=piece,
    )
    results = pl.pallas_call(
        functools.partial(layer_kernel, cfg, tuple(ins) + tuple(outs) + tuple(scratch)),
        out_shape=tuple(o[0] for o in outs.values()),
        in_specs=[i[1] for i in ins.values()],
        out_specs=tuple(o[1] for o in outs.values()),
        scratch_shapes=list(scratch.values()),
        compiler_params=pltpu.CompilerParams(
            collective_id=1, has_side_effects=True, vmem_limit_bytes=63 * 2**20
        ),
    )(*[i[0] for i in ins.values()])
    moved = [i for i, name in enumerate(outs) if name not in ("small_out", "raw_grads")]
    buckets_row = buckets[None]
    kinds = bias_table.shape[0]
    finals = pl.pallas_call(
        functools.partial(finish_kernel, len(moved), heads, seq),
        out_shape=(
            *(shape(results[i].shape, results[i].dtype) for i in moved),
            *(shape((width,), wide) for _ in range(3)),
            shape((heads, kinds), wide),
        ),
        in_specs=[HBM] * len(moved) + [VM, VM],
        out_specs=(HBM,) * len(moved) + (VM,) * 4,
        scratch_shapes=[
            *(vmem(results[i].shape, results[i].dtype) for i in moved),
            dma((len(moved),)),
        ],
    )(*[results[i] for i in moved], results[3], buckets_row)
    if in_kernel:
        grads = finals[3 : len(moved)]
    else:
        raw = results[4]
        parts = [raw[3][:, i * inner : (i + 1) * inner] for i in range(4)]
        parts += [raw[2][:, i * inner : (i + 1) * inner] for i in range(4)]
        grads = [
            lax.psum_scatter(part.astype(wide), "dp", scatter_dimension=0, tiled=True)
            for part in (*parts, raw[1], raw[0])
        ]
    gains = finals[len(moved) : len(moved) + 3]
    return (finals[0].T, finals[1].T, finals[2], *gains, finals[-1].T, *grads)


def solution(mesh):
    columns = P(None, "tensor")
    both = P("dp", "tensor")
    placed = (
        (P("dp", None), P("dp", None), P("dp"), P("dp"), P(), P(), P(), P())
        + (columns,) * 11
        + (P("dp", None),)
    )
    return jax.shard_map(
        per_device,
        mesh=mesh,
        in_specs=placed,
        out_specs=(both, both, P(("dp", "tensor"), None), P(), P(), P(), columns) + (both,) * 10,
        check_vma=False,
    )
```

```python
import functools
from types import SimpleNamespace
from typing import NamedTuple

import jax
import jax.numpy as jnp
from jax import lax
from jax.experimental import pallas as pl
from jax.experimental.pallas import tpu as pltpu
from jax.sharding import PartitionSpec as P

HD = 64
CHUNK_SLOTS = 2
GELU_ROWS = 32

norm_epsilon = 1e-06
masked_score = -1e30
highest = lax.Precision.HIGHEST
MESH = pl.DeviceIdType.MESH
VM = pl.BlockSpec(memory_space=pltpu.VMEM)
SM = pl.BlockSpec(memory_space=pltpu.SMEM)
HBM = pl.BlockSpec(memory_space=pl.ANY)
low = jnp.bfloat16
wide = jnp.float32


def dot(left, right):
    return lax.dot_general(left, right, (((1,), (0,)), ((), ())), preferred_element_type=wide)


def dot_t(left, right):
    return lax.dot_general(left, right, (((1,), (1,)), ((), ())), preferred_element_type=wide)


def t_dot(left, right):
    return lax.dot_general(left, right, (((0,), (0,)), ((), ())), preferred_element_type=wide)


def exact_dot(left, right):
    return jnp.dot(left, right, precision=highest, preferred_element_type=wide)


def inverse_rms(rows):
    return lax.rsqrt(jnp.mean(rows * rows, axis=-1, keepdims=True) + norm_epsilon)


def norm_back(rows, gain, grad):
    inverse = inverse_rms(rows)
    scaled = gain * grad
    inner = jnp.mean(scaled * rows, axis=-1, keepdims=True)
    grad_rows = inverse * scaled - rows * (inverse * inverse * inverse) * inner
    return grad_rows, jnp.sum(grad * rows * inverse, axis=0, keepdims=True)


def tensor_peer(bit):
    return (lax.axis_index("dp"), lax.axis_index("tensor") ^ bit)


def dp_peer(bit):
    return (lax.axis_index("dp") ^ bit, lax.axis_index("tensor"))


def piece_index(rank, order):
    return sum(((rank >> bit) & 1) << (len(order) - 1 - k) for k, bit in enumerate(order))


class Weights(NamedTuple):
    query_self: object
    key_self: object
    value_self: object
    output_self: object
    query_cross: object
    key_cross: object
    value_cross: object
    output_cross: object
    hidden_in: object
    hidden_out: object


def layer_kernel(cfg, names, *refs):
    a = SimpleNamespace(**dict(zip(names, refs, strict=True)))
    seq, enc_len, slots, width = cfg.seq, cfg.enc_len, cfg.slots, cfg.width
    heads, levels, in_kernel = cfg.heads, cfg.levels, cfg.in_kernel
    inner = heads * HD
    if in_kernel:
        a.lands = [getattr(a, "land%d" % i) for i in range(levels)]
        a.holds = [getattr(a, "hold%d" % i) for i in range(levels - 1)]
    chunks = slots // CHUNK_SLOTS
    chunk_rows = CHUNK_SLOTS * seq
    half_rows = chunk_rows // 2
    half_width = width // 2
    quarter_width = width // 4
    me = lax.axis_index("tensor")
    core = lax.rem(me, 2)
    y = me // 2
    dp_me = lax.axis_index("dp")
    c_peer, y_peer = tensor_peer(1), tensor_peer(2)

    def rows_of(k, count):
        return pl.ds(pl.multiple_of(k * count, count), count)

    def load(index, src, dst):
        return pltpu.make_async_copy(src, dst, a.load_sem.at[index])

    inner_rows = slice(0, inner), slice(inner, 2 * inner)
    first_rows, later_rows = pl.ds(0, chunk_rows), pl.ds(chunk_rows, slots * seq - chunk_rows)
    load_x = load(0, a.inputs.at[first_rows], a.x.at[first_rows])
    load_more = load(2 + len(Weights._fields), a.inputs.at[later_rows], a.x.at[later_rows])
    load_g = load(1, a.out_grad, a.g3)
    spots = {name: getattr(a, "w_" + name) for name in Weights._fields if hasattr(a, "w_" + name)}
    spots.update(key_cross=a.w_kv.at[inner_rows[0]], value_cross=a.w_kv.at[inner_rows[1]])
    loads = Weights(
        *(load(2 + i, getattr(a, name), spots[name]) for i, name in enumerate(Weights._fields))
    )
    load_x.start()
    for copy in loads[:3]:
        copy.start()
    loads.key_cross.start()
    loads.value_cross.start()
    loads.output_self.start()
    load_more.start()

    def enc_copy(slot, buffer):
        rows = pl.ds(pl.multiple_of(slot * enc_len, enc_len), enc_len)
        return pltpu.make_async_copy(a.encoded.at[rows], a.enc.at[rows_of(buffer, enc_len)], a.enc_sem.at[buffer])

    enc_copy(0, 0).start()
    for copy in (loads.query_cross, loads.output_cross, loads.hidden_in, loads.hidden_out, load_g):
        copy.start()

    barrier = pltpu.get_barrier_semaphore()
    peers = [c_peer, y_peer] + [dp_peer(1 << k) for k in range(levels)]
    for peer in peers:
        pl.semaphore_signal(barrier, inc=1, device_id=peer, device_id_type=MESH)

    gain_self, gain_cross, gain_ffn = (
        ref[...].reshape(1, width) for ref in (a.gain_self, a.gain_cross, a.gain_ffn)
    )

    lane = lax.broadcasted_iota(jnp.int32, (1, inner), 1)
    masks = [jnp.where(lane // HD == h, 1.0, 0.0).astype(wide) for h in range(heads)]
    masks_low = [m.astype(low) for m in masks]
    row_i = lax.broadcasted_iota(jnp.int32, (seq, seq), 0)
    col_i = lax.broadcasted_iota(jnp.int32, (seq, seq), 1)
    bucket = lax.broadcasted_iota(jnp.int32, (a.table_in.shape[1], seq), 0)
    chosen = jnp.where(a.buckets[...] == bucket, 1.0, 0.0).astype(wide)
    per_dist = exact_dot(a.table_in[...], chosen)
    backward = jnp.where((row_i + col_i) % seq == 0, 1.0, 0.0).astype(wide)
    lines = exact_dot(per_dist, backward)
    for h in range(heads):
        line = jnp.broadcast_to(lines[h : h + 1, :], (seq, seq))
        turned = pltpu.roll(line, 0, 1, stride=1, stride_axis=0)
        a.bias[h * seq : (h + 1) * seq, :] = jnp.where(row_i >= col_i, turned, masked_score)
    a.table[...] = jnp.zeros_like(a.table)
    a.small[...] = jnp.zeros_like(a.small)

    def stack(rows):
        return jnp.concatenate([rows * m for m in masks_low], axis=0)

    def unstack(rows):
        return sum(rows[h * seq : (h + 1) * seq] * masks[h] for h in range(heads))

    def softmax(scores):
        peak = jnp.max(scores, axis=-1, keepdims=True)
        terms = jnp.exp(scores - peak)
        return (terms / jnp.sum(terms, axis=-1, keepdims=True)).astype(low)

    def own_rows(k):
        return pl.ds(pl.multiple_of(k * chunk_rows + core * half_rows, half_rows), half_rows)

    def other_rows(k):
        return pl.ds(pl.multiple_of(k * chunk_rows + (1 - core) * half_rows, half_rows), half_rows)

    def remote(src, dst, sems, index, peer):
        return pltpu.make_async_remote_copy(
            src_ref=src,
            dst_ref=dst,
            send_sem=sems.at[(0,) + index],
            recv_sem=sems.at[(1,) + index],
            device_id=peer,
            device_id_type=MESH,
        )

    def add_gain(index, value):
        a.small[index : index + 1, :] += value

    def near_copy(p, k):
        return remote(a.part.at[other_rows(k)], a.near.at[k], a.near_sem, (p, k), c_peer)

    def far_copy(p, k):
        return remote(a.mine.at[k], a.far.at[p % 2, k], a.far_sem, (p, k), y_peer)

    def y_send(p, k):
        near_copy(p, k).wait()
        a.mine[k] = (a.part[own_rows(k)].astype(wide) + a.near[k].astype(wide)).astype(low)
        far_copy(p, k).start()

    def last_copies(k):
        return (
            remote(
                a.mine.at[k, :, pl.ds(0, half_width)],
                a.far.at[0, k, :, pl.ds(0, half_width)],
                a.far_sem,
                (4, k),
                y_peer,
            ),
            remote(a.inner_send.at[k], a.inner_far.at[k], a.inner_sem, (k,), y_peer),
        )

    def y_send_last(k):
        near_copy(4, k).wait()
        term = a.part[own_rows(k)].astype(wide) + a.near[k].astype(wide)
        a.h1[k] = term
        rows = a.x[own_rows(k)].astype(wide)
        product = term * rows
        row_inner = jnp.sum(product * gain_self, axis=-1, keepdims=True)
        add_gain(0, jnp.sum(product * inverse_rms(rows), axis=0, keepdims=True))
        a.inner_send[k] = jnp.broadcast_to(row_inner, (half_rows, half_rows)).T[:8]
        a.mine[k, :, :half_width] = jnp.where(
            y == 0, term[:, half_width:], term[:, :half_width]
        ).astype(low)
        for copy in last_copies(k):
            copy.start()

    def total(p, k):
        far_copy(p, k).wait()
        return a.mine[k].astype(wide) + a.far[p % 2, k].astype(wide)

    def share_copy(p, k, buffer):
        return remote(buffer.at[own_rows(k)], buffer.at[own_rows(k)], a.share_sem, (p, k), c_peer)

    def each_chunk(body):
        def step(k, carry):
            body(k)
            return carry

        lax.fori_loop(0, chunks, step, 0)

    def phase(p, finish, buffer, compute, extra=None, send=None):
        send = send or functools.partial(y_send, p)

        def body(k):
            finish(k, total(p - 1, k))
            share_copy(p, k, buffer).start()

            @pl.when(k > 0)
            def _():
                send(k - 1)

            share_copy(p, k, buffer).wait()
            compute(k)
            near_copy(p, k).start()
            if extra is not None:
                extra(k)

        each_chunk(body)
        send(chunks - 1)

    def project(slot, buffer):
        enc_copy(slot, buffer).wait()

        @pl.when(slot + 1 < slots)
        def _():
            enc_copy(slot + 1, 1 - buffer).start()

        rows = rows_of(slot, enc_len)
        a.k2[rows] = dot_t(a.enc[rows_of(buffer, enc_len)], a.w_kv[:inner]).astype(low)
        a.v2[rows] = dot_t(a.enc[rows_of(buffer, enc_len)], a.w_kv[inner : 2 * inner]).astype(low)

    def self_forward(k):
        rows = rows_of(k, chunk_rows)
        x = a.x[rows].astype(wide)
        normed = (x * inverse_rms(x) * gain_self).astype(low)
        a.n1[rows] = normed
        query = dot_t(normed, a.w_query_self[...]).astype(low)
        keys = dot_t(normed, a.w_key_self[...]).astype(low)
        values = dot_t(normed, a.w_value_self[...]).astype(low)
        a.q1[rows], a.k1[rows], a.v1[rows] = query, keys, values
        mixed = []
        for s in range(CHUNK_SLOTS):
            part = slice(s * seq, (s + 1) * seq)
            weights = softmax(dot_t(stack(query[part]), keys[part]) + a.bias[...])
            a.soft1[k * CHUNK_SLOTS + s] = weights
            mixed.append(unstack(dot(weights, values[part])).astype(low))
        mixed = jnp.concatenate(mixed, axis=0)
        a.o1[rows] = mixed
        a.part[rows] = dot(mixed, a.w_output_self[...]).astype(low)

    def peer_weights():
        own, theirs = pl.ds(0, 2 * inner), pl.ds(2 * inner, 2 * inner)
        return remote(a.w_kv.at[own], a.w_kv.at[theirs], a.kv_sem, (0,), y_peer)

    loads.key_cross.wait()
    loads.value_cross.wait()
    pl.semaphore_wait(barrier, len(peers))
    peer_weights().start()
    load_x.wait()
    for copy in loads[:4]:
        copy.wait()

    def phase_zero(k):
        @pl.when(k == 1)
        def _():
            load_more.wait()

        self_forward(k)
        near_copy(0, k).start()
        y_send(0, k)
        project(CHUNK_SLOTS * k, 0)
        project(CHUNK_SLOTS * k + 1, 1)

    each_chunk(phase_zero)
    loads.query_cross.wait()
    loads.output_cross.wait()
    peer_weights().wait()

    chip_slots = slots // 2

    def chip_slot(k):
        return chip_slots * y + k

    enc_copy(chip_slot(0), 0).start()

    def project_peer(k):
        buffer = lax.rem(k, 2)
        enc_copy(chip_slot(k), buffer).wait()

        @pl.when(k + 1 < chip_slots)
        def _():
            enc_copy(chip_slot(k + 1), 1 - buffer).start()

        rows = rows_of(k, enc_len)
        encoded = a.enc[rows_of(buffer, enc_len)]
        a.k2_peer[rows] = dot_t(encoded, a.w_kv[2 * inner : 3 * inner]).astype(low)
        a.v2_peer[rows] = dot_t(encoded, a.w_kv[3 * inner :]).astype(low)

    def finish_one(k, term):
        hidden = a.x[own_rows(k)].astype(wide) + term
        a.h1[k] = hidden
        a.n2[own_rows(k)] = (hidden * inverse_rms(hidden) * gain_cross).astype(low)

    def cross_forward(k):
        rows = rows_of(k, chunk_rows)
        query = dot_t(a.n2[rows], a.w_query_cross[...]).astype(low)
        a.q2[rows] = query
        mixed = []
        for s in range(CHUNK_SLOTS):
            slot = k * CHUNK_SLOTS + s
            enc_rows = rows_of(slot, enc_len)
            weights = softmax(dot_t(stack(query[s * seq : (s + 1) * seq]), a.k2[enc_rows]))
            a.soft2[slot] = weights
            mixed.append(unstack(dot(weights, a.v2[enc_rows])).astype(low))
        mixed = jnp.concatenate(mixed, axis=0)
        a.o2[rows] = mixed
        a.part[rows] = dot(mixed, a.w_output_cross[...]).astype(low)

    phase(1, finish_one, a.n2, cross_forward, project_peer)
    for copy in (loads.hidden_in, loads.hidden_out, load_g):
        copy.wait()

    def limit(slot):
        return jnp.where(slot < a.counts[0], a.lengths[slot], 0)

    def keep_rows(slot, rows):
        pos = lax.broadcasted_iota(jnp.int32, (seq, 1), 0)
        return jnp.where(pos < limit(slot), rows, 0.0)

    def finish_two(k, term):
        hidden = a.h1[k] + term
        a.h2[k] = hidden
        a.n3[own_rows(k)] = (hidden * inverse_rms(hidden) * gain_ffn).astype(low)

    def out_near_copy(k):
        return remote(a.out_part.at[k % 2, 1 - core], a.out_near.at[k], a.out_near_sem, (k,), c_peer)

    def out_far_copy(k):
        return remote(a.out_mine.at[k], a.out_far.at[k], a.out_far_sem, (k,), y_peer)

    def my_half(value):
        return jnp.where(y == 0, value[:, :half_width], value[:, half_width:])

    def other_half(value):
        return jnp.where(y == 0, value[:, half_width:], value[:, :half_width])

    def out_gather(k):
        out_near_copy(k).wait()
        term = a.out_part[k % 2, core].astype(wide) + a.out_near[k].astype(wide)
        a.out_mine[k] = other_half(term).astype(low)
        a.out_keep[k] = my_half(term) + my_half(a.h2[k])

    scale = 0.7978845608028654

    def feed_forward(k):
        rows = rows_of(k, chunk_rows)
        grad = jnp.concatenate(
            [
                keep_rows(k * CHUNK_SLOTS + s, a.g3[rows_of(k * CHUNK_SLOTS + s, seq)].astype(wide))
                for s in range(CHUNK_SLOTS)
            ],
            axis=0,
        ).astype(low)
        a.g3[rows] = grad
        a.pre[...] = dot(a.n3[rows], a.w_hidden_in[...])

        def gelu_rows(i, carry):
            part = rows_of(i, GELU_ROWS)
            pre = a.pre[part]
            square = pre * pre
            bend = jnp.tanh(scale * pre * (1.0 + 0.044715 * square))
            half = 0.5 * (1.0 + bend)
            curve = scale * (1.0 + 3 * 0.044715 * square)
            a.pre[part] = half + 0.5 * pre * (1.0 - bend * bend) * curve
            target = pl.ds(pl.multiple_of(k * chunk_rows + i * GELU_ROWS, GELU_ROWS), GELU_ROWS)
            a.act[target] = (pre * half).astype(low)
            return carry

        lax.fori_loop(0, chunk_rows // GELU_ROWS, gelu_rows, 0)
        out = dot_t(a.act[rows], a.w_hidden_out[...]).astype(low)
        a.out_part[k % 2, 0] = out[:half_rows]
        a.out_part[k % 2, 1] = out[half_rows:]
        out_near_copy(k).start()
        grad_pre = (a.pre[...] * dot(grad, a.w_hidden_out[...])).astype(low)
        a.d_pre[rows] = grad_pre
        a.part[rows] = dot_t(grad_pre, a.w_hidden_in[...]).astype(low)

    phase(2, finish_two, a.n3, feed_forward, out_gather)

    def column_copy(which, k):
        return remote(
            a.col_send.at[which, k],
            a.columns.at[which, :, own_rows(k)],
            a.col_sem,
            (which, k),
            c_peer,
        )

    def emit_columns(which, k, value):
        value = value.T
        left, right = value[:quarter_width], value[quarter_width:]
        first = core == 0
        a.columns[which, :, own_rows(k)] = jnp.where(first, left, right).astype(low)
        a.col_send[which, k] = jnp.where(first, right, left).astype(low)
        column_copy(which, k).start()

    def finish_out(k):
        out_far_copy(k).wait()
        value = a.out_keep[k] + a.out_far[k].astype(wide)
        emit_columns(0, k, keep_rows(k * CHUNK_SLOTS + core, value))

    orders = (tuple(range(levels)), (1, 0) + tuple(range(2, levels)))

    def dp_rank(half, level):
        return (dp_me >> orders[half][level]) & 1

    def dp_copy(block, half, level):
        buffer = block % 2
        count = 1 << (levels - 1 - level)
        source = a.term if level == 0 else a.holds[level - 1]
        part = pl.ds((1 - dp_rank(half, level)) * count, count)
        return remote(
            source.at[buffer, half, part],
            a.lands[level].at[buffer, half],
            a.dp_sem,
            (block, half, level),
            dp_peer(1 << orders[half][level]),
        )

    def raw_copy(block):
        return pltpu.make_async_copy(
            a.term.at[block % 2], a.raw_grads.at[block], a.dp_sem.at[0, block, 0, 0]
        )

    def credit_wait(block, half, level):
        pl.semaphore_wait(a.credit_sem.at[block % 2, half, level], 1)

    def dp_begin(block):
        if in_kernel:
            for half in range(2):
                if block >= 2:
                    credit_wait(block, half, 0)
                dp_copy(block, half, 0).start()
        else:
            raw_copy(block).start()

    def dp_advance(block, level):
        if not in_kernel:
            return
        buffer = block % 2
        count = 1 << (levels - 1 - level)
        for half in range(2):
            dp_copy(block, half, level).wait()
            source = a.term if level == 0 else a.holds[level - 1]
            part = pl.ds(dp_rank(half, level) * count, count)
            value = source[buffer, half, part].astype(wide)
            value += a.lands[level][buffer, half].astype(wide)
            if level == levels - 1:
                emit_grads(block, half, value[0])
            else:
                a.holds[level][buffer, half] = value.astype(low)
            if block < 2:
                pl.semaphore_signal(
                    a.credit_sem.at[buffer, half, level],
                    inc=1,
                    device_id=dp_peer(1 << orders[half][level]),
                    device_id_type=MESH,
                )
            if level + 1 < levels:
                if block >= 2:
                    credit_wait(block, half, level + 1)
                dp_copy(block, half, level + 1).start()

    def dp_finish_raw(block):
        if not in_kernel:
            raw_copy(block).wait()

    def emit_grads(block, half, value):
        columns = slice(half * half_width, (half + 1) * half_width)
        if block == 0:
            a.grad_hidden_out[:, columns] = value
        elif block == 1:
            a.grad_hidden_in[:, columns] = value
        else:
            start = (4 if block == 2 else 0) + 2 * half
            for i, name in enumerate(Weights._fields[start : start + 2]):
                getattr(a, "grad_" + name)[...] = value[:, i * inner : (i + 1) * inner]

    piece = cfg.piece
    groups = 2
    group_rows = width // groups
    pieces_each = max(group_rows // piece, 1) if in_kernel else 1

    def store_pieces(block, g, rows):
        if in_kernel:
            for i in range(pieces_each):
                for gg in range(groups):
                    if gg != g:
                        continue
                    for half in range(2):
                        index = piece_index(gg * pieces_each + i, orders[half])
                        a.term[block % 2, half, index] = rows[
                            i * piece : (i + 1) * piece,
                            half * half_width : (half + 1) * half_width,
                        ]
        else:
            a.term[block % 2, g * group_rows : (g + 1) * group_rows] = rows

    def plain_grads(block, left, right):
        for g in range(groups):
            columns = slice(g * group_rows, (g + 1) * group_rows)
            store_pieces(block, g, t_dot(left[:, columns], right[...]).astype(low))

    def turned_grads(block):
        for g in range(groups):
            columns = slice(g * group_rows, (g + 1) * group_rows)
            store_pieces(block, g, a.enc[all_turned, columns].T)

    def turned_rows(i):
        return slice(i * inner, (i + 1) * inner)

    all_turned = slice(0, 4 * inner)

    plain_grads(0, a.g3, a.act)
    dp_begin(0)
    plain_grads(1, a.n3, a.d_pre)
    dp_begin(1)

    def finish_three(k, term):
        grad_rows, grad_gain = norm_back(a.h2[k], gain_ffn, term)
        add_gain(2, grad_gain)
        grad = a.g3[own_rows(k)].astype(wide) + grad_rows
        a.dh[k] = grad
        a.dh2[own_rows(k)] = grad.astype(low)

    def score_back(soft, grad_soft):
        weights = soft.astype(wide)
        row_inner = jnp.sum(weights * grad_soft, axis=-1, keepdims=True)
        return (weights * (grad_soft - row_inner)).astype(low)

    def cross_backward(k):
        rows = rows_of(k, chunk_rows)
        grad_mixed = dot_t(a.dh2[rows], a.w_output_cross[...]).astype(low)
        a.do2[rows] = grad_mixed
        query = a.q2[rows]
        grads = []
        for s in range(CHUNK_SLOTS):
            slot = k * CHUNK_SLOTS + s
            part = slice(s * seq, (s + 1) * seq)
            enc_rows = rows_of(slot, enc_len)
            tall_grad, tall_query = stack(grad_mixed[part]), stack(query[part])
            soft = a.soft2[slot]
            grad_scores = score_back(soft, dot_t(tall_grad, a.v2[enc_rows]))
            a.dkv[slot, :inner] = t_dot(tall_query, grad_scores).astype(low)
            a.dkv[slot, inner:] = t_dot(tall_grad, soft).astype(low)
            grads.append(unstack(dot(grad_scores, a.k2[enc_rows])).astype(low))
        grads = jnp.concatenate(grads, axis=0)
        a.d_pre[rows, :inner] = grads
        a.part[rows] = dot(grads, a.w_query_cross[...]).astype(low)

        @pl.when(k == 2)
        def _():
            dp_advance(0, 0)

        @pl.when(k == 3)
        def _():
            dp_advance(0, 1)

    phase(3, finish_three, a.dh2, cross_backward)

    def peer_rows(index, source, target):
        rows = rows_of(1 - y, chip_slots * seq)
        return remote(source.at[rows], target, a.peer_sem, (index,), y_peer)

    peer_copies = peer_rows(0, a.q2, a.q2_peer), peer_rows(1, a.do2, a.do2_peer)
    for copy in peer_copies:
        copy.start()
    enc_copy(0, 0).start()
    dp_advance(1, 0)
    dp_advance(0, 2)

    kv_blocks = 2 * inner // half_rows
    for i in range(kv_blocks):
        a.h2[i] = jnp.zeros_like(a.h2[i])

    def add_kv(slot, buffer):
        value = dot(a.dkv[slot], a.enc[rows_of(buffer, enc_len)])
        for i in range(kv_blocks):
            a.h2[i] += value[i * half_rows : (i + 1) * half_rows]

    def kv_pair(j, carry):
        enc_copy(2 * j, 0).wait()
        enc_copy(2 * j + 1, 1).start()
        add_kv(2 * j, 0)
        enc_copy(2 * j + 1, 1).wait()

        @pl.when(2 * j + 2 < slots)
        def _():
            enc_copy(2 * j + 2, 0).start()

        add_kv(2 * j + 1, 1)
        return carry

    lax.fori_loop(0, slots // 2, kv_pair, 0)
    a.enc[turned_rows(0)] = t_dot(a.d_pre[:, :inner], a.n2[...]).astype(low)
    for i in range(kv_blocks):
        a.enc[inner + i * half_rows : inner + (i + 1) * half_rows] = a.h2[i].astype(low)
    a.enc[turned_rows(3)] = t_dot(a.o2[...], a.dh2[...]).astype(low)
    dp_advance(1, 1)
    dp_finish_raw(0)
    turned_grads(2)
    dp_begin(2)

    def finish_four(k, term):
        grad_rows, grad_gain = norm_back(a.h1[k], gain_cross, term)
        add_gain(1, grad_gain)
        grad = a.dh[k] + grad_rows
        a.dh[k] = grad
        a.dh1[own_rows(k)] = grad.astype(low)

    def self_backward(k):
        rows = rows_of(k, chunk_rows)
        grad_mixed = dot_t(a.dh1[rows], a.w_output_self[...]).astype(low)
        query, keys, values = a.q1[rows], a.k1[rows], a.v1[rows]
        grads = [[], [], []]
        for s in range(CHUNK_SLOTS):
            part = slice(s * seq, (s + 1) * seq)
            tall_grad, tall_query = stack(grad_mixed[part]), stack(query[part])
            soft = a.soft1[k * CHUNK_SLOTS + s]
            grad_scores = score_back(soft, dot_t(tall_grad, values[part]))
            a.table[...] += grad_scores.astype(wide)
            grads[0].append(unstack(dot(grad_scores, keys[part])).astype(low))
            grads[1].append(t_dot(grad_scores, tall_query).astype(low))
            grads[2].append(t_dot(soft, tall_grad).astype(low))
        grads = [jnp.concatenate(g, axis=0) for g in grads]
        a.q1[rows], a.k1[rows], a.v1[rows] = grads
        a.part[rows] = (
            dot(grads[0], a.w_query_self[...])
            + dot(grads[1], a.w_key_self[...])
            + dot(grads[2], a.w_value_self[...])
        ).astype(low)

        @pl.when(k == 1)
        def _():
            dp_advance(1, 2)

        @pl.when(k == 3)
        def _():
            dp_advance(2, 0)

    phase(4, finish_four, a.dh1, self_backward, send=y_send_last)
    for k in range(chunks):
        out_far_copy(k).start()
    a.enc[turned_rows(0)] = t_dot(a.q1[...], a.n1[...]).astype(low)
    a.enc[turned_rows(1)] = t_dot(a.k1[...], a.n1[...]).astype(low)
    a.enc[turned_rows(2)] = t_dot(a.v1[...], a.n1[...]).astype(low)
    a.enc[turned_rows(3)] = t_dot(a.o1[...], a.dh1[...]).astype(low)
    dp_finish_raw(1)
    turned_grads(3)
    dp_begin(3)
    dp_advance(2, 1)

    mirror = jnp.where(row_i + col_i == seq - 1, 1.0, 0.0).astype(wide)
    for h in range(heads):
        flipped = exact_dot(a.table[h * seq : (h + 1) * seq, :], mirror)
        turned = pltpu.roll(flipped, 0, 1, stride=1, stride_axis=0)
        a.small[3:4, h * seq : (h + 1) * seq] = jnp.sum(turned, axis=0, keepdims=True)

    def small_copy(i):
        peer = (c_peer, y_peer)[i] if i < 2 else dp_peer(1 << (i - 2))
        return remote(a.small, a.small_land.at[i], a.small_sem, (i,), peer)

    row = lax.broadcasted_iota(jnp.int32, a.small.shape, 0)

    def small_step(i):
        small_copy(i).wait()
        summed = (row < 3, row < 1)[i] if i < 2 else row < 8
        a.small[...] += jnp.where(summed, a.small_land[i], 0.0)
        if i < levels + 1:
            small_copy(i + 1).start()

    small_copy(0).start()
    for copy in peer_copies:
        copy.wait()

    def enc_partial(k):
        rows = rows_of(k, seq)
        enc_rows = rows_of(k, enc_len)
        tall_query, tall_grad = stack(a.q2_peer[rows]), stack(a.do2_peer[rows])
        soft = softmax(dot_t(tall_query, a.k2_peer[enc_rows]))
        grad_scores = score_back(soft, dot_t(tall_grad, a.v2_peer[enc_rows]))
        peer_grads = jnp.concatenate(
            [t_dot(tall_query, grad_scores).astype(low), t_dot(tall_grad, soft).astype(low)], axis=0
        )
        own = t_dot(a.dkv[chip_slot(k)], a.w_kv[: 2 * inner])
        return own + t_dot(peer_grads, a.w_kv[2 * inner :])

    enc_each = chip_slots // 2

    def enc_near_copy(j):
        rows = rows_of(j, enc_len)
        return remote(a.n3.at[rows], a.act.at[rows], a.enc_near_sem, (j,), c_peer)

    def enc_give(j, carry):
        a.n3[rows_of(j, enc_len)] = enc_partial((1 - core) * enc_each + j).astype(low)
        enc_near_copy(j).start()
        return carry

    def enc_keep(j, carry):
        partial = enc_partial(core * enc_each + j)
        enc_near_copy(j).wait()
        rows = rows_of(j, enc_len)
        a.enc_out[rows] = (partial + a.act[rows].astype(wide)).astype(low)
        return carry

    small_step(0)
    lax.fori_loop(0, enc_each, enc_give, 0)
    small_step(1)
    dp_advance(2, 2)
    dp_advance(3, 0)
    lax.fori_loop(0, enc_each, enc_keep, 0)
    store_enc = load(2, a.enc_out, a.encoded_grad)
    store_enc.start()
    small_step(2)
    dp_advance(3, 1)

    def phase_five(k):
        for copy in last_copies(k):
            copy.wait()
        rows = my_half(a.x[own_rows(k)]).astype(wide)
        inverse = inverse_rms(a.x[own_rows(k)].astype(wide))
        sums = (a.inner_send[k] + a.inner_far[k])[:1]
        row_inner = jnp.broadcast_to(sums, (half_rows, half_rows)).T[:, :1] * (1.0 / width)
        term = my_half(a.h1[k]) + a.far[0, k, :, :half_width].astype(wide)
        grad_rows = inverse * my_half(gain_self) * term
        grad_rows -= rows * (inverse * inverse * inverse) * row_inner
        emit_columns(1, k, my_half(a.dh[k]) + grad_rows)

    each_chunk(phase_five)
    each_chunk(finish_out)
    for i in range(3, levels + 2):
        small_step(i)
    dp_advance(3, 2)
    dp_finish_raw(2)
    dp_finish_raw(3)
    for k in range(chunks):
        column_copy(0, k).wait()
        column_copy(1, k).wait()
    stores = [
        load(0, a.columns.at[0], a.layer_out),
        load(1, a.columns.at[1], a.input_grad),
    ]
    for store in stores:
        store.start()
    a.small_out[...] = a.small[...]
    for store in (*stores, store_enc):
        store.wait()


def finish_kernel(count, heads, seq, *refs):
    small, buckets = refs[count], refs[count + 1]
    targets, held, sems = refs[count + 2 : 2 * count + 6], refs[2 * count + 6 : -1], refs[-1]
    copies = [pltpu.make_async_copy(refs[i], held[i], sems.at[i]) for i in range(count)]
    for copy in copies:
        copy.start()
    for i in range(count):
        copies[i].wait()
        copies[i] = pltpu.make_async_copy(held[i], targets[i], sems.at[i])
        copies[i].start()
    for i in range(3):
        targets[count + i][...] = small[i, :]
    sums = jnp.concatenate([small[3:4, h * seq : (h + 1) * seq] for h in range(heads)], axis=0)
    by_lane = pltpu.roll(jnp.broadcast_to(buckets[...], (8, seq)), seq - 1, 1)[:1]
    kinds = targets[count + 3].shape[1]
    bucket = lax.broadcasted_iota(jnp.int32, (kinds, seq), 0)
    chosen = jnp.where(by_lane == bucket, 1.0, 0.0).astype(wide)
    targets[count + 3][...] = lax.dot_general(
        sums,
        chosen,
        (((1,), (1,)), ((), ())),
        precision=highest,
        preferred_element_type=wide,
    )
    for copy in copies:
        copy.wait()


def per_device(*args):
    (
        inputs,
        encoded,
        example_counts,
        lengths,
        buckets,
        gain_self,
        gain_cross,
        gain_ffn,
        bias_table,
    ) = args[:9]
    weights = args[9:19]
    out_grad = args[19]
    rows, width = inputs.shape
    seq = buckets.shape[0]
    slots = lengths.shape[0]
    enc_rows = encoded.shape[0]
    enc_len = enc_rows // slots
    inner = weights[0].shape[1]
    hidden = weights[8].shape[1]
    heads = inner // HD
    dp_count = lax.axis_size("dp")
    levels = dp_count.bit_length() - 1
    piece = width // dp_count
    in_kernel = piece % 16 == 0
    chunks = slots // CHUNK_SLOTS
    half = CHUNK_SLOTS * seq // 2

    ins = dict(
        lengths=(lengths, SM),
        counts=(example_counts, SM),
        gain_self=(gain_self, VM),
        gain_cross=(gain_cross, VM),
        gain_ffn=(gain_ffn, VM),
        table_in=(bias_table.T, VM),
        buckets=(buckets[None], VM),
        inputs=(inputs, HBM),
        encoded=(encoded, HBM),
        out_grad=(out_grad, HBM),
    )
    for name, weight in zip(Weights._fields, weights, strict=True):
        ins[name] = (weight, HBM)
    for name in Weights._fields[:8]:
        ins[name] = (ins[name][0].T, HBM)
    shape = jax.ShapeDtypeStruct
    outs = dict(
        layer_out=(shape((width // 4, rows), low), HBM),
        input_grad=(shape((width // 4, rows), low), HBM),
        encoded_grad=(shape((enc_rows // 4, width), low), HBM),
        small_out=(shape((8, width), wide), VM),
    )
    if in_kernel:
        for name, weight in zip(Weights._fields, weights, strict=True):
            outs["grad_" + name] = (shape((piece, weight.shape[1]), wide), VM)
    else:
        outs.update(raw_grads=(shape((4, width, width), low), HBM))
    vmem, dma = pltpu.VMEM, pltpu.SemaphoreType.DMA
    quarter = width // 4
    whole_rows = vmem((rows, width), low)
    hidden_rows = vmem((rows, hidden), low)
    inner_rows = vmem((rows, inner), low)
    own_wide = vmem((chunks, half, width), wide)
    own_low = vmem((chunks, half, width), low)
    scratch = {
        "w_" + name: vmem(ins[name][0].shape, low)
        for name in Weights._fields
        if name not in Weights._fields[5:7]
    }
    scratch.update(
        x=whole_rows,
        g3=whole_rows,
        enc=vmem((2 * enc_len, width), low),
        n1=whole_rows,
        n2=whole_rows,
        n3=whole_rows,
        dh1=whole_rows,
        dh2=whole_rows,
        part=whole_rows,
        act=hidden_rows,
        d_pre=hidden_rows,
        q1=inner_rows,
        k1=inner_rows,
        v1=inner_rows,
        o1=inner_rows,
        q2=inner_rows,
        o2=inner_rows,
        k2=vmem((enc_rows, inner), low),
        v2=vmem((enc_rows, inner), low),
        h1=own_wide,
        h2=own_wide,
        dh=own_wide,
        soft1=vmem((slots, heads * seq, seq), low),
        soft2=vmem((slots, heads * seq, enc_len), low),
        dkv=vmem((slots, 2 * inner, enc_len), low),
        near=own_low,
        mine=own_low,
        far=vmem((2, chunks, half, width), low),
        out_part=vmem((2, 2, half, width), low),
        out_near=own_low,
        out_mine=vmem((chunks, half, width // 2), low),
        out_keep=vmem((chunks, half, width // 2), wide),
        out_far=vmem((chunks, half, width // 2), low),
        columns=vmem((2, quarter, rows), low),
        col_send=vmem((2, chunks, quarter, half), low),
        w_kv=vmem((4 * inner, width), low),
        k2_peer=vmem((enc_rows // 2, inner), low),
        v2_peer=vmem((enc_rows // 2, inner), low),
        q2_peer=vmem((rows // 2, inner), low),
        do2_peer=vmem((rows // 2, inner), low),
        do2=inner_rows,
        inner_send=vmem((chunks, 8, half), wide),
        inner_far=vmem((chunks, 8, half), wide),
        enc_out=vmem((enc_rows // 4, width), low),
        pre=vmem((CHUNK_SLOTS * seq, hidden), wide),
        bias=vmem((heads * seq, seq), wide),
        table=vmem((heads * seq, seq), wide),
        small=vmem((8, width), wide),
        small_land=vmem((levels + 2, 8, width), wide),
        load_sem=dma((3 + len(weights),)),
        enc_sem=dma((2,)),
        near_sem=dma((2, 5, chunks)),
        far_sem=dma((2, 5, chunks)),
        share_sem=dma((2, 5, chunks)),
        out_near_sem=dma((2, chunks)),
        out_far_sem=dma((2, chunks)),
        col_sem=dma((2, 2, chunks)),
        enc_near_sem=dma((2, 2)),
        peer_sem=dma((2, 2)),
        kv_sem=dma((2, 1)),
        inner_sem=dma((2, chunks)),
        dp_sem=dma((2, 4, 2, levels)),
        small_sem=dma((2, levels + 2)),
        credit_sem=pltpu.SemaphoreType.REGULAR((2, 2, levels)),
    )
    if in_kernel:
        scratch.update(term=vmem((2, 2, dp_count, piece, width // 2), low))
        for level in range(levels):
            count = 1 << (levels - 1 - level)
            scratch["land%d" % level] = vmem((2, 2, count, piece, width // 2), low)
            if level + 1 < levels:
                scratch["hold%d" % level] = vmem((2, 2, count, piece, width // 2), low)
    else:
        scratch.update(term=vmem((2, width, width), low))
    cfg = SimpleNamespace(
        seq=seq,
        enc_len=enc_len,
        slots=slots,
        width=width,
        heads=heads,
        levels=levels,
        in_kernel=in_kernel,
        piece=piece,
    )
    results = pl.pallas_call(
        functools.partial(layer_kernel, cfg, tuple(ins) + tuple(outs) + tuple(scratch)),
        out_shape=tuple(o[0] for o in outs.values()),
        in_specs=[i[1] for i in ins.values()],
        out_specs=tuple(o[1] for o in outs.values()),
        scratch_shapes=list(scratch.values()),
        compiler_params=pltpu.CompilerParams(
            collective_id=1, has_side_effects=True, vmem_limit_bytes=65000 * 2**10
        ),
    )(*[i[0] for i in ins.values()])
    moved = [i for i, name in enumerate(outs) if name not in ("small_out", "raw_grads")]
    buckets_row = buckets[None]
    kinds = bias_table.shape[0]
    finals = pl.pallas_call(
        functools.partial(finish_kernel, len(moved), heads, seq),
        out_shape=(
            *(shape(results[i].shape, results[i].dtype) for i in moved),
            *(shape((width,), wide) for _ in range(3)),
            shape((heads, kinds), wide),
        ),
        in_specs=[HBM] * len(moved) + [VM, VM],
        out_specs=(HBM,) * len(moved) + (VM,) * 4,
        scratch_shapes=[
            *(vmem(results[i].shape, results[i].dtype) for i in moved),
            dma((len(moved),)),
        ],
    )(*[results[i] for i in moved], results[3], buckets_row)
    if in_kernel:
        grads = finals[3 : len(moved)]
    else:
        raw = results[4]
        parts = [raw[3][:, i * inner : (i + 1) * inner] for i in range(4)]
        parts += [raw[2][:, i * inner : (i + 1) * inner] for i in range(4)]
        grads = [
            lax.psum_scatter(part.astype(wide), "dp", scatter_dimension=0, tiled=True)
            for part in (*parts, raw[1], raw[0])
        ]
    gains = finals[len(moved) : len(moved) + 3]
    return (finals[0].T, finals[1].T, finals[2], *gains, finals[-1].T, *grads)


def solution(mesh):
    columns = P(None, "tensor")
    both = P("dp", "tensor")
    placed = (
        (P("dp", None), P("dp", None), P("dp"), P("dp"), P(), P(), P(), P())
        + (columns,) * 11
        + (P("dp", None),)
    )
    return jax.shard_map(
        per_device,
        mesh=mesh,
        in_specs=placed,
        out_specs=(both, both, P(("dp", "tensor"), None), P(), P(), P(), columns) + (both,) * 10,
        check_vma=False,
    )
```

```python
import functools
from types import SimpleNamespace
from typing import NamedTuple

import jax
import jax.numpy as jnp
from jax import lax
from jax.experimental import pallas as pl
from jax.experimental.pallas import tpu as pltpu
from jax.sharding import PartitionSpec as P

HD = 64
CHUNK_SLOTS = 2
GELU_ROWS = 32

norm_epsilon = 1e-06
masked_score = -1e30
highest = lax.Precision.HIGHEST
MESH = pl.DeviceIdType.MESH
VM = pl.BlockSpec(memory_space=pltpu.VMEM)
SM = pl.BlockSpec(memory_space=pltpu.SMEM)
HBM = pl.BlockSpec(memory_space=pl.ANY)
low = jnp.bfloat16
wide = jnp.float32


def dot(left, right):
    return lax.dot_general(left, right, (((1,), (0,)), ((), ())), preferred_element_type=wide)


def dot_t(left, right):
    return lax.dot_general(left, right, (((1,), (1,)), ((), ())), preferred_element_type=wide)


def t_dot(left, right):
    return lax.dot_general(left, right, (((0,), (0,)), ((), ())), preferred_element_type=wide)


def exact_dot(left, right):
    return jnp.dot(left, right, precision=highest, preferred_element_type=wide)


def inverse_rms(rows):
    return lax.rsqrt(jnp.mean(rows * rows, axis=-1, keepdims=True) + norm_epsilon)


def norm_back(rows, gain, grad):
    inverse = inverse_rms(rows)
    scaled = gain * grad
    inner = jnp.mean(scaled * rows, axis=-1, keepdims=True)
    grad_rows = inverse * scaled - rows * (inverse * inverse * inverse) * inner
    return grad_rows, jnp.sum(grad * rows * inverse, axis=0, keepdims=True)


def tensor_peer(bit):
    return (lax.axis_index("dp"), lax.axis_index("tensor") ^ bit)


def dp_peer(bit):
    return (lax.axis_index("dp") ^ bit, lax.axis_index("tensor"))


def piece_index(rank, order):
    return sum(((rank >> bit) & 1) << (len(order) - 1 - k) for k, bit in enumerate(order))


class Weights(NamedTuple):
    query_self: object
    key_self: object
    value_self: object
    output_self: object
    query_cross: object
    key_cross: object
    value_cross: object
    output_cross: object
    hidden_in: object
    hidden_out: object


def layer_kernel(cfg, names, *refs):
    a = SimpleNamespace(**dict(zip(names, refs, strict=True)))
    seq, enc_len, slots, width = cfg.seq, cfg.enc_len, cfg.slots, cfg.width
    heads, levels, in_kernel = cfg.heads, cfg.levels, cfg.in_kernel
    inner = heads * HD
    if in_kernel:
        a.lands = [getattr(a, "land%d" % i) for i in range(levels)]
        a.holds = [getattr(a, "hold%d" % i) for i in range(levels - 1)]
    chunks = slots // CHUNK_SLOTS
    chunk_rows = CHUNK_SLOTS * seq
    half_rows = chunk_rows // 2
    half_width = width // 2
    quarter_width = width // 4
    me = lax.axis_index("tensor")
    core = lax.rem(me, 2)
    y = me // 2
    dp_me = lax.axis_index("dp")
    c_peer, y_peer = tensor_peer(1), tensor_peer(2)

    def rows_of(k, count):
        return pl.ds(pl.multiple_of(k * count, count), count)

    def load(index, src, dst):
        return pltpu.make_async_copy(src, dst, a.load_sem.at[index])

    inner_rows = slice(0, inner), slice(inner, 2 * inner)
    first_rows, later_rows = pl.ds(0, chunk_rows), pl.ds(chunk_rows, slots * seq - chunk_rows)
    load_x = load(0, a.inputs.at[first_rows], a.x.at[first_rows])
    load_more = load(2 + len(Weights._fields), a.inputs.at[later_rows], a.x.at[later_rows])
    load_g = load(1, a.out_grad, a.g3)
    spots = {name: getattr(a, "w_" + name) for name in Weights._fields if hasattr(a, "w_" + name)}
    spots.update(key_cross=a.w_kv.at[inner_rows[0]], value_cross=a.w_kv.at[inner_rows[1]])
    loads = Weights(
        *(load(2 + i, getattr(a, name), spots[name]) for i, name in enumerate(Weights._fields))
    )
    loads.key_cross.start()
    loads.value_cross.start()
    load_x.start()
    for copy in loads[:4]:
        copy.start()
    load_more.start()

    barrier = pltpu.get_barrier_semaphore()
    peers = [c_peer, y_peer] + [dp_peer(1 << k) for k in range(levels)]
    for peer in peers:
        pl.semaphore_signal(barrier, inc=1, device_id=peer, device_id_type=MESH)

    def remote(src, dst, sems, index, peer):
        return pltpu.make_async_remote_copy(
            src_ref=src,
            dst_ref=dst,
            send_sem=sems.at[(0,) + index],
            recv_sem=sems.at[(1,) + index],
            device_id=peer,
            device_id_type=MESH,
        )

    def peer_weights():
        own, theirs = pl.ds(0, 2 * inner), pl.ds(2 * inner, 2 * inner)
        return remote(a.w_kv.at[own], a.w_kv.at[theirs], a.kv_sem, (0,), y_peer)

    def enc_copy(slot, buffer):
        rows = pl.ds(pl.multiple_of(slot * enc_len, enc_len), enc_len)
        target = a.enc.at[rows_of(buffer, enc_len)]
        return pltpu.make_async_copy(a.encoded.at[rows], target, a.enc_sem.at[buffer])

    enc_copy(0, 0).start()
    for copy in (loads.query_cross, loads.output_cross, loads.hidden_in, loads.hidden_out, load_g):
        copy.start()

    loads.key_cross.wait()
    loads.value_cross.wait()
    pl.semaphore_wait(barrier, len(peers))
    peer_weights().start()

    gain_self, gain_cross, gain_ffn = (
        ref[...].reshape(1, width) for ref in (a.gain_self, a.gain_cross, a.gain_ffn)
    )

    lane = lax.broadcasted_iota(jnp.int32, (1, inner), 1)
    masks = [jnp.where(lane // HD == h, 1.0, 0.0).astype(wide) for h in range(heads)]
    masks_low = [m.astype(low) for m in masks]
    row_i = lax.broadcasted_iota(jnp.int32, (seq, seq), 0)
    col_i = lax.broadcasted_iota(jnp.int32, (seq, seq), 1)
    bucket = lax.broadcasted_iota(jnp.int32, (a.table_in.shape[1], seq), 0)
    chosen = jnp.where(a.buckets[...] == bucket, 1.0, 0.0).astype(wide)
    per_dist = exact_dot(a.table_in[...], chosen)
    backward = jnp.where((row_i + col_i) % seq == 0, 1.0, 0.0).astype(wide)
    lines = exact_dot(per_dist, backward)
    for h in range(heads):
        line = jnp.broadcast_to(lines[h : h + 1, :], (seq, seq))
        turned = pltpu.roll(line, 0, 1, stride=1, stride_axis=0)
        a.bias[h * seq : (h + 1) * seq, :] = jnp.where(row_i >= col_i, turned, masked_score)
    a.table[...] = jnp.zeros_like(a.table)
    a.small[...] = jnp.zeros_like(a.small)

    def stack(rows):
        return jnp.concatenate([rows * m for m in masks_low], axis=0)

    def unstack(rows):
        return sum(rows[h * seq : (h + 1) * seq] * masks[h] for h in range(heads))

    def softmax(scores):
        peak = jnp.max(scores, axis=-1, keepdims=True)
        terms = jnp.exp(scores - peak)
        return (terms / jnp.sum(terms, axis=-1, keepdims=True)).astype(low)

    def own_rows(k):
        return pl.ds(pl.multiple_of(k * chunk_rows + core * half_rows, half_rows), half_rows)

    def other_rows(k):
        return pl.ds(pl.multiple_of(k * chunk_rows + (1 - core) * half_rows, half_rows), half_rows)

    def add_gain(index, value):
        a.small[index : index + 1, :] += value

    def near_copy(p, k):
        return remote(a.part.at[other_rows(k)], a.near.at[k], a.near_sem, (p, k), c_peer)

    def far_copy(p, k):
        return remote(a.mine.at[k], a.far.at[p % 2, k], a.far_sem, (p, k), y_peer)

    def y_send(p, k):
        near_copy(p, k).wait()
        a.mine[k] = (a.part[own_rows(k)].astype(wide) + a.near[k].astype(wide)).astype(low)
        far_copy(p, k).start()

    def last_copies(k):
        return (
            remote(
                a.mine.at[k, :, pl.ds(0, half_width)],
                a.far.at[0, k, :, pl.ds(0, half_width)],
                a.far_sem,
                (4, k),
                y_peer,
            ),
            remote(a.inner_send.at[k], a.inner_far.at[k], a.inner_sem, (k,), y_peer),
        )

    def y_send_last(k):
        near_copy(4, k).wait()
        term = a.part[own_rows(k)].astype(wide) + a.near[k].astype(wide)
        a.h1[k] = term
        rows = a.x[own_rows(k)].astype(wide)
        product = term * rows
        row_inner = jnp.sum(product * gain_self, axis=-1, keepdims=True)
        add_gain(0, jnp.sum(product * inverse_rms(rows), axis=0, keepdims=True))
        a.inner_send[k] = jnp.broadcast_to(row_inner, (half_rows, half_rows)).T[:8]
        a.mine[k, :, :half_width] = jnp.where(
            y == 0, term[:, half_width:], term[:, :half_width]
        ).astype(low)
        for copy in last_copies(k):
            copy.start()

    def total(p, k):
        far_copy(p, k).wait()
        return a.mine[k].astype(wide) + a.far[p % 2, k].astype(wide)

    def share_copy(p, k, buffer):
        return remote(buffer.at[own_rows(k)], buffer.at[own_rows(k)], a.share_sem, (p, k), c_peer)

    def each_chunk(body):
        def step(k, carry):
            body(k)
            return carry

        lax.fori_loop(0, chunks, step, 0)

    def phase(p, finish, buffer, compute, extra=None, send=None):
        send = send or functools.partial(y_send, p)

        def body(k):
            finish(k, total(p - 1, k))
            share_copy(p, k, buffer).start()

            @pl.when(k > 0)
            def _():
                send(k - 1)

            share_copy(p, k, buffer).wait()
            compute(k)
            near_copy(p, k).start()
            if extra is not None:
                extra(k)

        each_chunk(body)
        send(chunks - 1)

    def project(slot, buffer):
        enc_copy(slot, buffer).wait()

        @pl.when(slot + 1 < slots)
        def _():
            enc_copy(slot + 1, 1 - buffer).start()

        rows = rows_of(slot, enc_len)
        a.k2[rows] = dot_t(a.enc[rows_of(buffer, enc_len)], a.w_kv[:inner]).astype(low)
        a.v2[rows] = dot_t(a.enc[rows_of(buffer, enc_len)], a.w_kv[inner : 2 * inner]).astype(low)

    def self_forward(k):
        rows = rows_of(k, chunk_rows)
        x = a.x[rows].astype(wide)
        normed = (x * inverse_rms(x) * gain_self).astype(low)
        a.n1[rows] = normed
        query = dot_t(normed, a.w_query_self[...]).astype(low)
        keys = dot_t(normed, a.w_key_self[...]).astype(low)
        values = dot_t(normed, a.w_value_self[...]).astype(low)
        a.q1[rows], a.k1[rows], a.v1[rows] = query, keys, values
        mixed = []
        for s in range(CHUNK_SLOTS):
            part = slice(s * seq, (s + 1) * seq)
            weights = softmax(dot_t(stack(query[part]), keys[part]) + a.bias[...])
            a.soft1[k * CHUNK_SLOTS + s] = weights
            mixed.append(unstack(dot(weights, values[part])).astype(low))
        mixed = jnp.concatenate(mixed, axis=0)
        a.o1[rows] = mixed
        a.part[rows] = dot(mixed, a.w_output_self[...]).astype(low)

    load_x.wait()
    for copy in loads[:4]:
        copy.wait()

    def phase_zero(k):
        @pl.when(k == 1)
        def _():
            load_more.wait()

        self_forward(k)
        near_copy(0, k).start()
        y_send(0, k)
        project(CHUNK_SLOTS * k, 0)
        project(CHUNK_SLOTS * k + 1, 1)

    each_chunk(phase_zero)
    loads.query_cross.wait()
    loads.output_cross.wait()
    peer_weights().wait()

    chip_slots = slots // 2

    def chip_slot(k):
        return chip_slots * y + k

    enc_copy(chip_slot(0), 0).start()

    def project_peer(k):
        buffer = lax.rem(k, 2)
        enc_copy(chip_slot(k), buffer).wait()

        @pl.when(k + 1 < chip_slots)
        def _():
            enc_copy(chip_slot(k + 1), 1 - buffer).start()

        rows = rows_of(k, enc_len)
        encoded = a.enc[rows_of(buffer, enc_len)]
        a.k2_peer[rows] = dot_t(encoded, a.w_kv[2 * inner : 3 * inner]).astype(low)
        a.v2_peer[rows] = dot_t(encoded, a.w_kv[3 * inner :]).astype(low)

    def finish_one(k, term):
        hidden = a.x[own_rows(k)].astype(wide) + term
        a.h1[k] = hidden
        a.n2[own_rows(k)] = (hidden * inverse_rms(hidden) * gain_cross).astype(low)

    def cross_forward(k):
        rows = rows_of(k, chunk_rows)
        query = dot_t(a.n2[rows], a.w_query_cross[...]).astype(low)
        a.q2[rows] = query
        mixed = []
        for s in range(CHUNK_SLOTS):
            slot = k * CHUNK_SLOTS + s
            enc_rows = rows_of(slot, enc_len)
            weights = softmax(dot_t(stack(query[s * seq : (s + 1) * seq]), a.k2[enc_rows]))
            a.soft2[slot] = weights
            mixed.append(unstack(dot(weights, a.v2[enc_rows])).astype(low))
        mixed = jnp.concatenate(mixed, axis=0)
        a.o2[rows] = mixed
        a.part[rows] = dot(mixed, a.w_output_cross[...]).astype(low)

    phase(1, finish_one, a.n2, cross_forward, project_peer)
    for copy in (loads.hidden_in, loads.hidden_out, load_g):
        copy.wait()

    def limit(slot):
        return jnp.where(slot < a.counts[0], a.lengths[slot], 0)

    def keep_rows(slot, rows):
        pos = lax.broadcasted_iota(jnp.int32, (seq, 1), 0)
        return jnp.where(pos < limit(slot), rows, 0.0)

    def finish_two(k, term):
        hidden = a.h1[k] + term
        a.h2[k] = hidden
        a.n3[own_rows(k)] = (hidden * inverse_rms(hidden) * gain_ffn).astype(low)

    def out_near_copy(k):
        return remote(a.out_part.at[k % 2, 1 - core], a.out_near.at[k], a.out_near_sem, (k,), c_peer)

    def out_far_copy(k):
        return remote(a.out_mine.at[k], a.out_far.at[k], a.out_far_sem, (k,), y_peer)

    def my_half(value):
        return jnp.where(y == 0, value[:, :half_width], value[:, half_width:])

    def other_half(value):
        return jnp.where(y == 0, value[:, half_width:], value[:, :half_width])

    def out_gather(k):
        out_near_copy(k).wait()
        term = a.out_part[k % 2, core].astype(wide) + a.out_near[k].astype(wide)
        a.out_mine[k] = other_half(term).astype(low)
        a.out_keep[k] = my_half(term) + my_half(a.h2[k])

    scale = 0.7978845608028654

    def feed_forward(k):
        rows = rows_of(k, chunk_rows)
        grad = jnp.concatenate(
            [
                keep_rows(k * CHUNK_SLOTS + s, a.g3[rows_of(k * CHUNK_SLOTS + s, seq)].astype(wide))
                for s in range(CHUNK_SLOTS)
            ],
            axis=0,
        ).astype(low)
        a.g3[rows] = grad
        a.pre[...] = dot(a.n3[rows], a.w_hidden_in[...])

        def gelu_rows(i, carry):
            part = rows_of(i, GELU_ROWS)
            pre = a.pre[part]
            square = pre * pre
            bend = jnp.tanh(scale * pre * (1.0 + 0.044715 * square))
            half = 0.5 * (1.0 + bend)
            curve = scale * (1.0 + 3 * 0.044715 * square)
            a.pre[part] = half + 0.5 * pre * (1.0 - bend * bend) * curve
            target = pl.ds(pl.multiple_of(k * chunk_rows + i * GELU_ROWS, GELU_ROWS), GELU_ROWS)
            a.act[target] = (pre * half).astype(low)
            return carry

        lax.fori_loop(0, chunk_rows // GELU_ROWS, gelu_rows, 0)
        out = dot_t(a.act[rows], a.w_hidden_out[...]).astype(low)
        a.out_part[k % 2, 0] = out[:half_rows]
        a.out_part[k % 2, 1] = out[half_rows:]
        out_near_copy(k).start()
        grad_pre = (a.pre[...] * dot(grad, a.w_hidden_out[...])).astype(low)
        a.d_pre[rows] = grad_pre
        a.part[rows] = dot_t(grad_pre, a.w_hidden_in[...]).astype(low)

    phase(2, finish_two, a.n3, feed_forward, out_gather)

    def column_copy(which, k):
        return remote(
            a.col_send.at[which, k],
            a.columns.at[which, :, own_rows(k)],
            a.col_sem,
            (which, k),
            c_peer,
        )

    def emit_columns(which, k, value):
        value = value.T
        left, right = value[:quarter_width], value[quarter_width:]
        first = core == 0
        a.columns[which, :, own_rows(k)] = jnp.where(first, left, right).astype(low)
        a.col_send[which, k] = jnp.where(first, right, left).astype(low)
        column_copy(which, k).start()

    def finish_out(k):
        out_far_copy(k).wait()
        value = a.out_keep[k] + a.out_far[k].astype(wide)
        emit_columns(0, k, keep_rows(k * CHUNK_SLOTS + core, value))

    orders = (tuple(range(levels)), (1, 0) + tuple(range(2, levels)))

    def dp_rank(half, level):
        return (dp_me >> orders[half][level]) & 1

    def dp_copy(block, half, level):
        buffer = block % 2
        count = 1 << (levels - 1 - level)
        source = a.term if level == 0 else a.holds[level - 1]
        part = pl.ds((1 - dp_rank(half, level)) * count, count)
        return remote(
            source.at[buffer, half, part],
            a.lands[level].at[buffer, half],
            a.dp_sem,
            (block, half, level),
            dp_peer(1 << orders[half][level]),
        )

    def raw_copy(block):
        return pltpu.make_async_copy(
            a.term.at[block % 2], a.raw_grads.at[block], a.dp_sem.at[0, block, 0, 0]
        )

    def credit_wait(block, half, level):
        pl.semaphore_wait(a.credit_sem.at[block % 2, half, level], 1)

    def dp_begin(block, halves=(0, 1)):
        if in_kernel:
            for half in halves:
                if block >= 2:
                    credit_wait(block, half, 0)
                dp_copy(block, half, 0).start()
        elif 1 in halves:
            raw_copy(block).start()

    def dp_advance(block, level, halves=(0, 1)):
        if not in_kernel:
            return
        buffer = block % 2
        count = 1 << (levels - 1 - level)
        for half in halves:
            dp_copy(block, half, level).wait()
            source = a.term if level == 0 else a.holds[level - 1]
            part = pl.ds(dp_rank(half, level) * count, count)
            value = source[buffer, half, part].astype(wide)
            value += a.lands[level][buffer, half].astype(wide)
            if level == levels - 1:
                emit_grads(block, half, value[0])
            else:
                a.holds[level][buffer, half] = value.astype(low)
            if block < 2:
                pl.semaphore_signal(
                    a.credit_sem.at[buffer, half, level],
                    inc=1,
                    device_id=dp_peer(1 << orders[half][level]),
                    device_id_type=MESH,
                )
            if level + 1 < levels:
                if block >= 2:
                    credit_wait(block, half, level + 1)
                dp_copy(block, half, level + 1).start()

    def at_chunk(k, step, *moves):
        @pl.when(k == step)
        def _():
            for move in moves:
                dp_advance(*move)

    def dp_finish_raw(block):
        if not in_kernel:
            raw_copy(block).wait()

    def emit_grads(block, half, value):
        columns = slice(half * half_width, (half + 1) * half_width)
        if block == 0:
            a.grad_hidden_out[:, columns] = value
        elif block == 1:
            a.grad_hidden_in[:, columns] = value
        else:
            start = (4 if block == 2 else 0) + 2 * half
            for i, name in enumerate(Weights._fields[start : start + 2]):
                getattr(a, "grad_" + name)[...] = value[:, i * inner : (i + 1) * inner]

    piece = cfg.piece
    groups = 2
    group_rows = width // groups
    pieces_each = max(group_rows // piece, 1) if in_kernel else 1

    def store_pieces(block, g, rows):
        if in_kernel:
            for i in range(pieces_each):
                for gg in range(groups):
                    if gg != g:
                        continue
                    for half in range(2):
                        index = piece_index(gg * pieces_each + i, orders[half])
                        a.term[block % 2, half, index] = rows[
                            i * piece : (i + 1) * piece,
                            half * half_width : (half + 1) * half_width,
                        ]
        else:
            a.term[block % 2, g * group_rows : (g + 1) * group_rows] = rows

    def plain_grads(block, left, right):
        for g in range(groups):
            columns = slice(g * group_rows, (g + 1) * group_rows)
            store_pieces(block, g, t_dot(left[:, columns], right[...]).astype(low))

    def turned_grads(block, half):
        value = a.enc[half * 2 * inner : (half + 1) * 2 * inner].T
        columns = slice(half * half_width, (half + 1) * half_width)
        if in_kernel:
            for i in range(width // piece):
                index = piece_index(i, orders[half])
                a.term[block % 2, half, index] = value[i * piece : (i + 1) * piece]
        else:
            a.term[block % 2, :, columns] = value

    def turned_rows(i):
        return slice(i * inner, (i + 1) * inner)

    plain_grads(0, a.g3, a.act)
    dp_begin(0)
    plain_grads(1, a.n3, a.d_pre)
    dp_begin(1)

    def finish_three(k, term):
        grad_rows, grad_gain = norm_back(a.h2[k], gain_ffn, term)
        add_gain(2, grad_gain)
        grad = a.g3[own_rows(k)].astype(wide) + grad_rows
        a.dh[k] = grad
        a.dh2[own_rows(k)] = grad.astype(low)

    def score_back(soft, grad_soft):
        weights = soft.astype(wide)
        row_inner = jnp.sum(weights * grad_soft, axis=-1, keepdims=True)
        return (weights * (grad_soft - row_inner)).astype(low)

    def cross_backward(k):
        rows = rows_of(k, chunk_rows)
        grad_mixed = dot_t(a.dh2[rows], a.w_output_cross[...]).astype(low)
        a.pair[rows, inner:] = grad_mixed
        a.pair[rows, :inner] = a.q2[rows]
        query = a.q2[rows]
        grads = []
        for s in range(CHUNK_SLOTS):
            slot = k * CHUNK_SLOTS + s
            part = slice(s * seq, (s + 1) * seq)
            enc_rows = rows_of(slot, enc_len)
            tall_grad, tall_query = stack(grad_mixed[part]), stack(query[part])
            soft = a.soft2[slot]
            grad_scores = score_back(soft, dot_t(tall_grad, a.v2[enc_rows]))
            a.dkv[slot, :inner] = t_dot(tall_query, grad_scores).astype(low)
            a.dkv[slot, inner:] = t_dot(tall_grad, soft).astype(low)
            grads.append(unstack(dot(grad_scores, a.k2[enc_rows])).astype(low))
        grads = jnp.concatenate(grads, axis=0)
        a.d_pre[rows, :inner] = grads
        a.part[rows] = dot(grads, a.w_query_cross[...]).astype(low)

    kv_blocks = 2 * inner // half_rows
    a.pre[...] = jnp.zeros_like(a.pre)

    def kv_part(i):
        if i == kv_blocks - 1:
            return a.h2.at[0]
        return a.pre.at[slice(i * half_rows, (i + 1) * half_rows)]

    def add_kv(slot, buffer):
        value = dot(a.dkv[slot], a.enc[rows_of(buffer, enc_len)])
        for i in range(kv_blocks):
            kv_part(i)[...] += value[i * half_rows : (i + 1) * half_rows]

    def kv_chunk(k):
        @pl.when(k == 0)
        def _():
            a.h2[0] = jnp.zeros_like(a.h2[0])

        for i in range(2):
            enc_copy(2 * k + i, i).wait()
            add_kv(2 * k + i, i)

            @pl.when(k + 1 < chunks)
            def _():
                enc_copy(2 * k + 2 + i, i).start()

        at_chunk(k, 2, (0, 0))
        at_chunk(k, 3, (1, 0))

    enc_copy(0, 0).start()
    enc_copy(1, 1).start()
    phase(3, finish_three, a.dh2, cross_backward, kv_chunk)

    peer_copy = remote(
        a.pair.at[rows_of(1 - y, chip_slots * seq)], a.pair_peer, a.peer_sem, (0,), y_peer
    )
    peer_copy.start()
    a.enc[turned_rows(0)] = t_dot(a.d_pre[:, :inner], a.n2[...]).astype(low)
    for i in range(kv_blocks):
        a.enc[inner + i * half_rows : inner + (i + 1) * half_rows] = kv_part(i)[...].astype(low)
    a.enc[turned_rows(3)] = t_dot(a.o2[...], a.dh2[...]).astype(low)
    dp_finish_raw(0)
    for half in range(2):
        turned_grads(2, half)
    dp_advance(0, 1)
    dp_begin(2)

    def finish_four(k, term):
        grad_rows, grad_gain = norm_back(a.h1[k], gain_cross, term)
        add_gain(1, grad_gain)
        grad = a.dh[k] + grad_rows
        a.dh[k] = grad
        a.dh1[own_rows(k)] = grad.astype(low)

    def self_backward(k):
        rows = rows_of(k, chunk_rows)
        grad_mixed = dot_t(a.dh1[rows], a.w_output_self[...]).astype(low)
        query, keys, values = a.q1[rows], a.k1[rows], a.v1[rows]
        grads = [[], [], []]
        for s in range(CHUNK_SLOTS):
            part = slice(s * seq, (s + 1) * seq)
            tall_grad, tall_query = stack(grad_mixed[part]), stack(query[part])
            soft = a.soft1[k * CHUNK_SLOTS + s]
            grad_scores = score_back(soft, dot_t(tall_grad, values[part]))
            a.table[...] += grad_scores.astype(wide)
            grads[0].append(unstack(dot(grad_scores, keys[part])).astype(low))
            grads[1].append(t_dot(grad_scores, tall_query).astype(low))
            grads[2].append(t_dot(soft, tall_grad).astype(low))
        grads = [jnp.concatenate(g, axis=0) for g in grads]
        a.q1[rows], a.k1[rows], a.v1[rows] = grads
        a.part[rows] = (
            dot(grads[0], a.w_query_self[...])
            + dot(grads[1], a.w_key_self[...])
            + dot(grads[2], a.w_value_self[...])
        ).astype(low)

    def self_moves(k):
        at_chunk(k, 1, (1, 1))
        at_chunk(k, 2, (0, 2))
        at_chunk(k, 3, (2, 0))

    phase(4, finish_four, a.dh1, self_backward, self_moves, y_send_last)
    for k in range(chunks):
        out_far_copy(k).start()
    mirror = jnp.where(row_i + col_i == seq - 1, 1.0, 0.0).astype(wide)
    for h in range(heads):
        flipped = exact_dot(a.table[h * seq : (h + 1) * seq, :], mirror)
        turned = pltpu.roll(flipped, 0, 1, stride=1, stride_axis=0)
        a.small[3:4, h * seq : (h + 1) * seq] = jnp.sum(turned, axis=0, keepdims=True)

    hops = [dp_peer(1 << k) for k in range(levels)] + [c_peer, y_peer]
    row = lax.broadcasted_iota(jnp.int32, a.small.shape, 0)

    def small_copy(i):
        return remote(a.small, a.small_land.at[i], a.small_sem, (i,), hops[i])

    def small_step(i):
        small_copy(i).wait()
        summed = row < (8 if i < levels else 3 if i == levels else 1)
        a.small[...] += jnp.where(summed, a.small_land[i], 0.0)
        if i < levels + 1:
            small_copy(i + 1).start()

    small_copy(0).start()
    a.enc[turned_rows(0)] = t_dot(a.q1[...], a.n1[...]).astype(low)
    a.enc[turned_rows(1)] = t_dot(a.k1[...], a.n1[...]).astype(low)
    dp_finish_raw(1)
    turned_grads(3, 0)
    dp_begin(3, (0,))
    a.enc[turned_rows(2)] = t_dot(a.v1[...], a.n1[...]).astype(low)
    a.enc[turned_rows(3)] = t_dot(a.o1[...], a.dh1[...]).astype(low)
    turned_grads(3, 1)
    dp_begin(3, (1,))
    small_step(0)
    dp_advance(2, 1)
    dp_advance(1, 2)
    peer_copy.wait()

    def enc_partial(k):
        rows = rows_of(k, seq)
        enc_rows = rows_of(k, enc_len)
        pair = a.pair_peer[rows]
        tall_query, tall_grad = stack(pair[:, :inner]), stack(pair[:, inner:])
        soft = softmax(dot_t(tall_query, a.k2_peer[enc_rows]))
        grad_scores = score_back(soft, dot_t(tall_grad, a.v2_peer[enc_rows]))
        peer_grads = jnp.concatenate(
            [t_dot(tall_query, grad_scores).astype(low), t_dot(tall_grad, soft).astype(low)], axis=0
        )
        own = t_dot(a.dkv[chip_slot(k)], a.w_kv[: 2 * inner])
        return own + t_dot(peer_grads, a.w_kv[2 * inner :])

    enc_each = chip_slots // 2

    def enc_near_copy(j):
        rows = rows_of(j, enc_len)
        return remote(a.n3.at[rows], a.act.at[rows], a.enc_near_sem, (j,), c_peer)

    def enc_give(j, carry):
        a.n3[rows_of(j, enc_len)] = enc_partial((1 - core) * enc_each + j).astype(low)
        enc_near_copy(j).start()
        return carry

    def enc_keep(j, carry):
        @pl.when(j == 1)
        def _():
            dp_advance(3, 0, (0,))

        partial = enc_partial(core * enc_each + j)
        enc_near_copy(j).wait()
        rows = rows_of(j, enc_len)
        a.enc_out[rows] = (partial + a.act[rows].astype(wide)).astype(low)
        return carry

    lax.fori_loop(0, enc_each, enc_give, 0)
    small_step(1)
    lax.fori_loop(0, enc_each, enc_keep, 0)
    for i in range(2, levels):
        small_step(i)
    dp_advance(3, 0, (1,))
    store_enc = load(2, a.enc_out, a.encoded_grad)
    store_enc.start()

    def phase_five(k):
        for copy in last_copies(k):
            copy.wait()
        rows = my_half(a.x[own_rows(k)]).astype(wide)
        inverse = inverse_rms(a.x[own_rows(k)].astype(wide))
        sums = (a.inner_send[k] + a.inner_far[k])[:1]
        row_inner = jnp.broadcast_to(sums, (half_rows, half_rows)).T[:, :1] * (1.0 / width)
        term = my_half(a.h1[k]) + a.far[0, k, :, :half_width].astype(wide)
        grad_rows = inverse * my_half(gain_self) * term
        grad_rows -= rows * (inverse * inverse * inverse) * row_inner
        emit_columns(1, k, my_half(a.dh[k]) + grad_rows)

    each_chunk(phase_five)
    dp_advance(2, 2)
    dp_advance(3, 1)
    small_step(levels)
    each_chunk(finish_out)
    dp_advance(3, 2)
    small_step(levels + 1)
    dp_finish_raw(2)
    dp_finish_raw(3)
    for k in range(chunks):
        column_copy(0, k).wait()
        column_copy(1, k).wait()
    stores = [
        load(0, a.columns.at[0], a.layer_out),
        load(1, a.columns.at[1], a.input_grad),
    ]
    for store in stores:
        store.start()
    a.small_out[...] = a.small[...]
    for store in (*stores, store_enc):
        store.wait()


def finish_kernel(count, heads, seq, *refs):
    small, buckets = refs[count], refs[count + 1]
    targets, held, sems = refs[count + 2 : 2 * count + 6], refs[2 * count + 6 : -1], refs[-1]
    copies = [pltpu.make_async_copy(refs[i], held[i], sems.at[i]) for i in range(count)]
    for copy in copies:
        copy.start()
    for i in range(count):
        copies[i].wait()
        copies[i] = pltpu.make_async_copy(held[i], targets[i], sems.at[i])
        copies[i].start()
    for i in range(3):
        targets[count + i][...] = small[i, :]
    sums = jnp.concatenate([small[3:4, h * seq : (h + 1) * seq] for h in range(heads)], axis=0)
    by_lane = pltpu.roll(jnp.broadcast_to(buckets[...], (8, seq)), seq - 1, 1)[:1]
    kinds = targets[count + 3].shape[1]
    bucket = lax.broadcasted_iota(jnp.int32, (kinds, seq), 0)
    chosen = jnp.where(by_lane == bucket, 1.0, 0.0).astype(wide)
    targets[count + 3][...] = lax.dot_general(
        sums,
        chosen,
        (((1,), (1,)), ((), ())),
        precision=highest,
        preferred_element_type=wide,
    )
    for copy in copies:
        copy.wait()


def per_device(*args):
    (
        inputs,
        encoded,
        example_counts,
        lengths,
        buckets,
        gain_self,
        gain_cross,
        gain_ffn,
        bias_table,
    ) = args[:9]
    weights = args[9:19]
    out_grad = args[19]
    rows, width = inputs.shape
    seq = buckets.shape[0]
    slots = lengths.shape[0]
    enc_rows = encoded.shape[0]
    enc_len = enc_rows // slots
    inner = weights[0].shape[1]
    hidden = weights[8].shape[1]
    heads = inner // HD
    dp_count = lax.axis_size("dp")
    levels = dp_count.bit_length() - 1
    piece = width // dp_count
    in_kernel = piece % 16 == 0
    chunks = slots // CHUNK_SLOTS
    half = CHUNK_SLOTS * seq // 2

    ins = dict(
        lengths=(lengths, SM),
        counts=(example_counts, SM),
        gain_self=(gain_self, VM),
        gain_cross=(gain_cross, VM),
        gain_ffn=(gain_ffn, VM),
        table_in=(bias_table.T, VM),
        buckets=(buckets[None], VM),
        inputs=(inputs, HBM),
        encoded=(encoded, HBM),
        out_grad=(out_grad, HBM),
    )
    for name, weight in zip(Weights._fields, weights, strict=True):
        ins[name] = (weight, HBM)
    for name in Weights._fields[:8]:
        ins[name] = (ins[name][0].T, HBM)
    shape = jax.ShapeDtypeStruct
    outs = dict(
        layer_out=(shape((width // 4, rows), low), HBM),
        input_grad=(shape((width // 4, rows), low), HBM),
        encoded_grad=(shape((enc_rows // 4, width), low), HBM),
        small_out=(shape((8, width), wide), VM),
    )
    if in_kernel:
        for name, weight in zip(Weights._fields, weights, strict=True):
            outs["grad_" + name] = (shape((piece, weight.shape[1]), wide), VM)
    else:
        outs.update(raw_grads=(shape((4, width, width), low), HBM))
    vmem, dma = pltpu.VMEM, pltpu.SemaphoreType.DMA
    quarter = width // 4
    whole_rows = vmem((rows, width), low)
    hidden_rows = vmem((rows, hidden), low)
    inner_rows = vmem((rows, inner), low)
    own_wide = vmem((chunks, half, width), wide)
    own_low = vmem((chunks, half, width), low)
    scratch = {
        "w_" + name: vmem(ins[name][0].shape, low)
        for name in Weights._fields
        if name not in Weights._fields[5:7]
    }
    scratch.update(
        x=whole_rows,
        g3=whole_rows,
        enc=vmem((2 * enc_len, width), low),
        n1=whole_rows,
        n2=whole_rows,
        n3=whole_rows,
        dh1=whole_rows,
        dh2=whole_rows,
        part=whole_rows,
        act=hidden_rows,
        d_pre=hidden_rows,
        q1=inner_rows,
        k1=inner_rows,
        v1=inner_rows,
        o1=inner_rows,
        q2=inner_rows,
        o2=inner_rows,
        k2=vmem((enc_rows, inner), low),
        v2=vmem((enc_rows, inner), low),
        h1=own_wide,
        h2=own_wide,
        dh=own_wide,
        soft1=vmem((slots, heads * seq, seq), low),
        soft2=vmem((slots, heads * seq, enc_len), low),
        dkv=vmem((slots, 2 * inner, enc_len), low),
        near=own_low,
        mine=own_low,
        far=vmem((2, chunks, half, width), low),
        out_part=vmem((2, 2, half, width), low),
        out_near=own_low,
        out_mine=vmem((chunks, half, width // 2), low),
        out_keep=vmem((chunks, half, width // 2), wide),
        out_far=vmem((chunks, half, width // 2), low),
        columns=vmem((2, quarter, rows), low),
        col_send=vmem((2, chunks, quarter, half), low),
        w_kv=vmem((4 * inner, width), low),
        k2_peer=vmem((enc_rows // 2, inner), low),
        v2_peer=vmem((enc_rows // 2, inner), low),
        pair=vmem((rows, 2 * inner), low),
        pair_peer=vmem((rows // 2, 2 * inner), low),
        inner_send=vmem((chunks, 8, half), wide),
        inner_far=vmem((chunks, 8, half), wide),
        enc_out=vmem((enc_rows // 4, width), low),
        pre=vmem((CHUNK_SLOTS * seq, hidden), wide),
        bias=vmem((heads * seq, seq), wide),
        table=vmem((heads * seq, seq), wide),
        small=vmem((8, width), wide),
        small_land=vmem((levels + 2, 8, width), wide),
        load_sem=dma((3 + len(weights),)),
        enc_sem=dma((2,)),
        near_sem=dma((2, 5, chunks)),
        far_sem=dma((2, 5, chunks)),
        share_sem=dma((2, 5, chunks)),
        out_near_sem=dma((2, chunks)),
        out_far_sem=dma((2, chunks)),
        col_sem=dma((2, 2, chunks)),
        enc_near_sem=dma((2, 2)),
        peer_sem=dma((2, 1)),
        kv_sem=dma((2, 1)),
        inner_sem=dma((2, chunks)),
        dp_sem=dma((2, 4, 2, levels)),
        small_sem=dma((2, levels + 2)),
        credit_sem=pltpu.SemaphoreType.REGULAR((2, 2, levels)),
    )
    if in_kernel:
        scratch.update(term=vmem((2, 2, dp_count, piece, width // 2), low))
        for level in range(levels):
            count = 1 << (levels - 1 - level)
            scratch["land%d" % level] = vmem((2, 2, count, piece, width // 2), low)
            if level + 1 < levels:
                scratch["hold%d" % level] = vmem((2, 2, count, piece, width // 2), low)
    else:
        scratch.update(term=vmem((2, width, width), low))
    cfg = SimpleNamespace(
        seq=seq,
        enc_len=enc_len,
        slots=slots,
        width=width,
        heads=heads,
        levels=levels,
        in_kernel=in_kernel,
        piece=piece,
    )
    results = pl.pallas_call(
        functools.partial(layer_kernel, cfg, tuple(ins) + tuple(outs) + tuple(scratch)),
        out_shape=tuple(o[0] for o in outs.values()),
        in_specs=[i[1] for i in ins.values()],
        out_specs=tuple(o[1] for o in outs.values()),
        scratch_shapes=list(scratch.values()),
        compiler_params=pltpu.CompilerParams(
            collective_id=1, has_side_effects=True, vmem_limit_bytes=65000 * 2**10
        ),
    )(*[i[0] for i in ins.values()])
    moved = [i for i, name in enumerate(outs) if name not in ("small_out", "raw_grads")]
    buckets_row = buckets[None]
    kinds = bias_table.shape[0]
    finals = pl.pallas_call(
        functools.partial(finish_kernel, len(moved), heads, seq),
        out_shape=(
            *(shape(results[i].shape, results[i].dtype) for i in moved),
            *(shape((width,), wide) for _ in range(3)),
            shape((heads, kinds), wide),
        ),
        in_specs=[HBM] * len(moved) + [VM, VM],
        out_specs=(HBM,) * len(moved) + (VM,) * 4,
        scratch_shapes=[
            *(vmem(results[i].shape, results[i].dtype) for i in moved),
            dma((len(moved),)),
        ],
    )(*[results[i] for i in moved], results[3], buckets_row)
    if in_kernel:
        grads = finals[3 : len(moved)]
    else:
        raw = results[4]
        parts = [raw[3][:, i * inner : (i + 1) * inner] for i in range(4)]
        parts += [raw[2][:, i * inner : (i + 1) * inner] for i in range(4)]
        grads = [
            lax.psum_scatter(part.astype(wide), "dp", scatter_dimension=0, tiled=True)
            for part in (*parts, raw[1], raw[0])
        ]
    gains = finals[len(moved) : len(moved) + 3]
    return (finals[0].T, finals[1].T, finals[2], *gains, finals[-1].T, *grads)


def solution(mesh):
    columns = P(None, "tensor")
    both = P("dp", "tensor")
    placed = (
        (P("dp", None), P("dp", None), P("dp"), P("dp"), P(), P(), P(), P())
        + (columns,) * 11
        + (P("dp", None),)
    )
    return jax.shard_map(
        per_device,
        mesh=mesh,
        in_specs=placed,
        out_specs=(both, both, P(("dp", "tensor"), None), P(), P(), P(), columns) + (both,) * 10,
        check_vma=False,
    )
```

```python
import functools
from types import SimpleNamespace
from typing import NamedTuple

import jax
import jax.numpy as jnp
from jax import lax
from jax.experimental import pallas as pl
from jax.experimental.pallas import tpu as pltpu
from jax.sharding import PartitionSpec as P

HD = 64
CHUNK_SLOTS = 2
GELU_ROWS = 32
MAIN_ROWS = 112
TAIL_ROWS = 2
TILE = (16, 128)

norm_epsilon = 1e-06
masked_score = -1e30
highest = lax.Precision.HIGHEST
MESH = pl.DeviceIdType.MESH
VM = pl.BlockSpec(memory_space=pltpu.VMEM)
SM = pl.BlockSpec(memory_space=pltpu.SMEM)
HBM = pl.BlockSpec(memory_space=pl.ANY)
low = jnp.bfloat16
wide = jnp.float32


def dot(left, right):
    return lax.dot_general(left, right, (((1,), (0,)), ((), ())), preferred_element_type=wide)


def dot_t(left, right):
    return lax.dot_general(left, right, (((1,), (1,)), ((), ())), preferred_element_type=wide)


def t_dot(left, right):
    return lax.dot_general(left, right, (((0,), (0,)), ((), ())), preferred_element_type=wide)


def exact_dot(left, right):
    return jnp.dot(left, right, precision=highest, preferred_element_type=wide)


def inverse_rms(rows):
    return lax.rsqrt(jnp.mean(rows * rows, axis=-1, keepdims=True) + norm_epsilon)


def norm_back(rows, gain, grad):
    inverse = inverse_rms(rows)
    scaled = gain * grad
    inner = jnp.mean(scaled * rows, axis=-1, keepdims=True)
    grad_rows = inverse * scaled - rows * (inverse * inverse * inverse) * inner
    return grad_rows, jnp.sum(grad * rows * inverse, axis=0, keepdims=True)


def tensor_peer(bit):
    return (lax.axis_index("dp"), lax.axis_index("tensor") ^ bit)


def dp_peer(bit):
    return (lax.axis_index("dp") ^ bit, lax.axis_index("tensor"))


def piece_index(rank, order):
    return sum(((rank >> bit) & 1) << (len(order) - 1 - k) for k, bit in enumerate(order))


class Weights(NamedTuple):
    query_self: object
    key_self: object
    value_self: object
    output_self: object
    query_cross: object
    key_cross: object
    value_cross: object
    output_cross: object
    hidden_in: object
    hidden_out: object


def layer_kernel(cfg, names, *refs):
    a = SimpleNamespace(**dict(zip(names, refs, strict=True)))
    seq, enc_len, slots, width = cfg.seq, cfg.enc_len, cfg.slots, cfg.width
    heads, levels, in_kernel = cfg.heads, cfg.levels, cfg.in_kernel
    inner = heads * HD
    if in_kernel:
        a.lands = [getattr(a, "land%d" % i) for i in range(levels)]
        a.holds = [getattr(a, "hold%d" % i) for i in range(levels - 1)]
    chunks = slots // CHUNK_SLOTS
    chunk_rows = CHUNK_SLOTS * seq
    half_rows = chunk_rows // 2
    half_width = width // 2
    quarter_width = width // 4
    me = lax.axis_index("tensor")
    core = lax.rem(me, 2)
    y = me // 2
    dp_me = lax.axis_index("dp")
    c_peer, y_peer = tensor_peer(1), tensor_peer(2)

    def rows_of(k, count):
        return pl.ds(pl.multiple_of(k * count, count), count)

    def load(index, src, dst):
        return pltpu.make_async_copy(src, dst, a.load_sem.at[index])

    inner_rows = slice(0, inner), slice(inner, 2 * inner)
    first_rows, later_rows = pl.ds(0, chunk_rows), pl.ds(chunk_rows, slots * seq - chunk_rows)
    load_x = load(0, a.inputs.at[first_rows], a.x.at[first_rows])
    load_more = load(2 + len(Weights._fields), a.inputs.at[later_rows], a.x.at[later_rows])
    load_g = load(1, a.out_grad, a.g3)
    spots = {name: getattr(a, "w_" + name) for name in Weights._fields if hasattr(a, "w_" + name)}
    spots.update(key_cross=a.w_kv.at[inner_rows[0]], value_cross=a.w_kv.at[inner_rows[1]])
    loads = Weights(
        *(load(2 + i, getattr(a, name), spots[name]) for i, name in enumerate(Weights._fields))
    )
    loads.key_cross.start()
    loads.value_cross.start()
    load_x.start()
    for copy in loads[:4]:
        copy.start()
    load_more.start()

    barrier = pltpu.get_barrier_semaphore()
    peers = [c_peer, y_peer] + [dp_peer(1 << k) for k in range(levels)]
    for peer in peers:
        pl.semaphore_signal(barrier, inc=1, device_id=peer, device_id_type=MESH)

    def remote(src, dst, sems, index, peer):
        return pltpu.make_async_remote_copy(
            src_ref=src,
            dst_ref=dst,
            send_sem=sems.at[(0,) + index],
            recv_sem=sems.at[(1,) + index],
            device_id=peer,
            device_id_type=MESH,
        )

    def peer_weights():
        own, theirs = pl.ds(0, 2 * inner), pl.ds(2 * inner, 2 * inner)
        return remote(a.w_kv.at[own], a.w_kv.at[theirs], a.kv_sem, (0,), y_peer)

    def enc_copy(slot, buffer):
        rows = pl.ds(pl.multiple_of(slot * enc_len, enc_len), enc_len)
        target = a.enc.at[rows_of(buffer, enc_len)]
        return pltpu.make_async_copy(a.encoded.at[rows], target, a.enc_sem.at[buffer])

    enc_copy(0, 0).start()
    for copy in (loads.query_cross, loads.output_cross, loads.hidden_in, loads.hidden_out, load_g):
        copy.start()

    loads.key_cross.wait()
    loads.value_cross.wait()
    pl.semaphore_wait(barrier, len(peers))
    peer_weights().start()

    gain_self, gain_cross, gain_ffn = (
        ref[...].reshape(1, width) for ref in (a.gain_self, a.gain_cross, a.gain_ffn)
    )

    lane = lax.broadcasted_iota(jnp.int32, (1, inner), 1)
    masks = [jnp.where(lane // HD == h, 1.0, 0.0).astype(wide) for h in range(heads)]
    masks_low = [m.astype(low) for m in masks]
    row_i = lax.broadcasted_iota(jnp.int32, (seq, seq), 0)
    col_i = lax.broadcasted_iota(jnp.int32, (seq, seq), 1)
    bucket = lax.broadcasted_iota(jnp.int32, (a.table_in.shape[1], seq), 0)
    chosen = jnp.where(a.buckets[...] == bucket, 1.0, 0.0).astype(wide)
    per_dist = exact_dot(a.table_in[...], chosen)
    backward = jnp.where((row_i + col_i) % seq == 0, 1.0, 0.0).astype(wide)
    lines = exact_dot(per_dist, backward)
    for h in range(heads):
        line = jnp.broadcast_to(lines[h : h + 1, :], (seq, seq))
        turned = pltpu.roll(line, 0, 1, stride=1, stride_axis=0)
        a.bias[h * seq : (h + 1) * seq, :] = jnp.where(row_i >= col_i, turned, masked_score)
    a.table[...] = jnp.zeros_like(a.table)
    a.small[...] = jnp.zeros_like(a.small)

    def stack(rows):
        return jnp.concatenate([rows * m for m in masks_low], axis=0)

    def unstack(rows):
        return sum(rows[h * seq : (h + 1) * seq] * masks[h] for h in range(heads))

    def softmax(scores):
        peak = jnp.max(scores, axis=-1, keepdims=True)
        terms = jnp.exp(scores - peak)
        return (terms / jnp.sum(terms, axis=-1, keepdims=True)).astype(low)

    def own_rows(k):
        return pl.ds(pl.multiple_of(k * chunk_rows + core * half_rows, half_rows), half_rows)

    def other_rows(k):
        return pl.ds(pl.multiple_of(k * chunk_rows + (1 - core) * half_rows, half_rows), half_rows)

    def add_gain(index, value):
        a.small[index : index + 1, :] += value

    def near_copy(p, k):
        return remote(a.part.at[other_rows(k)], a.near.at[k], a.near_sem, (p, k), c_peer)

    main_rows = pl.ds(0, MAIN_ROWS)

    def pack_tail(rows):
        tail = rows[MAIN_ROWS : MAIN_ROWS + TAIL_ROWS]
        lanes = TILE[1]
        parts = [
            tail[r : r + 1, c * lanes : (c + 1) * lanes]
            for r in range(TAIL_ROWS)
            for c in range(rows.shape[1] // lanes)
        ]
        parts.append(jnp.zeros((TILE[0] - len(parts), lanes), wide))
        return jnp.concatenate(parts, axis=0).astype(low)

    def unpack_rows(main, tile, columns):
        tile = tile.astype(wide)
        each = columns // TILE[1]
        rest = half_rows - MAIN_ROWS
        spot = lax.broadcasted_iota(jnp.int32, (rest, columns), 0)
        block = jnp.zeros((rest, columns), wide)
        for r in range(TAIL_ROWS):
            line = jnp.concatenate(
                [tile[r * each + c : r * each + c + 1] for c in range(each)], axis=1
            )
            block = jnp.where(spot == r, jnp.broadcast_to(line, (rest, columns)), block)
        return jnp.concatenate([main.astype(wide), block], axis=0)

    def far_copies(p, k):
        return (
            remote(
                a.mine.at[k, main_rows], a.far.at[p % 2, k, main_rows], a.far_sem, (p, k), y_peer
            ),
            remote(a.tail_send.at[k], a.tail_far.at[p % 2, k], a.tail_sem, (p, k), y_peer),
        )

    def y_send(p, k):
        near_copy(p, k).wait()
        term = a.part[own_rows(k)].astype(wide) + a.near[k].astype(wide)
        a.mine[k] = term.astype(low)
        a.tail_send[k] = pack_tail(term)
        for copy in far_copies(p, k):
            copy.start()

    def last_copies(k):
        return (
            remote(
                a.mine.at[k, main_rows, pl.ds(0, half_width)],
                a.far.at[0, k, main_rows, pl.ds(0, half_width)],
                a.far_sem,
                (4, k),
                y_peer,
            ),
            remote(a.tail_send.at[k], a.tail_far.at[0, k], a.tail_sem, (4, k), y_peer),
            remote(a.inner_send.at[k], a.inner_far.at[k], a.inner_sem, (k,), y_peer),
        )

    def y_send_last(k):
        near_copy(4, k).wait()
        term = a.part[own_rows(k)].astype(wide) + a.near[k].astype(wide)
        a.h1[k] = term
        rows = a.x[own_rows(k)].astype(wide)
        product = term * rows
        row_inner = jnp.sum(product * gain_self, axis=-1, keepdims=True)
        add_gain(0, jnp.sum(product * inverse_rms(rows), axis=0, keepdims=True))
        a.inner_send[k] = jnp.broadcast_to(row_inner, (half_rows, half_rows)).T[:8]
        away = jnp.where(y == 0, term[:, half_width:], term[:, :half_width])
        a.mine[k, :, :half_width] = away.astype(low)
        a.tail_send[k] = pack_tail(away)
        for copy in last_copies(k):
            copy.start()

    def total(p, k):
        for copy in far_copies(p, k):
            copy.wait()
        far = unpack_rows(a.far[p % 2, k, :MAIN_ROWS], a.tail_far[p % 2, k], width)
        return a.mine[k].astype(wide) + far

    def share_copy(p, k, buffer):
        return remote(buffer.at[own_rows(k)], buffer.at[own_rows(k)], a.share_sem, (p, k), c_peer)

    def each_chunk(body):
        def step(k, carry):
            body(k)
            return carry

        lax.fori_loop(0, chunks, step, 0)

    def phase(p, finish, buffer, compute, extra=None, send=None):
        send = send or functools.partial(y_send, p)

        def begin(k):
            finish(k, total(p - 1, k))
            share_copy(p, k, buffer).start()

        def body(k):
            share_copy(p, k, buffer).wait()

            @pl.when(k + 1 < chunks)
            def _():
                begin(k + 1)

            compute(k)
            near_copy(p, k).start()

            @pl.when(k > 0)
            def _():
                send(k - 1)

            if extra is not None:
                extra(k)

        begin(0)
        each_chunk(body)
        send(chunks - 1)

    def project(slot, buffer):
        enc_copy(slot, buffer).wait()

        @pl.when(slot + 1 < slots)
        def _():
            enc_copy(slot + 1, 1 - buffer).start()

        rows = rows_of(slot, enc_len)
        a.k2[rows] = dot_t(a.enc[rows_of(buffer, enc_len)], a.w_kv[:inner]).astype(low)
        a.v2[rows] = dot_t(a.enc[rows_of(buffer, enc_len)], a.w_kv[inner : 2 * inner]).astype(low)

    def self_forward(k):
        rows = rows_of(k, chunk_rows)
        x = a.x[rows].astype(wide)
        normed = (x * inverse_rms(x) * gain_self).astype(low)
        a.n1[rows] = normed
        query = dot_t(normed, a.w_query_self[...]).astype(low)
        keys = dot_t(normed, a.w_key_self[...]).astype(low)
        values = dot_t(normed, a.w_value_self[...]).astype(low)
        a.q1[rows], a.k1[rows], a.v1[rows] = query, keys, values
        mixed = []
        for s in range(CHUNK_SLOTS):
            part = slice(s * seq, (s + 1) * seq)
            weights = softmax(dot_t(stack(query[part]), keys[part]) + a.bias[...])
            a.soft1[k * CHUNK_SLOTS + s] = weights
            mixed.append(unstack(dot(weights, values[part])).astype(low))
        mixed = jnp.concatenate(mixed, axis=0)
        a.o1[rows] = mixed
        a.part[rows] = dot(mixed, a.w_output_self[...]).astype(low)

    load_x.wait()
    for copy in loads[:4]:
        copy.wait()

    def phase_zero(k):
        @pl.when(k == 1)
        def _():
            load_more.wait()

        self_forward(k)
        near_copy(0, k).start()
        y_send(0, k)
        project(CHUNK_SLOTS * k, 0)
        project(CHUNK_SLOTS * k + 1, 1)

    each_chunk(phase_zero)
    loads.query_cross.wait()
    loads.output_cross.wait()
    peer_weights().wait()

    chip_slots = slots // 2

    def chip_slot(k):
        return chip_slots * y + k

    enc_copy(chip_slot(0), 0).start()

    def project_peer(k):
        buffer = lax.rem(k, 2)
        enc_copy(chip_slot(k), buffer).wait()

        @pl.when(k + 1 < chip_slots)
        def _():
            enc_copy(chip_slot(k + 1), 1 - buffer).start()

        rows = rows_of(k, enc_len)
        encoded = a.enc[rows_of(buffer, enc_len)]
        a.k2_peer[rows] = dot_t(encoded, a.w_kv[2 * inner : 3 * inner]).astype(low)
        a.v2_peer[rows] = dot_t(encoded, a.w_kv[3 * inner :]).astype(low)

    def finish_one(k, term):
        hidden = a.x[own_rows(k)].astype(wide) + term
        a.h1[k] = hidden
        a.n2[own_rows(k)] = (hidden * inverse_rms(hidden) * gain_cross).astype(low)

    def cross_forward(k):
        rows = rows_of(k, chunk_rows)
        query = dot_t(a.n2[rows], a.w_query_cross[...]).astype(low)
        a.q2[rows] = query
        mixed = []
        for s in range(CHUNK_SLOTS):
            slot = k * CHUNK_SLOTS + s
            enc_rows = rows_of(slot, enc_len)
            weights = softmax(dot_t(stack(query[s * seq : (s + 1) * seq]), a.k2[enc_rows]))
            a.soft2[slot] = weights
            mixed.append(unstack(dot(weights, a.v2[enc_rows])).astype(low))
        mixed = jnp.concatenate(mixed, axis=0)
        a.o2[rows] = mixed
        a.part[rows] = dot(mixed, a.w_output_cross[...]).astype(low)

    phase(1, finish_one, a.n2, cross_forward, project_peer)
    for copy in (loads.hidden_in, loads.hidden_out, load_g):
        copy.wait()

    def limit(slot):
        return jnp.where(slot < a.counts[0], a.lengths[slot], 0)

    def keep_rows(slot, rows):
        pos = lax.broadcasted_iota(jnp.int32, (seq, 1), 0)
        return jnp.where(pos < limit(slot), rows, 0.0)

    def finish_two(k, term):
        hidden = a.h1[k] + term
        a.h2[k] = hidden
        a.n3[own_rows(k)] = (hidden * inverse_rms(hidden) * gain_ffn).astype(low)

    def out_near_copy(k):
        return remote(a.out_part.at[k % 2, 1 - core], a.out_near.at[k], a.out_near_sem, (k,), c_peer)

    def out_far_copies(k):
        return (
            remote(
                a.out_mine.at[k, main_rows],
                a.out_far.at[k, main_rows],
                a.out_far_sem,
                (0, k),
                y_peer,
            ),
            remote(a.out_tail_send.at[k], a.out_tail_far.at[k], a.out_far_sem, (1, k), y_peer),
        )

    def my_half(value):
        return jnp.where(y == 0, value[:, :half_width], value[:, half_width:])

    def other_half(value):
        return jnp.where(y == 0, value[:, half_width:], value[:, :half_width])

    def out_gather(k):
        out_near_copy(k).wait()
        term = a.out_part[k % 2, core].astype(wide) + a.out_near[k].astype(wide)
        away = other_half(term)
        a.out_mine[k] = away.astype(low)
        a.out_tail_send[k] = pack_tail(away)
        a.out_keep[k] = my_half(term) + my_half(a.h2[k])

    scale = 0.7978845608028654

    def feed_forward(k):
        rows = rows_of(k, chunk_rows)
        grad = jnp.concatenate(
            [
                keep_rows(k * CHUNK_SLOTS + s, a.g3[rows_of(k * CHUNK_SLOTS + s, seq)].astype(wide))
                for s in range(CHUNK_SLOTS)
            ],
            axis=0,
        ).astype(low)
        a.g3[rows] = grad
        a.pre[...] = dot(a.n3[rows], a.w_hidden_in[...])

        def gelu_rows(i, carry):
            part = rows_of(i, GELU_ROWS)
            pre = a.pre[part]
            square = pre * pre
            bend = jnp.tanh(scale * pre * (1.0 + 0.044715 * square))
            half = 0.5 * (1.0 + bend)
            curve = scale * (1.0 + 3 * 0.044715 * square)
            a.pre[part] = half + 0.5 * pre * (1.0 - bend * bend) * curve
            target = pl.ds(pl.multiple_of(k * chunk_rows + i * GELU_ROWS, GELU_ROWS), GELU_ROWS)
            a.act[target] = (pre * half).astype(low)
            return carry

        lax.fori_loop(0, chunk_rows // GELU_ROWS, gelu_rows, 0)
        out = dot_t(a.act[rows], a.w_hidden_out[...]).astype(low)
        a.out_part[k % 2, 0] = out[:half_rows]
        a.out_part[k % 2, 1] = out[half_rows:]
        out_near_copy(k).start()
        grad_pre = (a.pre[...] * dot(grad, a.w_hidden_out[...])).astype(low)
        a.d_pre[rows] = grad_pre
        a.part[rows] = dot_t(grad_pre, a.w_hidden_in[...]).astype(low)

    phase(2, finish_two, a.n3, feed_forward, out_gather)

    def column_copy(which, k):
        return remote(
            a.col_send.at[which, k],
            a.columns.at[which, :, own_rows(k)],
            a.col_sem,
            (which, k),
            c_peer,
        )

    def emit_columns(which, k, value):
        value = value.T
        left, right = value[:quarter_width], value[quarter_width:]
        first = core == 0
        a.columns[which, :, own_rows(k)] = jnp.where(first, left, right).astype(low)
        a.col_send[which, k] = jnp.where(first, right, left).astype(low)
        column_copy(which, k).start()

    def finish_out(k):
        for copy in out_far_copies(k):
            copy.wait()
        far = unpack_rows(a.out_far[k, :MAIN_ROWS], a.out_tail_far[k], half_width)
        value = a.out_keep[k] + far
        emit_columns(0, k, keep_rows(k * CHUNK_SLOTS + core, value))

    orders = (tuple(range(levels)), (1, 0) + tuple(range(2, levels)))

    def dp_rank(half, level):
        return (dp_me >> orders[half][level]) & 1

    def dp_copy(block, half, level):
        buffer = block % 2
        count = 1 << (levels - 1 - level)
        source = a.term if level == 0 else a.holds[level - 1]
        part = pl.ds((1 - dp_rank(half, level)) * count, count)
        return remote(
            source.at[buffer, half, part],
            a.lands[level].at[buffer, half],
            a.dp_sem,
            (block, half, level),
            dp_peer(1 << orders[half][level]),
        )

    def raw_copy(block):
        return pltpu.make_async_copy(
            a.term.at[block % 2], a.raw_grads.at[block], a.dp_sem.at[0, block, 0, 0]
        )

    def credit_wait(block, half, level):
        pl.semaphore_wait(a.credit_sem.at[block % 2, half, level], 1)

    def dp_begin(block, halves=(0, 1)):
        if in_kernel:
            for half in halves:
                if block >= 2:
                    credit_wait(block, half, 0)
                dp_copy(block, half, 0).start()
        elif 1 in halves:
            raw_copy(block).start()

    def dp_advance(block, level, halves=(0, 1)):
        if not in_kernel:
            return
        buffer = block % 2
        count = 1 << (levels - 1 - level)
        for half in halves:
            dp_copy(block, half, level).wait()
            source = a.term if level == 0 else a.holds[level - 1]
            part = pl.ds(dp_rank(half, level) * count, count)
            value = source[buffer, half, part].astype(wide)
            value += a.lands[level][buffer, half].astype(wide)
            if level == levels - 1:
                emit_grads(block, half, value[0])
            else:
                a.holds[level][buffer, half] = value.astype(low)
            if block < 2:
                pl.semaphore_signal(
                    a.credit_sem.at[buffer, half, level],
                    inc=1,
                    device_id=dp_peer(1 << orders[half][level]),
                    device_id_type=MESH,
                )
            if level + 1 < levels:
                if block >= 2:
                    credit_wait(block, half, level + 1)
                dp_copy(block, half, level + 1).start()

    def at_chunk(k, step, *moves):
        @pl.when(k == step)
        def _():
            for move in moves:
                dp_advance(*move)

    def dp_finish_raw(block):
        if not in_kernel:
            raw_copy(block).wait()

    def emit_grads(block, half, value):
        columns = slice(half * half_width, (half + 1) * half_width)
        if block == 0:
            a.grad_hidden_out[:, columns] = value
        elif block == 1:
            a.grad_hidden_in[:, columns] = value
        else:
            start = (4 if block == 2 else 0) + 2 * half
            for i, name in enumerate(Weights._fields[start : start + 2]):
                getattr(a, "grad_" + name)[...] = value[:, i * inner : (i + 1) * inner]

    piece = cfg.piece
    groups = 2
    group_rows = width // groups
    pieces_each = max(group_rows // piece, 1) if in_kernel else 1

    def store_pieces(block, g, rows):
        if in_kernel:
            for i in range(pieces_each):
                for gg in range(groups):
                    if gg != g:
                        continue
                    for half in range(2):
                        index = piece_index(gg * pieces_each + i, orders[half])
                        a.term[block % 2, half, index] = rows[
                            i * piece : (i + 1) * piece,
                            half * half_width : (half + 1) * half_width,
                        ]
        else:
            a.term[block % 2, g * group_rows : (g + 1) * group_rows] = rows

    def plain_grads(block, left, right):
        for g in range(groups):
            columns = slice(g * group_rows, (g + 1) * group_rows)
            store_pieces(block, g, t_dot(left[:, columns], right[...]).astype(low))

    def turned_grads(block, half):
        value = a.enc[half * 2 * inner : (half + 1) * 2 * inner].T
        columns = slice(half * half_width, (half + 1) * half_width)
        if in_kernel:
            for i in range(width // piece):
                index = piece_index(i, orders[half])
                a.term[block % 2, half, index] = value[i * piece : (i + 1) * piece]
        else:
            a.term[block % 2, :, columns] = value

    def turned_rows(i):
        return slice(i * inner, (i + 1) * inner)

    plain_grads(0, a.g3, a.act)
    dp_begin(0)
    plain_grads(1, a.n3, a.d_pre)
    dp_begin(1)

    def finish_three(k, term):
        grad_rows, grad_gain = norm_back(a.h2[k], gain_ffn, term)
        add_gain(2, grad_gain)
        grad = a.g3[own_rows(k)].astype(wide) + grad_rows
        a.dh[k] = grad
        a.dh2[own_rows(k)] = grad.astype(low)

    def inner_by_head(grad_mixed, mixed):
        product = grad_mixed.astype(wide) * mixed.astype(wide)
        return [jnp.sum(product * m, axis=-1, keepdims=True) for m in masks]

    def score_back(soft, grad_soft, row_inner):
        return (soft.astype(wide) * (grad_soft - row_inner)).astype(low)

    def cross_backward(k):
        rows = rows_of(k, chunk_rows)
        grad_mixed = dot_t(a.dh2[rows], a.w_output_cross[...]).astype(low)
        inners = inner_by_head(grad_mixed, a.o2[rows])
        a.pair[rows, inner:] = grad_mixed
        a.pair[rows, :inner] = a.q2[rows]
        query = a.q2[rows]
        grads = []
        for s in range(CHUNK_SLOTS):
            slot = k * CHUNK_SLOTS + s
            part = slice(s * seq, (s + 1) * seq)
            enc_rows = rows_of(slot, enc_len)
            tall_grad, tall_query = stack(grad_mixed[part]), stack(query[part])
            soft = a.soft2[slot]
            row_inner = jnp.concatenate([column[part] for column in inners], axis=0)
            grad_scores = score_back(soft, dot_t(tall_grad, a.v2[enc_rows]), row_inner)
            a.dkv[slot, :inner] = t_dot(tall_query, grad_scores).astype(low)
            a.dkv[slot, inner:] = t_dot(tall_grad, soft).astype(low)
            grads.append(unstack(dot(grad_scores, a.k2[enc_rows])).astype(low))
        grads = jnp.concatenate(grads, axis=0)
        a.d_pre[rows, :inner] = grads
        a.part[rows] = dot(grads, a.w_query_cross[...]).astype(low)

    kv_blocks = 2 * inner // half_rows
    a.pre[...] = jnp.zeros_like(a.pre)

    def kv_part(i):
        if i == kv_blocks - 1:
            return a.h2.at[0]
        return a.pre.at[slice(i * half_rows, (i + 1) * half_rows)]

    def add_kv(slot, buffer):
        value = dot(a.dkv[slot], a.enc[rows_of(buffer, enc_len)])
        for i in range(kv_blocks):
            kv_part(i)[...] += value[i * half_rows : (i + 1) * half_rows]

    def kv_chunk(k):
        @pl.when(k == 0)
        def _():
            a.h2[0] = jnp.zeros_like(a.h2[0])

        for i in range(2):
            enc_copy(2 * k + i, i).wait()
            add_kv(2 * k + i, i)

            @pl.when(k + 1 < chunks)
            def _():
                enc_copy(2 * k + 2 + i, i).start()

        at_chunk(k, 2, (0, 0))
        at_chunk(k, 3, (1, 0))

    enc_copy(0, 0).start()
    enc_copy(1, 1).start()
    phase(3, finish_three, a.dh2, cross_backward, kv_chunk)

    peer_copy = remote(
        a.pair.at[rows_of(1 - y, chip_slots * seq)], a.pair_peer, a.peer_sem, (0,), y_peer
    )
    peer_copy.start()
    a.enc[turned_rows(0)] = t_dot(a.d_pre[:, :inner], a.n2[...]).astype(low)
    for i in range(kv_blocks):
        a.enc[inner + i * half_rows : inner + (i + 1) * half_rows] = kv_part(i)[...].astype(low)
    a.enc[turned_rows(3)] = t_dot(a.o2[...], a.dh2[...]).astype(low)
    dp_finish_raw(0)
    for half in range(2):
        turned_grads(2, half)
    dp_advance(0, 1)
    dp_begin(2)

    def finish_four(k, term):
        grad_rows, grad_gain = norm_back(a.h1[k], gain_cross, term)
        add_gain(1, grad_gain)
        grad = a.dh[k] + grad_rows
        a.dh[k] = grad
        a.dh1[own_rows(k)] = grad.astype(low)

    def self_backward(k):
        rows = rows_of(k, chunk_rows)
        grad_mixed = dot_t(a.dh1[rows], a.w_output_self[...]).astype(low)
        inners = inner_by_head(grad_mixed, a.o1[rows])
        query, keys, values = a.q1[rows], a.k1[rows], a.v1[rows]
        grads = [[], [], []]
        for s in range(CHUNK_SLOTS):
            part = slice(s * seq, (s + 1) * seq)
            tall_grad, tall_query = stack(grad_mixed[part]), stack(query[part])
            soft = a.soft1[k * CHUNK_SLOTS + s]
            row_inner = jnp.concatenate([column[part] for column in inners], axis=0)
            grad_scores = score_back(soft, dot_t(tall_grad, values[part]), row_inner)
            a.table[...] += grad_scores.astype(wide)
            grads[0].append(unstack(dot(grad_scores, keys[part])).astype(low))
            grads[1].append(t_dot(grad_scores, tall_query).astype(low))
            grads[2].append(t_dot(soft, tall_grad).astype(low))
        grads = [jnp.concatenate(g, axis=0) for g in grads]
        a.q1[rows], a.k1[rows], a.v1[rows] = grads
        a.part[rows] = (
            dot(grads[0], a.w_query_self[...])
            + dot(grads[1], a.w_key_self[...])
            + dot(grads[2], a.w_value_self[...])
        ).astype(low)

    def self_moves(k):
        at_chunk(k, 1, (1, 1))
        at_chunk(k, 2, (0, 2))
        at_chunk(k, 3, (2, 0))

    phase(4, finish_four, a.dh1, self_backward, self_moves, y_send_last)
    for k in range(chunks):
        for copy in out_far_copies(k):
            copy.start()
    mirror = jnp.where(row_i + col_i == seq - 1, 1.0, 0.0).astype(wide)
    for h in range(heads):
        flipped = exact_dot(a.table[h * seq : (h + 1) * seq, :], mirror)
        turned = pltpu.roll(flipped, 0, 1, stride=1, stride_axis=0)
        a.small[3:4, h * seq : (h + 1) * seq] = jnp.sum(turned, axis=0, keepdims=True)

    hops = [dp_peer(1 << k) for k in range(levels)] + [c_peer, y_peer]
    row = lax.broadcasted_iota(jnp.int32, a.small.shape, 0)

    def small_copy(i):
        return remote(a.small, a.small_land.at[i], a.small_sem, (i,), hops[i])

    def small_step(i):
        small_copy(i).wait()
        summed = row < (8 if i < levels else 3 if i == levels else 1)
        a.small[...] += jnp.where(summed, a.small_land[i], 0.0)
        if i < levels + 1:
            small_copy(i + 1).start()

    small_copy(0).start()
    a.enc[turned_rows(0)] = t_dot(a.q1[...], a.n1[...]).astype(low)
    a.enc[turned_rows(1)] = t_dot(a.k1[...], a.n1[...]).astype(low)
    dp_finish_raw(1)
    turned_grads(3, 0)
    dp_begin(3, (0,))
    a.enc[turned_rows(2)] = t_dot(a.v1[...], a.n1[...]).astype(low)
    a.enc[turned_rows(3)] = t_dot(a.o1[...], a.dh1[...]).astype(low)
    turned_grads(3, 1)
    dp_begin(3, (1,))
    small_step(0)
    dp_advance(2, 1)
    dp_advance(1, 2)
    peer_copy.wait()

    def enc_partial(k):
        rows = rows_of(k, seq)
        enc_rows = rows_of(k, enc_len)
        pair = a.pair_peer[rows]
        tall_query, tall_grad = stack(pair[:, :inner]), stack(pair[:, inner:])
        soft = softmax(dot_t(tall_query, a.k2_peer[enc_rows]))
        grad_soft = dot_t(tall_grad, a.v2_peer[enc_rows])
        row_inner = jnp.sum(soft.astype(wide) * grad_soft, axis=-1, keepdims=True)
        grad_scores = score_back(soft, grad_soft, row_inner)
        peer_grads = jnp.concatenate(
            [t_dot(tall_query, grad_scores).astype(low), t_dot(tall_grad, soft).astype(low)], axis=0
        )
        own = t_dot(a.dkv[chip_slot(k)], a.w_kv[: 2 * inner])
        return own + t_dot(peer_grads, a.w_kv[2 * inner :])

    enc_each = chip_slots // 2

    def enc_near_copy(j):
        rows = rows_of(j, enc_len)
        return remote(a.n3.at[rows], a.act.at[rows], a.enc_near_sem, (j,), c_peer)

    def enc_give(j, carry):
        at_chunk(j, 1, (3, 0, (0,)))
        a.n3[rows_of(j, enc_len)] = enc_partial((1 - core) * enc_each + j).astype(low)
        enc_near_copy(j).start()
        return carry

    def enc_keep(j, carry):
        at_chunk(j, 1, (3, 1, (0,)))
        partial = enc_partial(core * enc_each + j)
        enc_near_copy(j).wait()
        rows = rows_of(j, enc_len)
        a.enc_out[rows] = (partial + a.act[rows].astype(wide)).astype(low)
        return carry

    lax.fori_loop(0, enc_each, enc_give, 0)
    dp_advance(3, 0, (1,))
    small_step(1)
    lax.fori_loop(0, enc_each, enc_keep, 0)
    dp_advance(3, 1, (1,))
    for i in range(2, levels):
        small_step(i)
    store_enc = load(2, a.enc_out, a.encoded_grad)
    store_enc.start()

    def phase_five(k):
        for copy in last_copies(k):
            copy.wait()
        rows = my_half(a.x[own_rows(k)]).astype(wide)
        inverse = inverse_rms(a.x[own_rows(k)].astype(wide))
        sums = (a.inner_send[k] + a.inner_far[k])[:1]
        row_inner = jnp.broadcast_to(sums, (half_rows, half_rows)).T[:, :1] * (1.0 / width)
        far = unpack_rows(a.far[0, k, :MAIN_ROWS, :half_width], a.tail_far[0, k], half_width)
        term = my_half(a.h1[k]) + far
        grad_rows = inverse * my_half(gain_self) * term
        grad_rows -= rows * (inverse * inverse * inverse) * row_inner
        emit_columns(1, k, my_half(a.dh[k]) + grad_rows)

    each_chunk(phase_five)
    dp_advance(2, 2)
    small_step(levels)
    each_chunk(finish_out)
    dp_advance(3, 2)
    small_step(levels + 1)
    dp_finish_raw(2)
    dp_finish_raw(3)
    for k in range(chunks):
        column_copy(0, k).wait()
        column_copy(1, k).wait()
    stores = [
        load(0, a.columns.at[0], a.layer_out),
        load(1, a.columns.at[1], a.input_grad),
    ]
    for store in stores:
        store.start()
    a.small_out[...] = a.small[...]
    for store in (*stores, store_enc):
        store.wait()


def finish_kernel(count, heads, seq, *refs):
    small, buckets = refs[count], refs[count + 1]
    targets, held, sems = refs[count + 2 : 2 * count + 6], refs[2 * count + 6 : -1], refs[-1]
    copies = [pltpu.make_async_copy(refs[i], held[i], sems.at[i]) for i in range(count)]
    for copy in copies:
        copy.start()
    for i in range(count):
        copies[i].wait()
        copies[i] = pltpu.make_async_copy(held[i], targets[i], sems.at[i])
        copies[i].start()
    for i in range(3):
        targets[count + i][...] = small[i, :]
    sums = jnp.concatenate([small[3:4, h * seq : (h + 1) * seq] for h in range(heads)], axis=0)
    by_lane = pltpu.roll(jnp.broadcast_to(buckets[...], (8, seq)), seq - 1, 1)[:1]
    kinds = targets[count + 3].shape[1]
    bucket = lax.broadcasted_iota(jnp.int32, (kinds, seq), 0)
    chosen = jnp.where(by_lane == bucket, 1.0, 0.0).astype(wide)
    targets[count + 3][...] = lax.dot_general(
        sums,
        chosen,
        (((1,), (1,)), ((), ())),
        precision=highest,
        preferred_element_type=wide,
    )
    for copy in copies:
        copy.wait()


def per_device(*args):
    (
        inputs,
        encoded,
        example_counts,
        lengths,
        buckets,
        gain_self,
        gain_cross,
        gain_ffn,
        bias_table,
    ) = args[:9]
    weights = args[9:19]
    out_grad = args[19]
    rows, width = inputs.shape
    seq = buckets.shape[0]
    slots = lengths.shape[0]
    enc_rows = encoded.shape[0]
    enc_len = enc_rows // slots
    inner = weights[0].shape[1]
    hidden = weights[8].shape[1]
    heads = inner // HD
    dp_count = lax.axis_size("dp")
    levels = dp_count.bit_length() - 1
    piece = width // dp_count
    in_kernel = piece % 16 == 0
    chunks = slots // CHUNK_SLOTS
    half = CHUNK_SLOTS * seq // 2

    ins = dict(
        lengths=(lengths, SM),
        counts=(example_counts, SM),
        gain_self=(gain_self, VM),
        gain_cross=(gain_cross, VM),
        gain_ffn=(gain_ffn, VM),
        table_in=(bias_table.T, VM),
        buckets=(buckets[None], VM),
        inputs=(inputs, HBM),
        encoded=(encoded, HBM),
        out_grad=(out_grad, HBM),
    )
    for name, weight in zip(Weights._fields, weights, strict=True):
        ins[name] = (weight, HBM)
    for name in Weights._fields[:8]:
        ins[name] = (ins[name][0].T, HBM)
    shape = jax.ShapeDtypeStruct
    outs = dict(
        layer_out=(shape((width // 4, rows), low), HBM),
        input_grad=(shape((width // 4, rows), low), HBM),
        encoded_grad=(shape((enc_rows // 4, width), low), HBM),
        small_out=(shape((8, width), wide), VM),
    )
    if in_kernel:
        for name, weight in zip(Weights._fields, weights, strict=True):
            outs["grad_" + name] = (shape((piece, weight.shape[1]), wide), VM)
    else:
        outs.update(raw_grads=(shape((4, width, width), low), HBM))
    vmem, dma = pltpu.VMEM, pltpu.SemaphoreType.DMA
    quarter = width // 4
    whole_rows = vmem((rows, width), low)
    hidden_rows = vmem((rows, hidden), low)
    inner_rows = vmem((rows, inner), low)
    own_wide = vmem((chunks, half, width), wide)
    own_low = vmem((chunks, half, width), low)
    scratch = {
        "w_" + name: vmem(ins[name][0].shape, low)
        for name in Weights._fields
        if name not in Weights._fields[5:7]
    }
    scratch.update(
        x=whole_rows,
        g3=whole_rows,
        enc=vmem((2 * enc_len, width), low),
        n1=whole_rows,
        n2=whole_rows,
        n3=whole_rows,
        dh1=whole_rows,
        dh2=whole_rows,
        part=whole_rows,
        act=hidden_rows,
        d_pre=hidden_rows,
        q1=inner_rows,
        k1=inner_rows,
        v1=inner_rows,
        o1=inner_rows,
        q2=inner_rows,
        o2=inner_rows,
        k2=vmem((enc_rows, inner), low),
        v2=vmem((enc_rows, inner), low),
        h1=own_wide,
        h2=own_wide,
        dh=own_wide,
        soft1=vmem((slots, heads * seq, seq), low),
        soft2=vmem((slots, heads * seq, enc_len), low),
        dkv=vmem((slots, 2 * inner, enc_len), low),
        near=own_low,
        mine=own_low,
        far=vmem((2, chunks, half, width), low),
        out_part=vmem((2, 2, half, width), low),
        out_near=own_low,
        out_mine=vmem((chunks, half, width // 2), low),
        out_keep=vmem((chunks, half, width // 2), wide),
        out_far=vmem((chunks, half, width // 2), low),
        columns=vmem((2, quarter, rows), low),
        col_send=vmem((2, chunks, quarter, half), low),
        w_kv=vmem((4 * inner, width), low),
        k2_peer=vmem((enc_rows // 2, inner), low),
        v2_peer=vmem((enc_rows // 2, inner), low),
        pair=vmem((rows, 2 * inner), low),
        pair_peer=vmem((rows // 2, 2 * inner), low),
        tail_send=vmem((chunks, *TILE), low),
        tail_far=vmem((2, chunks, *TILE), low),
        out_tail_send=vmem((chunks, *TILE), low),
        out_tail_far=vmem((chunks, *TILE), low),
        inner_send=vmem((chunks, 8, half), wide),
        inner_far=vmem((chunks, 8, half), wide),
        enc_out=vmem((enc_rows // 4, width), low),
        pre=vmem((CHUNK_SLOTS * seq, hidden), wide),
        bias=vmem((heads * seq, seq), wide),
        table=vmem((heads * seq, seq), wide),
        small=vmem((8, width), wide),
        small_land=vmem((levels + 2, 8, width), wide),
        load_sem=dma((3 + len(weights),)),
        enc_sem=dma((2,)),
        near_sem=dma((2, 5, chunks)),
        far_sem=dma((2, 5, chunks)),
        share_sem=dma((2, 5, chunks)),
        out_near_sem=dma((2, chunks)),
        out_far_sem=dma((2, 2, chunks)),
        tail_sem=dma((2, 5, chunks)),
        col_sem=dma((2, 2, chunks)),
        enc_near_sem=dma((2, 2)),
        peer_sem=dma((2, 1)),
        kv_sem=dma((2, 1)),
        inner_sem=dma((2, chunks)),
        dp_sem=dma((2, 4, 2, levels)),
        small_sem=dma((2, levels + 2)),
        credit_sem=pltpu.SemaphoreType.REGULAR((2, 2, levels)),
    )
    if in_kernel:
        scratch.update(term=vmem((2, 2, dp_count, piece, width // 2), low))
        for level in range(levels):
            count = 1 << (levels - 1 - level)
            scratch["land%d" % level] = vmem((2, 2, count, piece, width // 2), low)
            if level + 1 < levels:
                scratch["hold%d" % level] = vmem((2, 2, count, piece, width // 2), low)
    else:
        scratch.update(term=vmem((2, width, width), low))
    cfg = SimpleNamespace(
        seq=seq,
        enc_len=enc_len,
        slots=slots,
        width=width,
        heads=heads,
        levels=levels,
        in_kernel=in_kernel,
        piece=piece,
    )
    results = pl.pallas_call(
        functools.partial(layer_kernel, cfg, tuple(ins) + tuple(outs) + tuple(scratch)),
        out_shape=tuple(o[0] for o in outs.values()),
        in_specs=[i[1] for i in ins.values()],
        out_specs=tuple(o[1] for o in outs.values()),
        scratch_shapes=list(scratch.values()),
        compiler_params=pltpu.CompilerParams(
            collective_id=1, has_side_effects=True, vmem_limit_bytes=65000 * 2**10
        ),
    )(*[i[0] for i in ins.values()])
    moved = [i for i, name in enumerate(outs) if name not in ("small_out", "raw_grads")]
    buckets_row = buckets[None]
    kinds = bias_table.shape[0]
    finals = pl.pallas_call(
        functools.partial(finish_kernel, len(moved), heads, seq),
        out_shape=(
            *(shape(results[i].shape, results[i].dtype) for i in moved),
            *(shape((width,), wide) for _ in range(3)),
            shape((heads, kinds), wide),
        ),
        in_specs=[HBM] * len(moved) + [VM, VM],
        out_specs=(HBM,) * len(moved) + (VM,) * 4,
        scratch_shapes=[
            *(vmem(results[i].shape, results[i].dtype) for i in moved),
            dma((len(moved),)),
        ],
    )(*[results[i] for i in moved], results[3], buckets_row)
    if in_kernel:
        grads = finals[3 : len(moved)]
    else:
        raw = results[4]
        parts = [raw[3][:, i * inner : (i + 1) * inner] for i in range(4)]
        parts += [raw[2][:, i * inner : (i + 1) * inner] for i in range(4)]
        grads = [
            lax.psum_scatter(part.astype(wide), "dp", scatter_dimension=0, tiled=True)
            for part in (*parts, raw[1], raw[0])
        ]
    gains = finals[len(moved) : len(moved) + 3]
    return (finals[0].T, finals[1].T, finals[2], *gains, finals[-1].T, *grads)


def solution(mesh):
    columns = P(None, "tensor")
    both = P("dp", "tensor")
    placed = (
        (P("dp", None), P("dp", None), P("dp"), P("dp"), P(), P(), P(), P())
        + (columns,) * 11
        + (P("dp", None),)
    )
    return jax.shard_map(
        per_device,
        mesh=mesh,
        in_specs=placed,
        out_specs=(both, both, P(("dp", "tensor"), None), P(), P(), P(), columns) + (both,) * 10,
        check_vma=False,
    )
```

```python
import functools
from types import SimpleNamespace
from typing import NamedTuple

import jax
import jax.numpy as jnp
from jax import lax
from jax.experimental import pallas as pl
from jax.experimental.pallas import tpu as pltpu
from jax.sharding import PartitionSpec as P

HD = 64
CHUNK_SLOTS = 2
GELU_ROWS = 32
MAIN_ROWS = 112
TAIL_ROWS = 2
TILE = (16, 128)

norm_epsilon = 1e-06
masked_score = -1e30
highest = lax.Precision.HIGHEST
MESH = pl.DeviceIdType.MESH
VM = pl.BlockSpec(memory_space=pltpu.VMEM)
SM = pl.BlockSpec(memory_space=pltpu.SMEM)
HBM = pl.BlockSpec(memory_space=pl.ANY)
low = jnp.bfloat16
wide = jnp.float32


def dot(left, right):
    return lax.dot_general(left, right, (((1,), (0,)), ((), ())), preferred_element_type=wide)


def dot_t(left, right):
    return lax.dot_general(left, right, (((1,), (1,)), ((), ())), preferred_element_type=wide)


def t_dot(left, right):
    return lax.dot_general(left, right, (((0,), (0,)), ((), ())), preferred_element_type=wide)


def exact_dot(left, right):
    return jnp.dot(left, right, precision=highest, preferred_element_type=wide)


def inverse_rms(rows):
    return lax.rsqrt(jnp.mean(rows * rows, axis=-1, keepdims=True) + norm_epsilon)


def norm_back(rows, gain, grad):
    inverse = inverse_rms(rows)
    scaled = gain * grad
    inner = jnp.mean(scaled * rows, axis=-1, keepdims=True)
    grad_rows = inverse * scaled - rows * (inverse * inverse * inverse) * inner
    return grad_rows, jnp.sum(grad * rows * inverse, axis=0, keepdims=True)


def tensor_peer(bit):
    return (lax.axis_index("dp"), lax.axis_index("tensor") ^ bit)


def dp_peer(bit):
    return (lax.axis_index("dp") ^ bit, lax.axis_index("tensor"))


def piece_index(rank, order):
    return sum(((rank >> bit) & 1) << (len(order) - 1 - k) for k, bit in enumerate(order))


class Weights(NamedTuple):
    query_self: object
    key_self: object
    value_self: object
    output_self: object
    query_cross: object
    key_cross: object
    value_cross: object
    output_cross: object
    hidden_in: object
    hidden_out: object


def layer_kernel(cfg, names, *refs):
    a = SimpleNamespace(**dict(zip(names, refs, strict=True)))
    seq, enc_len, slots, width = cfg.seq, cfg.enc_len, cfg.slots, cfg.width
    heads, levels, in_kernel = cfg.heads, cfg.levels, cfg.in_kernel
    inner = heads * HD
    if in_kernel:
        a.lands = [getattr(a, "land%d" % i) for i in range(levels)]
        a.holds = [getattr(a, "hold%d" % i) for i in range(levels - 1)]
    chunks = slots // CHUNK_SLOTS
    chunk_rows = CHUNK_SLOTS * seq
    half_rows = chunk_rows // 2
    half_width = width // 2
    quarter_width = width // 4
    me = lax.axis_index("tensor")
    core = lax.rem(me, 2)
    y = me // 2
    dp_me = lax.axis_index("dp")
    c_peer, y_peer = tensor_peer(1), tensor_peer(2)

    def rows_of(k, count):
        return pl.ds(pl.multiple_of(k * count, count), count)

    def load(index, src, dst):
        return pltpu.make_async_copy(src, dst, a.load_sem.at[index])

    inner_rows = slice(0, inner), slice(inner, 2 * inner)
    first_rows, later_rows = pl.ds(0, chunk_rows), pl.ds(chunk_rows, slots * seq - chunk_rows)
    load_x = load(0, a.inputs.at[first_rows], a.x.at[first_rows])
    load_more = load(2 + len(Weights._fields), a.inputs.at[later_rows], a.x.at[later_rows])
    load_g = load(1, a.out_grad, a.g3)
    spots = {name: getattr(a, "w_" + name) for name in Weights._fields if hasattr(a, "w_" + name)}
    spots.update(key_cross=a.w_kv.at[inner_rows[0]], value_cross=a.w_kv.at[inner_rows[1]])
    loads = Weights(
        *(load(2 + i, getattr(a, name), spots[name]) for i, name in enumerate(Weights._fields))
    )
    loads.key_cross.start()
    loads.value_cross.start()
    load_x.start()
    for copy in loads[:4]:
        copy.start()
    load_more.start()

    barrier = pltpu.get_barrier_semaphore()
    peers = [c_peer, y_peer] + [dp_peer(1 << k) for k in range(levels)]
    for peer in peers:
        pl.semaphore_signal(barrier, inc=1, device_id=peer, device_id_type=MESH)

    def remote(src, dst, sems, index, peer):
        return pltpu.make_async_remote_copy(
            src_ref=src,
            dst_ref=dst,
            send_sem=sems.at[(0,) + index],
            recv_sem=sems.at[(1,) + index],
            device_id=peer,
            device_id_type=MESH,
        )

    def peer_weights():
        own, theirs = pl.ds(0, 2 * inner), pl.ds(2 * inner, 2 * inner)
        return remote(a.w_kv.at[own], a.w_kv.at[theirs], a.kv_sem, (0,), y_peer)

    def enc_copy(slot, buffer):
        rows = pl.ds(pl.multiple_of(slot * enc_len, enc_len), enc_len)
        target = a.enc.at[rows_of(buffer, enc_len)]
        return pltpu.make_async_copy(a.encoded.at[rows], target, a.enc_sem.at[buffer])

    enc_copy(0, 0).start()
    for copy in (loads.query_cross, loads.output_cross, loads.hidden_in, loads.hidden_out, load_g):
        copy.start()

    loads.key_cross.wait()
    loads.value_cross.wait()
    pl.semaphore_wait(barrier, len(peers))
    peer_weights().start()

    gain_self, gain_cross, gain_ffn = (
        ref[...].reshape(1, width) for ref in (a.gain_self, a.gain_cross, a.gain_ffn)
    )

    lane = lax.broadcasted_iota(jnp.int32, (1, inner), 1)
    masks = [jnp.where(lane // HD == h, 1.0, 0.0).astype(wide) for h in range(heads)]
    masks_low = [m.astype(low) for m in masks]
    row_i = lax.broadcasted_iota(jnp.int32, (seq, seq), 0)
    col_i = lax.broadcasted_iota(jnp.int32, (seq, seq), 1)
    bucket = lax.broadcasted_iota(jnp.int32, (a.table_in.shape[1], seq), 0)
    chosen = jnp.where(a.buckets[...] == bucket, 1.0, 0.0).astype(wide)
    per_dist = exact_dot(a.table_in[...], chosen)
    backward = jnp.where((row_i + col_i) % seq == 0, 1.0, 0.0).astype(wide)
    lines = exact_dot(per_dist, backward)
    for h in range(heads):
        line = jnp.broadcast_to(lines[h : h + 1, :], (seq, seq))
        turned = pltpu.roll(line, 0, 1, stride=1, stride_axis=0)
        a.bias[h * seq : (h + 1) * seq, :] = jnp.where(row_i >= col_i, turned, masked_score)
    a.table[...] = jnp.zeros_like(a.table)
    a.small[...] = jnp.zeros_like(a.small)

    def stack(rows):
        return jnp.concatenate([rows * m for m in masks_low], axis=0)

    def unstack(rows):
        return sum(rows[h * seq : (h + 1) * seq] * masks[h] for h in range(heads))

    def softmax(scores):
        peak = jnp.max(scores, axis=-1, keepdims=True)
        terms = jnp.exp(scores - peak)
        return (terms / jnp.sum(terms, axis=-1, keepdims=True)).astype(low)

    def own_rows(k):
        return pl.ds(pl.multiple_of(k * chunk_rows + core * half_rows, half_rows), half_rows)

    def other_rows(k):
        return pl.ds(pl.multiple_of(k * chunk_rows + (1 - core) * half_rows, half_rows), half_rows)

    def add_gain(index, value):
        a.small[index : index + 1, :] += value

    def near_copy(p, k):
        return remote(a.part.at[other_rows(k)], a.near.at[k], a.near_sem, (p, k), c_peer)

    main_rows = pl.ds(0, MAIN_ROWS)

    def pack_tail(rows):
        tail = rows[MAIN_ROWS : MAIN_ROWS + TAIL_ROWS]
        lanes = TILE[1]
        parts = [
            tail[r : r + 1, c * lanes : (c + 1) * lanes]
            for r in range(TAIL_ROWS)
            for c in range(rows.shape[1] // lanes)
        ]
        parts.append(jnp.zeros((TILE[0] - len(parts), lanes), wide))
        return jnp.concatenate(parts, axis=0).astype(low)

    def unpack_rows(main, tile, columns):
        tile = tile.astype(wide)
        each = columns // TILE[1]
        rest = half_rows - MAIN_ROWS
        spot = lax.broadcasted_iota(jnp.int32, (rest, columns), 0)
        block = jnp.zeros((rest, columns), wide)
        for r in range(TAIL_ROWS):
            line = jnp.concatenate(
                [tile[r * each + c : r * each + c + 1] for c in range(each)], axis=1
            )
            block = jnp.where(spot == r, jnp.broadcast_to(line, (rest, columns)), block)
        return jnp.concatenate([main.astype(wide), block], axis=0)

    def far_copies(p, k):
        return (
            remote(
                a.mine.at[k, main_rows], a.far.at[p % 2, k, main_rows], a.far_sem, (p, k), y_peer
            ),
            remote(a.tail_send.at[k], a.tail_far.at[p % 2, k], a.tail_sem, (p, k), y_peer),
        )

    def y_send(p, k):
        near_copy(p, k).wait()
        term = a.part[own_rows(k)].astype(wide) + a.near[k].astype(wide)
        a.mine[k] = term.astype(low)
        a.tail_send[k] = pack_tail(term)
        for copy in far_copies(p, k):
            copy.start()

    def last_copies(k):
        return (
            remote(
                a.mine.at[k, main_rows, pl.ds(0, half_width)],
                a.far.at[0, k, main_rows, pl.ds(0, half_width)],
                a.far_sem,
                (4, k),
                y_peer,
            ),
            remote(a.tail_send.at[k], a.tail_far.at[0, k], a.tail_sem, (4, k), y_peer),
            remote(a.inner_send.at[k], a.inner_far.at[k], a.inner_sem, (k,), y_peer),
        )

    def y_send_last(k):
        near_copy(4, k).wait()
        term = a.part[own_rows(k)].astype(wide) + a.near[k].astype(wide)
        a.h1[k] = term
        rows = a.x[own_rows(k)].astype(wide)
        product = term * rows
        row_inner = jnp.sum(product * gain_self, axis=-1, keepdims=True)
        add_gain(0, jnp.sum(product * inverse_rms(rows), axis=0, keepdims=True))
        a.inner_send[k] = jnp.broadcast_to(row_inner, (half_rows, half_rows)).T[:8]
        away = jnp.where(y == 0, term[:, half_width:], term[:, :half_width])
        a.mine[k, :, :half_width] = away.astype(low)
        a.tail_send[k] = pack_tail(away)
        for copy in last_copies(k):
            copy.start()

    def total(p, k):
        for copy in far_copies(p, k):
            copy.wait()
        far = unpack_rows(a.far[p % 2, k, :MAIN_ROWS], a.tail_far[p % 2, k], width)
        return a.mine[k].astype(wide) + far

    def share_copy(p, k, buffer):
        return remote(buffer.at[own_rows(k)], buffer.at[own_rows(k)], a.share_sem, (p, k), c_peer)

    def each_chunk(body):
        def step(k, carry):
            body(k)
            return carry

        lax.fori_loop(0, chunks, step, 0)

    def phase(p, finish, buffer, compute, extra=None, send=None):
        send = send or functools.partial(y_send, p)

        def begin(k):
            finish(k, total(p - 1, k))
            share_copy(p, k, buffer).start()

        def body(k):
            share_copy(p, k, buffer).wait()

            @pl.when(k + 1 < chunks)
            def _():
                begin(k + 1)

            compute(k)
            near_copy(p, k).start()

            @pl.when(k > 0)
            def _():
                send(k - 1)

            if extra is not None:
                extra(k)

        begin(0)
        each_chunk(body)
        send(chunks - 1)

    def project(slot, buffer):
        enc_copy(slot, buffer).wait()

        @pl.when(slot + 1 < slots)
        def _():
            enc_copy(slot + 1, 1 - buffer).start()

        rows = rows_of(slot, enc_len)
        a.k2[rows] = dot_t(a.enc[rows_of(buffer, enc_len)], a.w_kv[:inner]).astype(low)
        a.v2[rows] = dot_t(a.enc[rows_of(buffer, enc_len)], a.w_kv[inner : 2 * inner]).astype(low)

    def self_forward(k):
        rows = rows_of(k, chunk_rows)
        x = a.x[rows].astype(wide)
        normed = (x * inverse_rms(x) * gain_self).astype(low)
        a.n1[rows] = normed
        query = dot_t(normed, a.w_query_self[...]).astype(low)
        keys = dot_t(normed, a.w_key_self[...]).astype(low)
        values = dot_t(normed, a.w_value_self[...]).astype(low)
        a.q1[rows], a.k1[rows], a.v1[rows] = query, keys, values
        parts = [slice(s * seq, (s + 1) * seq) for s in range(CHUNK_SLOTS)]
        scores = [dot_t(stack(query[part]), keys[part]) + a.bias[...] for part in parts]
        weights = [softmax(score) for score in scores]
        mixed = []
        for s, part in enumerate(parts):
            a.soft1[k * CHUNK_SLOTS + s] = weights[s]
            mixed.append(unstack(dot(weights[s], values[part])).astype(low))
        mixed = jnp.concatenate(mixed, axis=0)
        a.o1[rows] = mixed
        a.part[rows] = dot(mixed, a.w_output_self[...]).astype(low)

    load_x.wait()
    for copy in loads[:4]:
        copy.wait()

    def phase_zero(k):
        @pl.when(k == 1)
        def _():
            load_more.wait()

        self_forward(k)
        near_copy(0, k).start()
        y_send(0, k)
        project(CHUNK_SLOTS * k, 0)
        project(CHUNK_SLOTS * k + 1, 1)

    each_chunk(phase_zero)
    loads.query_cross.wait()
    loads.output_cross.wait()
    peer_weights().wait()

    chip_slots = slots // 2

    def chip_slot(k):
        return chip_slots * y + k

    enc_copy(chip_slot(0), 0).start()

    def project_peer(k):
        buffer = lax.rem(k, 2)
        enc_copy(chip_slot(k), buffer).wait()

        @pl.when(k + 1 < chip_slots)
        def _():
            enc_copy(chip_slot(k + 1), 1 - buffer).start()

        rows = rows_of(k, enc_len)
        encoded = a.enc[rows_of(buffer, enc_len)]
        a.k2_peer[rows] = dot_t(encoded, a.w_kv[2 * inner : 3 * inner]).astype(low)
        a.v2_peer[rows] = dot_t(encoded, a.w_kv[3 * inner :]).astype(low)

    def finish_one(k, term):
        hidden = a.x[own_rows(k)].astype(wide) + term
        a.h1[k] = hidden
        a.n2[own_rows(k)] = (hidden * inverse_rms(hidden) * gain_cross).astype(low)

    def cross_forward(k):
        rows = rows_of(k, chunk_rows)
        query = dot_t(a.n2[rows], a.w_query_cross[...]).astype(low)
        a.q2[rows] = query
        slots_here = [k * CHUNK_SLOTS + s for s in range(CHUNK_SLOTS)]
        enc_parts = [rows_of(slot, enc_len) for slot in slots_here]
        scores = [
            dot_t(stack(query[s * seq : (s + 1) * seq]), a.k2[enc_rows])
            for s, enc_rows in enumerate(enc_parts)
        ]
        weights = [softmax(score) for score in scores]
        mixed = []
        for s, slot in enumerate(slots_here):
            a.soft2[slot] = weights[s]
            mixed.append(unstack(dot(weights[s], a.v2[enc_parts[s]])).astype(low))
        mixed = jnp.concatenate(mixed, axis=0)
        a.o2[rows] = mixed
        a.part[rows] = dot(mixed, a.w_output_cross[...]).astype(low)

    phase(1, finish_one, a.n2, cross_forward, project_peer)
    for copy in (loads.hidden_in, loads.hidden_out, load_g):
        copy.wait()

    def limit(slot):
        return jnp.where(slot < a.counts[0], a.lengths[slot], 0)

    def keep_rows(slot, rows):
        pos = lax.broadcasted_iota(jnp.int32, (seq, 1), 0)
        return jnp.where(pos < limit(slot), rows, 0.0)

    def finish_two(k, term):
        hidden = a.h1[k] + term
        a.h2[k] = hidden
        a.n3[own_rows(k)] = (hidden * inverse_rms(hidden) * gain_ffn).astype(low)

    def out_near_copy(k):
        return remote(a.out_part.at[k % 2, 1 - core], a.out_near.at[k], a.out_near_sem, (k,), c_peer)

    def out_far_copies(k):
        return (
            remote(
                a.out_mine.at[k, main_rows],
                a.out_far.at[k, main_rows],
                a.out_far_sem,
                (0, k),
                y_peer,
            ),
            remote(a.out_tail_send.at[k], a.out_tail_far.at[k], a.out_far_sem, (1, k), y_peer),
        )

    def my_half(value):
        return jnp.where(y == 0, value[:, :half_width], value[:, half_width:])

    def other_half(value):
        return jnp.where(y == 0, value[:, half_width:], value[:, :half_width])

    def out_gather(k):
        out_near_copy(k).wait()
        term = a.out_part[k % 2, core].astype(wide) + a.out_near[k].astype(wide)
        away = other_half(term)
        a.out_mine[k] = away.astype(low)
        a.out_tail_send[k] = pack_tail(away)
        a.out_keep[k] = my_half(term) + my_half(a.h2[k])

    scale = 0.7978845608028654

    def feed_forward(k):
        rows = rows_of(k, chunk_rows)
        grad = jnp.concatenate(
            [
                keep_rows(k * CHUNK_SLOTS + s, a.g3[rows_of(k * CHUNK_SLOTS + s, seq)].astype(wide))
                for s in range(CHUNK_SLOTS)
            ],
            axis=0,
        ).astype(low)
        a.g3[rows] = grad
        a.pre[...] = dot(a.n3[rows], a.w_hidden_in[...])

        def gelu_rows(i, carry):
            part = rows_of(i, GELU_ROWS)
            pre = a.pre[part]
            square = pre * pre
            bend = jnp.tanh(scale * pre * (1.0 + 0.044715 * square))
            half = 0.5 * (1.0 + bend)
            curve = scale * (1.0 + 3 * 0.044715 * square)
            a.pre[part] = half + 0.5 * pre * (1.0 - bend * bend) * curve
            target = pl.ds(pl.multiple_of(k * chunk_rows + i * GELU_ROWS, GELU_ROWS), GELU_ROWS)
            a.act[target] = (pre * half).astype(low)
            return carry

        lax.fori_loop(0, chunk_rows // GELU_ROWS, gelu_rows, 0)
        out = dot_t(a.act[rows], a.w_hidden_out[...]).astype(low)
        a.out_part[k % 2, 0] = out[:half_rows]
        a.out_part[k % 2, 1] = out[half_rows:]
        out_near_copy(k).start()
        grad_pre = (a.pre[...] * dot(grad, a.w_hidden_out[...])).astype(low)
        a.d_pre[rows] = grad_pre
        a.part[rows] = dot_t(grad_pre, a.w_hidden_in[...]).astype(low)

    phase(2, finish_two, a.n3, feed_forward, out_gather)

    def column_copy(which, k):
        return remote(
            a.col_send.at[which, k],
            a.columns.at[which, :, own_rows(k)],
            a.col_sem,
            (which, k),
            c_peer,
        )

    def emit_columns(which, k, value):
        value = value.T
        left, right = value[:quarter_width], value[quarter_width:]
        first = core == 0
        a.columns[which, :, own_rows(k)] = jnp.where(first, left, right).astype(low)
        a.col_send[which, k] = jnp.where(first, right, left).astype(low)
        column_copy(which, k).start()

    def finish_out(k):
        for copy in out_far_copies(k):
            copy.wait()
        far = unpack_rows(a.out_far[k, :MAIN_ROWS], a.out_tail_far[k], half_width)
        value = a.out_keep[k] + far
        emit_columns(0, k, keep_rows(k * CHUNK_SLOTS + core, value))

    orders = (tuple(range(levels)), (1, 0) + tuple(range(2, levels)))

    def dp_rank(half, level):
        return (dp_me >> orders[half][level]) & 1

    def dp_copy(block, half, level):
        buffer = block % 2
        count = 1 << (levels - 1 - level)
        source = a.term if level == 0 else a.holds[level - 1]
        part = pl.ds((1 - dp_rank(half, level)) * count, count)
        return remote(
            source.at[buffer, half, part],
            a.lands[level].at[buffer, half],
            a.dp_sem,
            (block, half, level),
            dp_peer(1 << orders[half][level]),
        )

    def raw_copy(block):
        return pltpu.make_async_copy(
            a.term.at[block % 2], a.raw_grads.at[block], a.dp_sem.at[0, block, 0, 0]
        )

    def credit_wait(block, half, level):
        pl.semaphore_wait(a.credit_sem.at[block % 2, half, level], 1)

    def dp_begin(block, halves=(0, 1)):
        if in_kernel:
            for half in halves:
                if block >= 2:
                    credit_wait(block, half, 0)
                dp_copy(block, half, 0).start()
        elif 1 in halves:
            raw_copy(block).start()

    def dp_advance(block, level, halves=(0, 1)):
        if not in_kernel:
            return
        buffer = block % 2
        count = 1 << (levels - 1 - level)
        for half in halves:
            dp_copy(block, half, level).wait()
            source = a.term if level == 0 else a.holds[level - 1]
            part = pl.ds(dp_rank(half, level) * count, count)
            value = source[buffer, half, part].astype(wide)
            value += a.lands[level][buffer, half].astype(wide)
            if level == levels - 1:
                emit_grads(block, half, value[0])
            else:
                a.holds[level][buffer, half] = value.astype(low)
            if block < 2:
                pl.semaphore_signal(
                    a.credit_sem.at[buffer, half, level],
                    inc=1,
                    device_id=dp_peer(1 << orders[half][level]),
                    device_id_type=MESH,
                )
            if level + 1 < levels:
                if block >= 2:
                    credit_wait(block, half, level + 1)
                dp_copy(block, half, level + 1).start()

    def at_chunk(k, step, *moves):
        @pl.when(k == step)
        def _():
            for move in moves:
                dp_advance(*move)

    def dp_finish_raw(block):
        if not in_kernel:
            raw_copy(block).wait()

    def grad_store(index):
        if index < 8:
            source, target = a.held.at[index], getattr(a, "grad_" + Weights._fields[index])
        else:
            block, half = divmod(index - 8, 2)
            source = a.held_wide.at[block, half]
            target = (a.grad_hidden_out, a.grad_hidden_in)[block]
            target = target.at[:, pl.ds(half * half_width, half_width)]
        return pltpu.make_async_copy(source, target, a.grad_sem.at[index])

    def emit_grads(block, half, value):
        if block < 2:
            a.held_wide[block, half] = value
            grad_store(8 + 2 * block + half).start()
        else:
            start = (4 if block == 2 else 0) + 2 * half
            for i in range(2):
                a.held[start + i] = value[:, i * inner : (i + 1) * inner]
                grad_store(start + i).start()

    piece = cfg.piece
    groups = 2
    group_rows = width // groups
    pieces_each = max(group_rows // piece, 1) if in_kernel else 1

    def store_pieces(block, g, rows):
        if in_kernel:
            for i in range(pieces_each):
                for gg in range(groups):
                    if gg != g:
                        continue
                    for half in range(2):
                        index = piece_index(gg * pieces_each + i, orders[half])
                        a.term[block % 2, half, index] = rows[
                            i * piece : (i + 1) * piece,
                            half * half_width : (half + 1) * half_width,
                        ]
        else:
            a.term[block % 2, g * group_rows : (g + 1) * group_rows] = rows

    def plain_grads(block, left, right):
        for g in range(groups):
            columns = slice(g * group_rows, (g + 1) * group_rows)
            store_pieces(block, g, t_dot(left[:, columns], right[...]).astype(low))

    def turned_grads(block, half):
        value = a.enc[half * 2 * inner : (half + 1) * 2 * inner].T
        columns = slice(half * half_width, (half + 1) * half_width)
        if in_kernel:
            for i in range(width // piece):
                index = piece_index(i, orders[half])
                a.term[block % 2, half, index] = value[i * piece : (i + 1) * piece]
        else:
            a.term[block % 2, :, columns] = value

    def turned_rows(i):
        return slice(i * inner, (i + 1) * inner)

    plain_grads(0, a.g3, a.act)
    dp_begin(0)
    plain_grads(1, a.n3, a.d_pre)
    dp_begin(1)

    def finish_three(k, term):
        grad_rows, grad_gain = norm_back(a.h2[k], gain_ffn, term)
        add_gain(2, grad_gain)
        grad = a.g3[own_rows(k)].astype(wide) + grad_rows
        a.dh[k] = grad
        a.dh2[own_rows(k)] = grad.astype(low)

    def inner_by_head(grad_mixed, mixed):
        product = grad_mixed.astype(wide) * mixed.astype(wide)
        return [jnp.sum(product * m, axis=-1, keepdims=True) for m in masks]

    def score_back(soft, grad_soft, row_inner):
        return (soft.astype(wide) * (grad_soft - row_inner)).astype(low)

    def cross_backward(k):
        rows = rows_of(k, chunk_rows)
        grad_mixed = dot_t(a.dh2[rows], a.w_output_cross[...]).astype(low)
        inners = inner_by_head(grad_mixed, a.o2[rows])
        a.pair[rows, inner:] = grad_mixed
        a.pair[rows, :inner] = a.q2[rows]
        query = a.q2[rows]
        parts = [slice(s * seq, (s + 1) * seq) for s in range(CHUNK_SLOTS)]
        slots_here = [k * CHUNK_SLOTS + s for s in range(CHUNK_SLOTS)]
        enc_parts = [rows_of(slot, enc_len) for slot in slots_here]
        tall_grads = [stack(grad_mixed[part]) for part in parts]
        tall_queries = [stack(query[part]) for part in parts]
        grad_softs = [dot_t(tall_grads[s], a.v2[enc_parts[s]]) for s in range(CHUNK_SLOTS)]
        softs = [a.soft2[slot] for slot in slots_here]
        grad_scores = [
            score_back(
                softs[s],
                grad_softs[s],
                jnp.concatenate([column[part] for column in inners], axis=0),
            )
            for s, part in enumerate(parts)
        ]
        grads = [
            unstack(dot(grad_scores[s], a.k2[enc_parts[s]])).astype(low) for s in range(CHUNK_SLOTS)
        ]
        for s, slot in enumerate(slots_here):
            a.dkv[slot, :inner] = t_dot(tall_queries[s], grad_scores[s]).astype(low)
            a.dkv[slot, inner:] = t_dot(tall_grads[s], softs[s]).astype(low)
        grads = jnp.concatenate(grads, axis=0)
        a.d_pre[rows, :inner] = grads
        a.part[rows] = dot(grads, a.w_query_cross[...]).astype(low)

    kv_blocks = 2 * inner // half_rows
    a.pre[...] = jnp.zeros_like(a.pre)

    def kv_part(i):
        if i == kv_blocks - 1:
            return a.h2.at[0]
        return a.pre.at[slice(i * half_rows, (i + 1) * half_rows)]

    def add_kv(slot, buffer):
        value = dot(a.dkv[slot], a.enc[rows_of(buffer, enc_len)])
        for i in range(kv_blocks):
            kv_part(i)[...] += value[i * half_rows : (i + 1) * half_rows]

    def kv_chunk(k):
        @pl.when(k == 0)
        def _():
            a.h2[0] = jnp.zeros_like(a.h2[0])

        for i in range(2):
            enc_copy(2 * k + i, i).wait()
            add_kv(2 * k + i, i)

            @pl.when(k + 1 < chunks)
            def _():
                enc_copy(2 * k + 2 + i, i).start()

        at_chunk(k, 2, (0, 0))
        at_chunk(k, 3, (1, 0))

    enc_copy(0, 0).start()
    enc_copy(1, 1).start()
    phase(3, finish_three, a.dh2, cross_backward, kv_chunk)

    peer_copy = remote(
        a.pair.at[rows_of(1 - y, chip_slots * seq)], a.pair_peer, a.peer_sem, (0,), y_peer
    )
    peer_copy.start()
    a.enc[turned_rows(0)] = t_dot(a.d_pre[:, :inner], a.n2[...]).astype(low)
    for i in range(kv_blocks):
        a.enc[inner + i * half_rows : inner + (i + 1) * half_rows] = kv_part(i)[...].astype(low)
    a.enc[turned_rows(3)] = t_dot(a.o2[...], a.dh2[...]).astype(low)
    dp_finish_raw(0)
    for half in range(2):
        turned_grads(2, half)
    dp_advance(0, 1)
    dp_begin(2)

    def finish_four(k, term):
        grad_rows, grad_gain = norm_back(a.h1[k], gain_cross, term)
        add_gain(1, grad_gain)
        grad = a.dh[k] + grad_rows
        a.dh[k] = grad
        a.dh1[own_rows(k)] = grad.astype(low)

    def self_backward(k):
        rows = rows_of(k, chunk_rows)
        grad_mixed = dot_t(a.dh1[rows], a.w_output_self[...]).astype(low)
        inners = inner_by_head(grad_mixed, a.o1[rows])
        query, keys, values = a.q1[rows], a.k1[rows], a.v1[rows]
        parts = [slice(s * seq, (s + 1) * seq) for s in range(CHUNK_SLOTS)]
        tall_grads = [stack(grad_mixed[part]) for part in parts]
        tall_queries = [stack(query[part]) for part in parts]
        softs = [a.soft1[k * CHUNK_SLOTS + s] for s in range(CHUNK_SLOTS)]
        grad_softs = [dot_t(tall_grads[s], values[part]) for s, part in enumerate(parts)]
        grad_scores = [
            score_back(
                softs[s],
                grad_softs[s],
                jnp.concatenate([column[part] for column in inners], axis=0),
            )
            for s, part in enumerate(parts)
        ]
        a.table[...] += sum(g.astype(wide) for g in grad_scores)
        grads = [
            [unstack(dot(grad_scores[s], keys[part])).astype(low) for s, part in enumerate(parts)],
            [t_dot(g, q).astype(low) for g, q in zip(grad_scores, tall_queries, strict=True)],
            [t_dot(w, g).astype(low) for w, g in zip(softs, tall_grads, strict=True)],
        ]
        grads = [jnp.concatenate(g, axis=0) for g in grads]
        a.q1[rows], a.k1[rows], a.v1[rows] = grads
        a.part[rows] = (
            dot(grads[0], a.w_query_self[...])
            + dot(grads[1], a.w_key_self[...])
            + dot(grads[2], a.w_value_self[...])
        ).astype(low)

    def self_moves(k):
        at_chunk(k, 1, (1, 1))
        at_chunk(k, 2, (0, 2))
        at_chunk(k, 3, (2, 0))

    phase(4, finish_four, a.dh1, self_backward, self_moves, y_send_last)
    for k in range(chunks):
        for copy in out_far_copies(k):
            copy.start()
    mirror = jnp.where(row_i + col_i == seq - 1, 1.0, 0.0).astype(wide)
    for h in range(heads):
        flipped = exact_dot(a.table[h * seq : (h + 1) * seq, :], mirror)
        turned = pltpu.roll(flipped, 0, 1, stride=1, stride_axis=0)
        a.small[3:4, h * seq : (h + 1) * seq] = jnp.sum(turned, axis=0, keepdims=True)

    hops = [dp_peer(1 << k) for k in range(levels)] + [c_peer, y_peer]
    row = lax.broadcasted_iota(jnp.int32, a.small.shape, 0)

    def small_copy(i):
        return remote(a.small, a.small_land.at[i], a.small_sem, (i,), hops[i])

    def small_step(i):
        small_copy(i).wait()
        summed = row < (8 if i < levels else 3 if i == levels else 1)
        a.small[...] += jnp.where(summed, a.small_land[i], 0.0)
        if i < levels + 1:
            small_copy(i + 1).start()

    small_copy(0).start()
    a.enc[turned_rows(0)] = t_dot(a.q1[...], a.n1[...]).astype(low)
    a.enc[turned_rows(1)] = t_dot(a.k1[...], a.n1[...]).astype(low)
    dp_finish_raw(1)
    turned_grads(3, 0)
    dp_begin(3, (0,))
    a.enc[turned_rows(2)] = t_dot(a.v1[...], a.n1[...]).astype(low)
    a.enc[turned_rows(3)] = t_dot(a.o1[...], a.dh1[...]).astype(low)
    turned_grads(3, 1)
    dp_begin(3, (1,))
    small_step(0)
    dp_advance(2, 1)
    peer_copy.wait()

    def enc_partial(k):
        rows = rows_of(k, seq)
        enc_rows = rows_of(k, enc_len)
        pair = a.pair_peer[rows]
        tall_query, tall_grad = stack(pair[:, :inner]), stack(pair[:, inner:])
        soft = softmax(dot_t(tall_query, a.k2_peer[enc_rows]))
        grad_soft = dot_t(tall_grad, a.v2_peer[enc_rows])
        row_inner = jnp.sum(soft.astype(wide) * grad_soft, axis=-1, keepdims=True)
        grad_scores = score_back(soft, grad_soft, row_inner)
        peer_grads = jnp.concatenate(
            [t_dot(tall_query, grad_scores).astype(low), t_dot(tall_grad, soft).astype(low)], axis=0
        )
        own = t_dot(a.dkv[chip_slot(k)], a.w_kv[: 2 * inner])
        return own + t_dot(peer_grads, a.w_kv[2 * inner :])

    enc_each = chip_slots // 2

    def enc_near_copy(j):
        rows = rows_of(j, enc_len)
        return remote(a.n3.at[rows], a.act.at[rows], a.enc_near_sem, (j,), c_peer)

    def enc_give(j, carry):
        at_chunk(j, 1, (1, 2), (3, 0, (0,)))
        a.n3[rows_of(j, enc_len)] = enc_partial((1 - core) * enc_each + j).astype(low)
        enc_near_copy(j).start()
        return carry

    def enc_keep(j, carry):
        at_chunk(j, 1, (3, 1, (0,)))
        partial = enc_partial(core * enc_each + j)
        enc_near_copy(j).wait()
        rows = rows_of(j, enc_len)
        a.d_pre[rows] = (partial + a.act[rows].astype(wide)).astype(low)
        return carry

    lax.fori_loop(0, enc_each, enc_give, 0)
    dp_advance(3, 0, (1,))
    small_step(1)
    lax.fori_loop(0, enc_each, enc_keep, 0)
    dp_advance(3, 1, (1,))
    for i in range(2, levels):
        small_step(i)
    store_enc = load(2, a.d_pre, a.encoded_grad)
    store_enc.start()

    def phase_five(k):
        for copy in last_copies(k):
            copy.wait()
        rows = my_half(a.x[own_rows(k)]).astype(wide)
        inverse = inverse_rms(a.x[own_rows(k)].astype(wide))
        sums = (a.inner_send[k] + a.inner_far[k])[:1]
        row_inner = jnp.broadcast_to(sums, (half_rows, half_rows)).T[:, :1] * (1.0 / width)
        far = unpack_rows(a.far[0, k, :MAIN_ROWS, :half_width], a.tail_far[0, k], half_width)
        term = my_half(a.h1[k]) + far
        grad_rows = inverse * my_half(gain_self) * term
        grad_rows -= rows * (inverse * inverse * inverse) * row_inner
        emit_columns(1, k, my_half(a.dh[k]) + grad_rows)

    each_chunk(phase_five)
    dp_advance(2, 2)
    small_step(levels)
    each_chunk(finish_out)
    for k in range(chunks):
        column_copy(0, k).wait()
        column_copy(1, k).wait()
    stores = [
        load(0, a.columns.at[0], a.layer_out),
        load(1, a.columns.at[1], a.input_grad),
    ]
    for store in stores:
        store.start()
    dp_advance(3, 2)
    small_step(levels + 1)
    dp_finish_raw(2)
    dp_finish_raw(3)
    a.small_out[...] = a.small[...]
    for store in (*stores, store_enc):
        store.wait()
    if in_kernel:
        for index in range(12):
            grad_store(index).wait()


def finish_kernel(count, heads, seq, *refs):
    small, buckets = refs[count], refs[count + 1]
    targets, held, sems = refs[count + 2 : 2 * count + 6], refs[2 * count + 6 : -1], refs[-1]
    parts = []
    for i in range(count):
        cuts = 1
        rows = refs[i].shape[0] // cuts
        parts += [(i, pl.ds(c * rows, rows)) for c in range(cuts)]
    copies = [
        pltpu.make_async_copy(refs[i].at[rows], held[i].at[rows], sems.at[n])
        for n, (i, rows) in enumerate(parts)
    ]
    for copy in copies:
        copy.start()
    for n, (i, rows) in enumerate(parts):
        copies[n].wait()
        copies[n] = pltpu.make_async_copy(held[i].at[rows], targets[i].at[rows], sems.at[n])
        copies[n].start()
    for i in range(3):
        targets[count + i][...] = small[i, :]
    sums = jnp.concatenate([small[3:4, h * seq : (h + 1) * seq] for h in range(heads)], axis=0)
    by_lane = pltpu.roll(jnp.broadcast_to(buckets[...], (8, seq)), seq - 1, 1)[:1]
    kinds = targets[count + 3].shape[1]
    bucket = lax.broadcasted_iota(jnp.int32, (kinds, seq), 0)
    chosen = jnp.where(by_lane == bucket, 1.0, 0.0).astype(wide)
    targets[count + 3][...] = lax.dot_general(
        sums,
        chosen,
        (((1,), (1,)), ((), ())),
        precision=highest,
        preferred_element_type=wide,
    )
    for copy in copies:
        copy.wait()


def per_device(*args):
    (
        inputs,
        encoded,
        example_counts,
        lengths,
        buckets,
        gain_self,
        gain_cross,
        gain_ffn,
        bias_table,
    ) = args[:9]
    weights = args[9:19]
    out_grad = args[19]
    rows, width = inputs.shape
    seq = buckets.shape[0]
    slots = lengths.shape[0]
    enc_rows = encoded.shape[0]
    enc_len = enc_rows // slots
    inner = weights[0].shape[1]
    hidden = weights[8].shape[1]
    heads = inner // HD
    dp_count = lax.axis_size("dp")
    levels = dp_count.bit_length() - 1
    piece = width // dp_count
    in_kernel = piece % 16 == 0
    chunks = slots // CHUNK_SLOTS
    half = CHUNK_SLOTS * seq // 2

    ins = dict(
        lengths=(lengths, SM),
        counts=(example_counts, SM),
        gain_self=(gain_self, VM),
        gain_cross=(gain_cross, VM),
        gain_ffn=(gain_ffn, VM),
        table_in=(bias_table.T, VM),
        buckets=(buckets[None], VM),
        inputs=(inputs, HBM),
        encoded=(encoded, HBM),
        out_grad=(out_grad, HBM),
    )
    for name, weight in zip(Weights._fields, weights, strict=True):
        ins[name] = (weight, HBM)
    for name in Weights._fields[:8]:
        ins[name] = (ins[name][0].T, HBM)
    shape = jax.ShapeDtypeStruct
    outs = dict(
        layer_out=(shape((width // 4, rows), low), HBM),
        input_grad=(shape((width // 4, rows), low), HBM),
        encoded_grad=(shape((enc_rows // 4, width), low), HBM),
        small_out=(shape((8, width), wide), VM),
    )
    if in_kernel:
        for name, weight in zip(Weights._fields, weights, strict=True):
            outs["grad_" + name] = (shape((piece, weight.shape[1]), wide), HBM)
    else:
        outs.update(raw_grads=(shape((4, width, width), low), HBM))
    vmem, dma = pltpu.VMEM, pltpu.SemaphoreType.DMA
    quarter = width // 4
    whole_rows = vmem((rows, width), low)
    hidden_rows = vmem((rows, hidden), low)
    inner_rows = vmem((rows, inner), low)
    own_wide = vmem((chunks, half, width), wide)
    own_low = vmem((chunks, half, width), low)
    scratch = {
        "w_" + name: vmem(ins[name][0].shape, low)
        for name in Weights._fields
        if name not in Weights._fields[5:7]
    }
    scratch.update(
        x=whole_rows,
        g3=whole_rows,
        enc=vmem((2 * enc_len, width), low),
        n1=whole_rows,
        n2=whole_rows,
        n3=whole_rows,
        dh1=whole_rows,
        dh2=whole_rows,
        part=whole_rows,
        act=hidden_rows,
        d_pre=hidden_rows,
        q1=inner_rows,
        k1=inner_rows,
        v1=inner_rows,
        o1=inner_rows,
        q2=inner_rows,
        o2=inner_rows,
        k2=vmem((enc_rows, inner), low),
        v2=vmem((enc_rows, inner), low),
        h1=own_wide,
        h2=own_wide,
        dh=own_wide,
        soft1=vmem((slots, heads * seq, seq), low),
        soft2=vmem((slots, heads * seq, enc_len), low),
        dkv=vmem((slots, 2 * inner, enc_len), low),
        near=own_low,
        mine=own_low,
        far=vmem((2, chunks, half, width), low),
        out_part=vmem((2, 2, half, width), low),
        out_near=own_low,
        out_mine=vmem((chunks, half, width // 2), low),
        out_keep=vmem((chunks, half, width // 2), wide),
        out_far=vmem((chunks, half, width // 2), low),
        columns=vmem((2, quarter, rows), low),
        col_send=vmem((2, chunks, quarter, half), low),
        w_kv=vmem((4 * inner, width), low),
        k2_peer=vmem((enc_rows // 2, inner), low),
        v2_peer=vmem((enc_rows // 2, inner), low),
        pair=vmem((rows, 2 * inner), low),
        pair_peer=vmem((rows // 2, 2 * inner), low),
        tail_send=vmem((chunks, *TILE), low),
        tail_far=vmem((2, chunks, *TILE), low),
        out_tail_send=vmem((chunks, *TILE), low),
        out_tail_far=vmem((chunks, *TILE), low),
        inner_send=vmem((chunks, 8, half), wide),
        inner_far=vmem((chunks, 8, half), wide),
        pre=vmem((CHUNK_SLOTS * seq, hidden), wide),
        bias=vmem((heads * seq, seq), wide),
        table=vmem((heads * seq, seq), wide),
        small=vmem((8, width), wide),
        small_land=vmem((levels + 2, 8, width), wide),
        load_sem=dma((3 + len(weights),)),
        enc_sem=dma((2,)),
        near_sem=dma((2, 5, chunks)),
        far_sem=dma((2, 5, chunks)),
        share_sem=dma((2, 5, chunks)),
        out_near_sem=dma((2, chunks)),
        out_far_sem=dma((2, 2, chunks)),
        tail_sem=dma((2, 5, chunks)),
        col_sem=dma((2, 2, chunks)),
        enc_near_sem=dma((2, 2)),
        peer_sem=dma((2, 1)),
        kv_sem=dma((2, 1)),
        inner_sem=dma((2, chunks)),
        dp_sem=dma((2, 4, 2, levels)),
        small_sem=dma((2, levels + 2)),
        credit_sem=pltpu.SemaphoreType.REGULAR((2, 2, levels)),
    )
    if in_kernel:
        scratch.update(
            term=vmem((2, 2, dp_count, piece, width // 2), low),
            held=vmem((8, piece, inner), wide),
            held_wide=vmem((2, 2, piece, width // 2), wide),
            grad_sem=dma((12,)),
        )
        for level in range(levels):
            count = 1 << (levels - 1 - level)
            scratch["land%d" % level] = vmem((2, 2, count, piece, width // 2), low)
            if level + 1 < levels:
                scratch["hold%d" % level] = vmem((2, 2, count, piece, width // 2), low)
    else:
        scratch.update(term=vmem((2, width, width), low))
    cfg = SimpleNamespace(
        seq=seq,
        enc_len=enc_len,
        slots=slots,
        width=width,
        heads=heads,
        levels=levels,
        in_kernel=in_kernel,
        piece=piece,
    )
    results = pl.pallas_call(
        functools.partial(layer_kernel, cfg, tuple(ins) + tuple(outs) + tuple(scratch)),
        out_shape=tuple(o[0] for o in outs.values()),
        in_specs=[i[1] for i in ins.values()],
        out_specs=tuple(o[1] for o in outs.values()),
        scratch_shapes=list(scratch.values()),
        compiler_params=pltpu.CompilerParams(
            collective_id=1, has_side_effects=True, vmem_limit_bytes=65000 * 2**10
        ),
    )(*[i[0] for i in ins.values()])
    moved = [i for i, name in enumerate(outs) if name not in ("small_out", "raw_grads")]
    buckets_row = buckets[None]
    kinds = bias_table.shape[0]
    finals = pl.pallas_call(
        functools.partial(finish_kernel, len(moved), heads, seq),
        out_shape=(
            *(shape(results[i].shape, results[i].dtype) for i in moved),
            *(shape((width,), wide) for _ in range(3)),
            shape((heads, kinds), wide),
        ),
        in_specs=[HBM] * len(moved) + [VM, VM],
        out_specs=(HBM,) * len(moved) + (VM,) * 4,
        scratch_shapes=[
            *(vmem(results[i].shape, results[i].dtype) for i in moved),
            dma((4 * len(moved),)),
        ],
    )(*[results[i] for i in moved], results[3], buckets_row)
    if in_kernel:
        grads = finals[3 : len(moved)]
    else:
        raw = results[4]
        parts = [raw[3][:, i * inner : (i + 1) * inner] for i in range(4)]
        parts += [raw[2][:, i * inner : (i + 1) * inner] for i in range(4)]
        grads = [
            lax.psum_scatter(part.astype(wide), "dp", scatter_dimension=0, tiled=True)
            for part in (*parts, raw[1], raw[0])
        ]
    gains = finals[len(moved) : len(moved) + 3]
    return (finals[0].T, finals[1].T, finals[2], *gains, finals[-1].T, *grads)


def solution(mesh):
    columns = P(None, "tensor")
    both = P("dp", "tensor")
    placed = (
        (P("dp", None), P("dp", None), P("dp"), P("dp"), P(), P(), P(), P())
        + (columns,) * 11
        + (P("dp", None),)
    )
    return jax.shard_map(
        per_device,
        mesh=mesh,
        in_specs=placed,
        out_specs=(both, both, P(("dp", "tensor"), None), P(), P(), P(), columns) + (both,) * 10,
        check_vma=False,
    )
```

```python
import functools
from types import SimpleNamespace
from typing import NamedTuple

import jax
import jax.numpy as jnp
from jax import lax
from jax.experimental import pallas as pl
from jax.experimental.pallas import tpu as pltpu
from jax.sharding import PartitionSpec as P

HD = 64
CHUNK_SLOTS = 2
GELU_ROWS = 32
MAIN_ROWS = 112
TAIL_ROWS = 2
TILE = (16, 128)

norm_epsilon = 1e-06
masked_score = -1e30
highest = lax.Precision.HIGHEST
MESH = pl.DeviceIdType.MESH
VM = pl.BlockSpec(memory_space=pltpu.VMEM)
SM = pl.BlockSpec(memory_space=pltpu.SMEM)
HBM = pl.BlockSpec(memory_space=pl.ANY)
low = jnp.bfloat16
wide = jnp.float32


def dot(left, right):
    return lax.dot_general(left, right, (((1,), (0,)), ((), ())), preferred_element_type=wide)


def dot_t(left, right):
    return lax.dot_general(left, right, (((1,), (1,)), ((), ())), preferred_element_type=wide)


def t_dot(left, right):
    return lax.dot_general(left, right, (((0,), (0,)), ((), ())), preferred_element_type=wide)


def exact_dot(left, right):
    return jnp.dot(left, right, precision=highest, preferred_element_type=wide)


def inverse_rms(rows):
    return lax.rsqrt(jnp.mean(rows * rows, axis=-1, keepdims=True) + norm_epsilon)


def norm_back(rows, gain, grad):
    inverse = inverse_rms(rows)
    scaled = gain * grad
    inner = jnp.mean(scaled * rows, axis=-1, keepdims=True)
    grad_rows = inverse * scaled - rows * (inverse * inverse * inverse) * inner
    return grad_rows, jnp.sum(grad * rows * inverse, axis=0, keepdims=True)


def tensor_peer(bit):
    return (lax.axis_index("dp"), lax.axis_index("tensor") ^ bit)


def dp_peer(bit):
    return (lax.axis_index("dp") ^ bit, lax.axis_index("tensor"))


def piece_index(rank, order):
    return sum(((rank >> bit) & 1) << (len(order) - 1 - k) for k, bit in enumerate(order))


class Weights(NamedTuple):
    query_self: object
    key_self: object
    value_self: object
    output_self: object
    query_cross: object
    key_cross: object
    value_cross: object
    output_cross: object
    hidden_in: object
    hidden_out: object


def layer_kernel(cfg, names, *refs):
    a = SimpleNamespace(**dict(zip(names, refs, strict=True)))
    seq, enc_len, slots, width = cfg.seq, cfg.enc_len, cfg.slots, cfg.width
    heads, levels, in_kernel = cfg.heads, cfg.levels, cfg.in_kernel
    inner = heads * HD
    if in_kernel:
        a.lands = [getattr(a, "land%d" % i) for i in range(levels)]
        a.holds = [getattr(a, "hold%d" % i) for i in range(levels - 1)]
    chunks = slots // CHUNK_SLOTS
    chunk_rows = CHUNK_SLOTS * seq
    half_rows = chunk_rows // 2
    half_width = width // 2
    quarter_width = width // 4
    me = lax.axis_index("tensor")
    core = lax.rem(me, 2)
    y = me // 2
    dp_me = lax.axis_index("dp")
    c_peer, y_peer = tensor_peer(1), tensor_peer(2)

    def rows_of(k, count):
        return pl.ds(pl.multiple_of(k * count, count), count)

    def load(index, src, dst):
        return pltpu.make_async_copy(src, dst, a.load_sem.at[index])

    inner_rows = slice(0, inner), slice(inner, 2 * inner)
    first_rows, later_rows = pl.ds(0, chunk_rows), pl.ds(chunk_rows, slots * seq - chunk_rows)
    load_x = load(0, a.inputs.at[first_rows], a.x.at[first_rows])
    load_more = load(2 + len(Weights._fields), a.inputs.at[later_rows], a.x.at[later_rows])
    load_g = load(1, a.out_grad, a.g3)
    spots = {name: getattr(a, "w_" + name) for name in Weights._fields if hasattr(a, "w_" + name)}
    spots.update(key_cross=a.w_kv.at[inner_rows[0]], value_cross=a.w_kv.at[inner_rows[1]])
    loads = Weights(
        *(load(2 + i, getattr(a, name), spots[name]) for i, name in enumerate(Weights._fields))
    )
    loads.key_cross.start()
    loads.value_cross.start()
    load_x.start()
    for copy in loads[:4]:
        copy.start()
    load_more.start()

    barrier = pltpu.get_barrier_semaphore()
    peers = [c_peer, y_peer] + [dp_peer(1 << k) for k in range(levels)]
    for peer in peers:
        pl.semaphore_signal(barrier, inc=1, device_id=peer, device_id_type=MESH)

    def remote(src, dst, sems, index, peer):
        return pltpu.make_async_remote_copy(
            src_ref=src,
            dst_ref=dst,
            send_sem=sems.at[(0,) + index],
            recv_sem=sems.at[(1,) + index],
            device_id=peer,
            device_id_type=MESH,
        )

    def peer_weights():
        own, theirs = pl.ds(0, 2 * inner), pl.ds(2 * inner, 2 * inner)
        return remote(a.w_kv.at[own], a.w_kv.at[theirs], a.kv_sem, (0,), y_peer)

    def enc_copy(slot, buffer):
        rows = pl.ds(pl.multiple_of(slot * enc_len, enc_len), enc_len)
        target = a.enc.at[rows_of(buffer, enc_len)]
        return pltpu.make_async_copy(a.encoded.at[rows], target, a.enc_sem.at[buffer])

    enc_copy(0, 0).start()
    for copy in (loads.query_cross, loads.output_cross, loads.hidden_in, loads.hidden_out, load_g):
        copy.start()

    loads.key_cross.wait()
    loads.value_cross.wait()
    pl.semaphore_wait(barrier, len(peers))
    peer_weights().start()

    gain_self, gain_cross, gain_ffn = (
        ref[...].reshape(1, width) for ref in (a.gain_self, a.gain_cross, a.gain_ffn)
    )

    lane = lax.broadcasted_iota(jnp.int32, (1, inner), 1)
    masks = [jnp.where(lane // HD == h, 1.0, 0.0).astype(wide) for h in range(heads)]
    masks_low = [m.astype(low) for m in masks]
    row_i = lax.broadcasted_iota(jnp.int32, (seq, seq), 0)
    col_i = lax.broadcasted_iota(jnp.int32, (seq, seq), 1)
    bucket = lax.broadcasted_iota(jnp.int32, (a.table_in.shape[1], seq), 0)
    chosen = jnp.where(a.buckets[...] == bucket, 1.0, 0.0).astype(wide)
    per_dist = exact_dot(a.table_in[...], chosen)
    backward = jnp.where((row_i + col_i) % seq == 0, 1.0, 0.0).astype(wide)
    lines = exact_dot(per_dist, backward)
    for h in range(heads):
        line = jnp.broadcast_to(lines[h : h + 1, :], (seq, seq))
        turned = pltpu.roll(line, 0, 1, stride=1, stride_axis=0)
        a.bias[h * seq : (h + 1) * seq, :] = jnp.where(row_i >= col_i, turned, masked_score)
    a.table[...] = jnp.zeros_like(a.table)
    a.small[...] = jnp.zeros_like(a.small)

    def stack(rows):
        return jnp.concatenate([rows * m for m in masks_low], axis=0)

    def unstack(rows):
        return sum(rows[h * seq : (h + 1) * seq] * masks[h] for h in range(heads))

    def softmax(scores):
        peak = jnp.max(scores, axis=-1, keepdims=True)
        terms = jnp.exp(scores - peak)
        return (terms / jnp.sum(terms, axis=-1, keepdims=True)).astype(low)

    def own_rows(k):
        return pl.ds(pl.multiple_of(k * chunk_rows + core * half_rows, half_rows), half_rows)

    def other_rows(k):
        return pl.ds(pl.multiple_of(k * chunk_rows + (1 - core) * half_rows, half_rows), half_rows)

    def add_gain(index, value):
        a.small[index : index + 1, :] += value

    def near_copy(p, k):
        return remote(a.part.at[other_rows(k)], a.near.at[k], a.near_sem, (p, k), c_peer)

    main_rows = pl.ds(0, MAIN_ROWS)

    def pack_tail(rows):
        tail = rows[MAIN_ROWS : MAIN_ROWS + TAIL_ROWS]
        lanes = TILE[1]
        parts = [
            tail[r : r + 1, c * lanes : (c + 1) * lanes]
            for r in range(TAIL_ROWS)
            for c in range(rows.shape[1] // lanes)
        ]
        parts.append(jnp.zeros((TILE[0] - len(parts), lanes), wide))
        return jnp.concatenate(parts, axis=0).astype(low)

    def unpack_rows(main, tile, columns):
        tile = tile.astype(wide)
        each = columns // TILE[1]
        rest = half_rows - MAIN_ROWS
        spot = lax.broadcasted_iota(jnp.int32, (rest, columns), 0)
        block = jnp.zeros((rest, columns), wide)
        for r in range(TAIL_ROWS):
            line = jnp.concatenate(
                [tile[r * each + c : r * each + c + 1] for c in range(each)], axis=1
            )
            block = jnp.where(spot == r, jnp.broadcast_to(line, (rest, columns)), block)
        return jnp.concatenate([main.astype(wide), block], axis=0)

    def far_copies(p, k):
        return (
            remote(
                a.mine.at[k, main_rows], a.far.at[p % 2, k, main_rows], a.far_sem, (p, k), y_peer
            ),
            remote(a.tail_send.at[k], a.tail_far.at[p % 2, k], a.tail_sem, (p, k), y_peer),
        )

    def y_send(p, k):
        near_copy(p, k).wait()
        term = a.part[own_rows(k)].astype(wide) + a.near[k].astype(wide)
        a.mine[k] = term.astype(low)
        a.tail_send[k] = pack_tail(term)
        for copy in far_copies(p, k):
            copy.start()

    def last_copies(k):
        return (
            remote(
                a.mine.at[k, main_rows, pl.ds(0, half_width)],
                a.far.at[0, k, main_rows, pl.ds(0, half_width)],
                a.far_sem,
                (4, k),
                y_peer,
            ),
            remote(a.tail_send.at[k], a.tail_far.at[0, k], a.tail_sem, (4, k), y_peer),
            remote(a.inner_send.at[k], a.inner_far.at[k], a.inner_sem, (k,), y_peer),
        )

    def y_send_last(k):
        near_copy(4, k).wait()
        term = a.part[own_rows(k)].astype(wide) + a.near[k].astype(wide)
        a.h1[k] = term
        rows = a.x[own_rows(k)].astype(wide)
        product = term * rows
        row_inner = jnp.sum(product * gain_self, axis=-1, keepdims=True)
        add_gain(0, jnp.sum(product * inverse_rms(rows), axis=0, keepdims=True))
        a.inner_send[k] = jnp.broadcast_to(row_inner, (half_rows, half_rows)).T[:8]
        away = jnp.where(y == 0, term[:, half_width:], term[:, :half_width])
        a.mine[k, :, :half_width] = away.astype(low)
        a.tail_send[k] = pack_tail(away)
        for copy in last_copies(k):
            copy.start()

    def total(p, k):
        for copy in far_copies(p, k):
            copy.wait()
        far = unpack_rows(a.far[p % 2, k, :MAIN_ROWS], a.tail_far[p % 2, k], width)
        return a.mine[k].astype(wide) + far

    def share_copy(p, k, buffer):
        return remote(buffer.at[own_rows(k)], buffer.at[own_rows(k)], a.share_sem, (p, k), c_peer)

    def each_chunk(body):
        def step(k, carry):
            body(k)
            return carry

        lax.fori_loop(0, chunks, step, 0)

    def phase(p, finish, buffer, compute, extra=None, send=None):
        send = send or functools.partial(y_send, p)

        def begin(k):
            finish(k, total(p - 1, k))
            share_copy(p, k, buffer).start()

        def body(k):
            share_copy(p, k, buffer).wait()

            @pl.when(k + 1 < chunks)
            def _():
                begin(k + 1)

            compute(k)
            near_copy(p, k).start()

            @pl.when(k > 0)
            def _():
                send(k - 1)

            if extra is not None:
                extra(k)

        begin(0)
        each_chunk(body)
        send(chunks - 1)

    def project(slot, buffer):
        enc_copy(slot, buffer).wait()

        @pl.when(slot + 1 < slots)
        def _():
            enc_copy(slot + 1, 1 - buffer).start()

        rows = rows_of(slot, enc_len)
        a.k2[rows] = dot_t(a.enc[rows_of(buffer, enc_len)], a.w_kv[:inner]).astype(low)
        a.v2[rows] = dot_t(a.enc[rows_of(buffer, enc_len)], a.w_kv[inner : 2 * inner]).astype(low)

    def self_forward(k):
        rows = rows_of(k, chunk_rows)
        x = a.x[rows].astype(wide)
        normed = (x * inverse_rms(x) * gain_self).astype(low)
        a.n1[rows] = normed
        query = dot_t(normed, a.w_query_self[...]).astype(low)
        keys = dot_t(normed, a.w_key_self[...]).astype(low)
        values = dot_t(normed, a.w_value_self[...]).astype(low)
        a.q1[rows], a.k1[rows], a.v1[rows] = query, keys, values
        parts = [slice(s * seq, (s + 1) * seq) for s in range(CHUNK_SLOTS)]
        scores = [dot_t(stack(query[part]), keys[part]) + a.bias[...] for part in parts]
        weights = [softmax(score) for score in scores]
        mixed = []
        for s, part in enumerate(parts):
            a.soft1[k * CHUNK_SLOTS + s] = weights[s]
            mixed.append(unstack(dot(weights[s], values[part])).astype(low))
        mixed = jnp.concatenate(mixed, axis=0)
        a.o1[rows] = mixed
        a.part[rows] = dot(mixed, a.w_output_self[...]).astype(low)

    load_x.wait()
    for copy in loads[:4]:
        copy.wait()

    def phase_zero(k):
        @pl.when(k == 1)
        def _():
            load_more.wait()

        self_forward(k)
        near_copy(0, k).start()
        y_send(0, k)
        project(CHUNK_SLOTS * k, 0)
        project(CHUNK_SLOTS * k + 1, 1)

    each_chunk(phase_zero)
    loads.query_cross.wait()
    loads.output_cross.wait()
    peer_weights().wait()

    chip_slots = slots // 2

    def chip_slot(k):
        return chip_slots * y + k

    enc_copy(chip_slot(0), 0).start()

    def project_peer(k):
        buffer = lax.rem(k, 2)
        enc_copy(chip_slot(k), buffer).wait()

        @pl.when(k + 1 < chip_slots)
        def _():
            enc_copy(chip_slot(k + 1), 1 - buffer).start()

        rows = rows_of(k, enc_len)
        encoded = a.enc[rows_of(buffer, enc_len)]
        a.k2_peer[rows] = dot_t(encoded, a.w_kv[2 * inner : 3 * inner]).astype(low)
        a.v2_peer[rows] = dot_t(encoded, a.w_kv[3 * inner :]).astype(low)

    def finish_one(k, term):
        hidden = a.x[own_rows(k)].astype(wide) + term
        a.h1[k] = hidden
        a.n2[own_rows(k)] = (hidden * inverse_rms(hidden) * gain_cross).astype(low)

    def cross_forward(k):
        rows = rows_of(k, chunk_rows)
        query = dot_t(a.n2[rows], a.w_query_cross[...]).astype(low)
        a.q2[rows] = query
        slots_here = [k * CHUNK_SLOTS + s for s in range(CHUNK_SLOTS)]
        enc_parts = [rows_of(slot, enc_len) for slot in slots_here]
        scores = [
            dot_t(stack(query[s * seq : (s + 1) * seq]), a.k2[enc_rows])
            for s, enc_rows in enumerate(enc_parts)
        ]
        weights = [softmax(score) for score in scores]
        mixed = []
        for s, slot in enumerate(slots_here):
            a.soft2[slot] = weights[s]
            mixed.append(unstack(dot(weights[s], a.v2[enc_parts[s]])).astype(low))
        mixed = jnp.concatenate(mixed, axis=0)
        a.o2[rows] = mixed
        a.part[rows] = dot(mixed, a.w_output_cross[...]).astype(low)

    phase(1, finish_one, a.n2, cross_forward, project_peer)
    for copy in (loads.hidden_in, loads.hidden_out, load_g):
        copy.wait()

    def limit(slot):
        return jnp.where(slot < a.counts[0], a.lengths[slot], 0)

    def keep_rows(slot, rows):
        pos = lax.broadcasted_iota(jnp.int32, (seq, 1), 0)
        return jnp.where(pos < limit(slot), rows, 0.0)

    def finish_two(k, term):
        hidden = a.h1[k] + term
        a.h2[k] = hidden
        a.n3[own_rows(k)] = (hidden * inverse_rms(hidden) * gain_ffn).astype(low)

    def out_near_copy(k):
        return remote(a.out_part.at[k % 2, 1 - core], a.out_near.at[k], a.out_near_sem, (k,), c_peer)

    def out_far_copies(k):
        return (
            remote(
                a.out_mine.at[k, main_rows],
                a.out_far.at[k, main_rows],
                a.out_far_sem,
                (0, k),
                y_peer,
            ),
            remote(a.out_tail_send.at[k], a.out_tail_far.at[k], a.out_far_sem, (1, k), y_peer),
        )

    def my_half(value):
        return jnp.where(y == 0, value[:, :half_width], value[:, half_width:])

    def other_half(value):
        return jnp.where(y == 0, value[:, half_width:], value[:, :half_width])

    def out_gather(k):
        out_near_copy(k).wait()
        term = a.out_part[k % 2, core].astype(wide) + a.out_near[k].astype(wide)
        away = other_half(term)
        a.out_mine[k] = away.astype(low)
        a.out_tail_send[k] = pack_tail(away)
        a.out_keep[k] = my_half(term) + my_half(a.h2[k])

    scale = 0.7978845608028654

    def feed_forward(k):
        rows = rows_of(k, chunk_rows)
        grad = jnp.concatenate(
            [
                keep_rows(k * CHUNK_SLOTS + s, a.g3[rows_of(k * CHUNK_SLOTS + s, seq)].astype(wide))
                for s in range(CHUNK_SLOTS)
            ],
            axis=0,
        ).astype(low)
        a.g3[rows] = grad
        a.pre[...] = dot(a.n3[rows], a.w_hidden_in[...])

        def gelu_rows(i, carry):
            part = rows_of(i, GELU_ROWS)
            pre = a.pre[part]
            square = pre * pre
            bend = jnp.tanh(scale * pre * (1.0 + 0.044715 * square))
            half = 0.5 * (1.0 + bend)
            curve = scale * (1.0 + 3 * 0.044715 * square)
            a.pre[part] = half + 0.5 * pre * (1.0 - bend * bend) * curve
            target = pl.ds(pl.multiple_of(k * chunk_rows + i * GELU_ROWS, GELU_ROWS), GELU_ROWS)
            a.act[target] = (pre * half).astype(low)
            return carry

        lax.fori_loop(0, chunk_rows // GELU_ROWS, gelu_rows, 0)
        out = dot_t(a.act[rows], a.w_hidden_out[...]).astype(low)
        a.out_part[k % 2, 0] = out[:half_rows]
        a.out_part[k % 2, 1] = out[half_rows:]
        out_near_copy(k).start()
        grad_pre = (a.pre[...] * dot(grad, a.w_hidden_out[...])).astype(low)
        a.d_pre[rows] = grad_pre
        a.part[rows] = dot_t(grad_pre, a.w_hidden_in[...]).astype(low)

    phase(2, finish_two, a.n3, feed_forward, out_gather)

    def column_copy(which, k):
        return remote(
            a.col_send.at[which, k],
            a.columns.at[which, :, own_rows(k)],
            a.col_sem,
            (which, k),
            c_peer,
        )

    def emit_columns(which, k, value):
        value = value.T
        left, right = value[:quarter_width], value[quarter_width:]
        first = core == 0
        a.columns[which, :, own_rows(k)] = jnp.where(first, left, right).astype(low)
        a.col_send[which, k] = jnp.where(first, right, left).astype(low)
        column_copy(which, k).start()

    def finish_out(k):
        for copy in out_far_copies(k):
            copy.wait()
        far = unpack_rows(a.out_far[k, :MAIN_ROWS], a.out_tail_far[k], half_width)
        value = a.out_keep[k] + far
        emit_columns(0, k, keep_rows(k * CHUNK_SLOTS + core, value))

    orders = (tuple(range(levels)), (1, 0) + tuple(range(2, levels)))

    def dp_rank(half, level):
        return (dp_me >> orders[half][level]) & 1

    def dp_copy(block, half, level):
        buffer = block % 2
        count = 1 << (levels - 1 - level)
        source = a.term if level == 0 else a.holds[level - 1]
        part = pl.ds((1 - dp_rank(half, level)) * count, count)
        return remote(
            source.at[buffer, half, part],
            a.lands[level].at[buffer, half],
            a.dp_sem,
            (block, half, level),
            dp_peer(1 << orders[half][level]),
        )

    def raw_copy(block):
        return pltpu.make_async_copy(
            a.term.at[block % 2], a.raw_grads.at[block], a.dp_sem.at[0, block, 0, 0]
        )

    def credit_wait(block, half, level):
        pl.semaphore_wait(a.credit_sem.at[block % 2, half, level], 1)

    def dp_begin(block, halves=(0, 1)):
        if in_kernel:
            for half in halves:
                if block >= 2:
                    credit_wait(block, half, 0)
                dp_copy(block, half, 0).start()
        elif 1 in halves:
            raw_copy(block).start()

    def dp_advance(block, level, halves=(0, 1)):
        if not in_kernel:
            return
        buffer = block % 2
        count = 1 << (levels - 1 - level)
        for half in halves:
            dp_copy(block, half, level).wait()
            source = a.term if level == 0 else a.holds[level - 1]
            part = pl.ds(dp_rank(half, level) * count, count)
            value = source[buffer, half, part].astype(wide)
            value += a.lands[level][buffer, half].astype(wide)
            if level == levels - 1:
                emit_grads(block, half, value[0])
            else:
                a.holds[level][buffer, half] = value.astype(low)
            if block < 2:
                pl.semaphore_signal(
                    a.credit_sem.at[buffer, half, level],
                    inc=1,
                    device_id=dp_peer(1 << orders[half][level]),
                    device_id_type=MESH,
                )
            if level + 1 < levels:
                if block >= 2:
                    credit_wait(block, half, level + 1)
                dp_copy(block, half, level + 1).start()

    def at_chunk(k, step, *moves):
        @pl.when(k == step)
        def _():
            for move in moves:
                dp_advance(*move)

    def dp_finish_raw(block):
        if not in_kernel:
            raw_copy(block).wait()

    def grad_store(index):
        if index < 8:
            source, target = a.held.at[index], getattr(a, "grad_" + Weights._fields[index])
        else:
            block, half = divmod(index - 8, 2)
            source = a.held_wide.at[block, half]
            target = (a.grad_hidden_out, a.grad_hidden_in)[block]
            target = target.at[:, pl.ds(half * half_width, half_width)]
        return pltpu.make_async_copy(source, target, a.grad_sem.at[index])

    def emit_grads(block, half, value):
        if block < 2:
            a.held_wide[block, half] = value
            grad_store(8 + 2 * block + half).start()
        else:
            start = (4 if block == 2 else 0) + 2 * half
            for i in range(2):
                a.held[start + i] = value[:, i * inner : (i + 1) * inner]
                grad_store(start + i).start()

    piece = cfg.piece
    groups = 2
    group_rows = width // groups
    pieces_each = max(group_rows // piece, 1) if in_kernel else 1

    def store_pieces(block, g, rows):
        if in_kernel:
            for i in range(pieces_each):
                for gg in range(groups):
                    if gg != g:
                        continue
                    for half in range(2):
                        index = piece_index(gg * pieces_each + i, orders[half])
                        a.term[block % 2, half, index] = rows[
                            i * piece : (i + 1) * piece,
                            half * half_width : (half + 1) * half_width,
                        ]
        else:
            a.term[block % 2, g * group_rows : (g + 1) * group_rows] = rows

    def plain_grads(block, left, right):
        for g in range(groups):
            columns = slice(g * group_rows, (g + 1) * group_rows)
            store_pieces(block, g, t_dot(left[:, columns], right[...]).astype(low))

    def turned_grads(block, half):
        value = a.enc[half * 2 * inner : (half + 1) * 2 * inner].T
        columns = slice(half * half_width, (half + 1) * half_width)
        if in_kernel:
            for i in range(width // piece):
                index = piece_index(i, orders[half])
                a.term[block % 2, half, index] = value[i * piece : (i + 1) * piece]
        else:
            a.term[block % 2, :, columns] = value

    def turned_rows(i):
        return slice(i * inner, (i + 1) * inner)

    plain_grads(0, a.g3, a.act)
    dp_begin(0)
    plain_grads(1, a.n3, a.d_pre)
    dp_begin(1)

    def finish_three(k, term):
        grad_rows, grad_gain = norm_back(a.h2[k], gain_ffn, term)
        add_gain(2, grad_gain)
        grad = a.g3[own_rows(k)].astype(wide) + grad_rows
        a.dh[k] = grad
        a.dh2[own_rows(k)] = grad.astype(low)

    def inner_by_head(grad_mixed, mixed):
        product = grad_mixed.astype(wide) * mixed.astype(wide)
        return [jnp.sum(product * m, axis=-1, keepdims=True) for m in masks]

    def score_back(soft, grad_soft, row_inner):
        return (soft.astype(wide) * (grad_soft - row_inner)).astype(low)

    def cross_backward(k):
        rows = rows_of(k, chunk_rows)
        grad_mixed = dot_t(a.dh2[rows], a.w_output_cross[...]).astype(low)
        inners = inner_by_head(grad_mixed, a.o2[rows])
        a.pair[rows, inner:] = grad_mixed
        a.pair[rows, :inner] = a.q2[rows]
        query = a.q2[rows]
        parts = [slice(s * seq, (s + 1) * seq) for s in range(CHUNK_SLOTS)]
        slots_here = [k * CHUNK_SLOTS + s for s in range(CHUNK_SLOTS)]
        enc_parts = [rows_of(slot, enc_len) for slot in slots_here]
        tall_grads = [stack(grad_mixed[part]) for part in parts]
        tall_queries = [stack(query[part]) for part in parts]
        grad_softs = [dot_t(tall_grads[s], a.v2[enc_parts[s]]) for s in range(CHUNK_SLOTS)]
        softs = [a.soft2[slot] for slot in slots_here]
        grad_scores = [
            score_back(
                softs[s],
                grad_softs[s],
                jnp.concatenate([column[part] for column in inners], axis=0),
            )
            for s, part in enumerate(parts)
        ]
        grads = [
            unstack(dot(grad_scores[s], a.k2[enc_parts[s]])).astype(low) for s in range(CHUNK_SLOTS)
        ]
        for s, slot in enumerate(slots_here):
            a.dkv[slot, :inner] = t_dot(tall_queries[s], grad_scores[s]).astype(low)
            a.dkv[slot, inner:] = t_dot(tall_grads[s], softs[s]).astype(low)
        grads = jnp.concatenate(grads, axis=0)
        a.d_pre[rows, :inner] = grads
        a.part[rows] = dot(grads, a.w_query_cross[...]).astype(low)

    kv_blocks = 2 * inner // half_rows
    a.pre[...] = jnp.zeros_like(a.pre)

    def kv_part(i):
        if i == kv_blocks - 1:
            return a.h2.at[0]
        return a.pre.at[slice(i * half_rows, (i + 1) * half_rows)]

    def add_kv(slot, buffer):
        value = dot(a.dkv[slot], a.enc[rows_of(buffer, enc_len)])
        for i in range(kv_blocks):
            kv_part(i)[...] += value[i * half_rows : (i + 1) * half_rows]

    def kv_chunk(k):
        @pl.when(k == 0)
        def _():
            a.h2[0] = jnp.zeros_like(a.h2[0])

        for i in range(2):
            enc_copy(2 * k + i, i).wait()
            add_kv(2 * k + i, i)

            @pl.when(k + 1 < chunks)
            def _():
                enc_copy(2 * k + 2 + i, i).start()

        at_chunk(k, 2, (0, 0))
        at_chunk(k, 3, (1, 0))

    enc_copy(0, 0).start()
    enc_copy(1, 1).start()
    phase(3, finish_three, a.dh2, cross_backward, kv_chunk)

    peer_copy = remote(
        a.pair.at[rows_of(1 - y, chip_slots * seq)], a.pair_peer, a.peer_sem, (0,), y_peer
    )
    peer_copy.start()
    a.enc[turned_rows(0)] = t_dot(a.d_pre[:, :inner], a.n2[...]).astype(low)
    for i in range(kv_blocks):
        a.enc[inner + i * half_rows : inner + (i + 1) * half_rows] = kv_part(i)[...].astype(low)
    a.enc[turned_rows(3)] = t_dot(a.o2[...], a.dh2[...]).astype(low)
    dp_finish_raw(0)
    for half in range(2):
        turned_grads(2, half)
    dp_advance(0, 1)
    dp_begin(2)

    def finish_four(k, term):
        grad_rows, grad_gain = norm_back(a.h1[k], gain_cross, term)
        add_gain(1, grad_gain)
        grad = a.dh[k] + grad_rows
        a.dh[k] = grad
        a.dh1[own_rows(k)] = grad.astype(low)

    def self_backward(k):
        rows = rows_of(k, chunk_rows)
        grad_mixed = dot_t(a.dh1[rows], a.w_output_self[...]).astype(low)
        inners = inner_by_head(grad_mixed, a.o1[rows])
        query, keys, values = a.q1[rows], a.k1[rows], a.v1[rows]
        parts = [slice(s * seq, (s + 1) * seq) for s in range(CHUNK_SLOTS)]
        tall_grads = [stack(grad_mixed[part]) for part in parts]
        tall_queries = [stack(query[part]) for part in parts]
        softs = [a.soft1[k * CHUNK_SLOTS + s] for s in range(CHUNK_SLOTS)]
        grad_softs = [dot_t(tall_grads[s], values[part]) for s, part in enumerate(parts)]
        grad_scores = [
            score_back(
                softs[s],
                grad_softs[s],
                jnp.concatenate([column[part] for column in inners], axis=0),
            )
            for s, part in enumerate(parts)
        ]
        a.table[...] += sum(g.astype(wide) for g in grad_scores)
        grads = [
            [unstack(dot(grad_scores[s], keys[part])).astype(low) for s, part in enumerate(parts)],
            [t_dot(g, q).astype(low) for g, q in zip(grad_scores, tall_queries, strict=True)],
            [t_dot(w, g).astype(low) for w, g in zip(softs, tall_grads, strict=True)],
        ]
        grads = [jnp.concatenate(g, axis=0) for g in grads]
        a.q1[rows], a.k1[rows], a.v1[rows] = grads
        a.part[rows] = (
            dot(grads[0], a.w_query_self[...])
            + dot(grads[1], a.w_key_self[...])
            + dot(grads[2], a.w_value_self[...])
        ).astype(low)

    def self_moves(k):
        at_chunk(k, 1, (1, 1))
        at_chunk(k, 2, (0, 2))
        at_chunk(k, 3, (2, 0))

    phase(4, finish_four, a.dh1, self_backward, self_moves, y_send_last)
    for k in range(chunks):
        for copy in out_far_copies(k):
            copy.start()
    mirror = jnp.where(row_i + col_i == seq - 1, 1.0, 0.0).astype(wide)
    for h in range(heads):
        flipped = exact_dot(a.table[h * seq : (h + 1) * seq, :], mirror)
        turned = pltpu.roll(flipped, 0, 1, stride=1, stride_axis=0)
        a.small[3:4, h * seq : (h + 1) * seq] = jnp.sum(turned, axis=0, keepdims=True)

    hops = [dp_peer(1 << k) for k in range(levels)] + [c_peer, y_peer]
    row = lax.broadcasted_iota(jnp.int32, a.small.shape, 0)

    def small_copy(i):
        return remote(a.small, a.small_land.at[i], a.small_sem, (i,), hops[i])

    def small_step(i):
        small_copy(i).wait()
        summed = row < (8 if i < levels else 3 if i == levels else 1)
        a.small[...] += jnp.where(summed, a.small_land[i], 0.0)
        if i < levels + 1:
            small_copy(i + 1).start()

    small_copy(0).start()
    a.enc[turned_rows(0)] = t_dot(a.q1[...], a.n1[...]).astype(low)
    a.enc[turned_rows(1)] = t_dot(a.k1[...], a.n1[...]).astype(low)
    dp_finish_raw(1)
    turned_grads(3, 0)
    dp_begin(3, (0,))
    a.enc[turned_rows(2)] = t_dot(a.v1[...], a.n1[...]).astype(low)
    a.enc[turned_rows(3)] = t_dot(a.o1[...], a.dh1[...]).astype(low)
    turned_grads(3, 1)
    dp_begin(3, (1,))
    small_step(0)
    dp_advance(2, 1)
    peer_copy.wait()

    def enc_partial(k):
        rows = rows_of(k, seq)
        enc_rows = rows_of(k, enc_len)
        pair = a.pair_peer[rows]
        tall_query, tall_grad = stack(pair[:, :inner]), stack(pair[:, inner:])
        soft = softmax(dot_t(tall_query, a.k2_peer[enc_rows]))
        grad_soft = dot_t(tall_grad, a.v2_peer[enc_rows])
        row_inner = jnp.sum(soft.astype(wide) * grad_soft, axis=-1, keepdims=True)
        grad_scores = score_back(soft, grad_soft, row_inner)
        peer_grads = jnp.concatenate(
            [t_dot(tall_query, grad_scores).astype(low), t_dot(tall_grad, soft).astype(low)], axis=0
        )
        own = t_dot(a.dkv[chip_slot(k)], a.w_kv[: 2 * inner])
        return own + t_dot(peer_grads, a.w_kv[2 * inner :])

    enc_each = chip_slots // 2

    def enc_near_copy(j):
        rows = rows_of(j, enc_len)
        return remote(a.n3.at[rows], a.act.at[rows], a.enc_near_sem, (j,), c_peer)

    def enc_give(j, carry):
        at_chunk(j, 1, (1, 2), (3, 0, (0,)))
        a.n3[rows_of(j, enc_len)] = enc_partial((1 - core) * enc_each + j).astype(low)
        enc_near_copy(j).start()
        return carry

    def enc_keep(j, carry):
        at_chunk(j, 0, (3, 0, (1,)))
        at_chunk(j, 1, (3, 1, (0,)))
        partial = enc_partial(core * enc_each + j)
        enc_near_copy(j).wait()
        rows = rows_of(j, enc_len)
        a.d_pre[rows] = (partial + a.act[rows].astype(wide)).astype(low)
        return carry

    lax.fori_loop(0, enc_each, enc_give, 0)
    small_step(1)
    lax.fori_loop(0, enc_each, enc_keep, 0)
    dp_advance(3, 1, (1,))
    for i in range(2, levels):
        small_step(i)
    store_enc = load(2, a.d_pre, a.encoded_grad)
    store_enc.start()

    def phase_five(k):
        for copy in last_copies(k):
            copy.wait()
        rows = my_half(a.x[own_rows(k)]).astype(wide)
        inverse = inverse_rms(a.x[own_rows(k)].astype(wide))
        sums = (a.inner_send[k] + a.inner_far[k])[:1]
        row_inner = jnp.broadcast_to(sums, (half_rows, half_rows)).T[:, :1] * (1.0 / width)
        far = unpack_rows(a.far[0, k, :MAIN_ROWS, :half_width], a.tail_far[0, k], half_width)
        term = my_half(a.h1[k]) + far
        grad_rows = inverse * my_half(gain_self) * term
        grad_rows -= rows * (inverse * inverse * inverse) * row_inner
        emit_columns(1, k, my_half(a.dh[k]) + grad_rows)

    each_chunk(phase_five)
    dp_advance(2, 2)
    small_step(levels)
    each_chunk(finish_out)
    for k in range(chunks):
        column_copy(0, k).wait()
        column_copy(1, k).wait()
    stores = [
        load(0, a.columns.at[0], a.layer_out),
        load(1, a.columns.at[1], a.input_grad),
    ]
    for store in stores:
        store.start()
    dp_advance(3, 2)
    small_step(levels + 1)
    dp_finish_raw(2)
    dp_finish_raw(3)
    a.small_out[...] = a.small[...]
    for store in (*stores, store_enc):
        store.wait()
    if in_kernel:
        for index in range(12):
            grad_store(index).wait()


def finish_kernel(count, heads, seq, *refs):
    small, buckets = refs[count], refs[count + 1]
    targets, held, sems = refs[count + 2 : 2 * count + 6], refs[2 * count + 6 : -1], refs[-1]
    parts = []
    for i in range(count):
        cuts = 1
        rows = refs[i].shape[0] // cuts
        parts += [(i, pl.ds(c * rows, rows)) for c in range(cuts)]
    copies = [
        pltpu.make_async_copy(refs[i].at[rows], held[i].at[rows], sems.at[n])
        for n, (i, rows) in enumerate(parts)
    ]
    for copy in copies:
        copy.start()
    for n, (i, rows) in enumerate(parts):
        copies[n].wait()
        copies[n] = pltpu.make_async_copy(held[i].at[rows], targets[i].at[rows], sems.at[n])
        copies[n].start()
    for i in range(3):
        targets[count + i][...] = small[i, :]
    sums = jnp.concatenate([small[3:4, h * seq : (h + 1) * seq] for h in range(heads)], axis=0)
    by_lane = pltpu.roll(jnp.broadcast_to(buckets[...], (8, seq)), seq - 1, 1)[:1]
    kinds = targets[count + 3].shape[1]
    bucket = lax.broadcasted_iota(jnp.int32, (kinds, seq), 0)
    chosen = jnp.where(by_lane == bucket, 1.0, 0.0).astype(wide)
    targets[count + 3][...] = lax.dot_general(
        sums,
        chosen,
        (((1,), (1,)), ((), ())),
        precision=highest,
        preferred_element_type=wide,
    )
    for copy in copies:
        copy.wait()


def per_device(*args):
    (
        inputs,
        encoded,
        example_counts,
        lengths,
        buckets,
        gain_self,
        gain_cross,
        gain_ffn,
        bias_table,
    ) = args[:9]
    weights = args[9:19]
    out_grad = args[19]
    rows, width = inputs.shape
    seq = buckets.shape[0]
    slots = lengths.shape[0]
    enc_rows = encoded.shape[0]
    enc_len = enc_rows // slots
    inner = weights[0].shape[1]
    hidden = weights[8].shape[1]
    heads = inner // HD
    dp_count = lax.axis_size("dp")
    levels = dp_count.bit_length() - 1
    piece = width // dp_count
    in_kernel = piece % 16 == 0
    chunks = slots // CHUNK_SLOTS
    half = CHUNK_SLOTS * seq // 2

    ins = dict(
        lengths=(lengths, SM),
        counts=(example_counts, SM),
        gain_self=(gain_self, VM),
        gain_cross=(gain_cross, VM),
        gain_ffn=(gain_ffn, VM),
        table_in=(bias_table.T, VM),
        buckets=(buckets[None], VM),
        inputs=(inputs, HBM),
        encoded=(encoded, HBM),
        out_grad=(out_grad, HBM),
    )
    for name, weight in zip(Weights._fields, weights, strict=True):
        ins[name] = (weight, HBM)
    for name in Weights._fields[:8]:
        ins[name] = (ins[name][0].T, HBM)
    shape = jax.ShapeDtypeStruct
    outs = dict(
        layer_out=(shape((width // 4, rows), low), HBM),
        input_grad=(shape((width // 4, rows), low), HBM),
        encoded_grad=(shape((enc_rows // 4, width), low), HBM),
        small_out=(shape((8, width), wide), VM),
    )
    if in_kernel:
        for name, weight in zip(Weights._fields, weights, strict=True):
            outs["grad_" + name] = (shape((piece, weight.shape[1]), wide), HBM)
    else:
        outs.update(raw_grads=(shape((4, width, width), low), HBM))
    vmem, dma = pltpu.VMEM, pltpu.SemaphoreType.DMA
    quarter = width // 4
    whole_rows = vmem((rows, width), low)
    hidden_rows = vmem((rows, hidden), low)
    inner_rows = vmem((rows, inner), low)
    own_wide = vmem((chunks, half, width), wide)
    own_low = vmem((chunks, half, width), low)
    scratch = {
        "w_" + name: vmem(ins[name][0].shape, low)
        for name in Weights._fields
        if name not in Weights._fields[5:7]
    }
    scratch.update(
        x=whole_rows,
        g3=whole_rows,
        enc=vmem((2 * enc_len, width), low),
        n1=whole_rows,
        n2=whole_rows,
        n3=whole_rows,
        dh1=whole_rows,
        dh2=whole_rows,
        part=whole_rows,
        act=hidden_rows,
        d_pre=hidden_rows,
        q1=inner_rows,
        k1=inner_rows,
        v1=inner_rows,
        o1=inner_rows,
        q2=inner_rows,
        o2=inner_rows,
        k2=vmem((enc_rows, inner), low),
        v2=vmem((enc_rows, inner), low),
        h1=own_wide,
        h2=own_wide,
        dh=own_wide,
        soft1=vmem((slots, heads * seq, seq), low),
        soft2=vmem((slots, heads * seq, enc_len), low),
        dkv=vmem((slots, 2 * inner, enc_len), low),
        near=own_low,
        mine=own_low,
        far=vmem((2, chunks, half, width), low),
        out_part=vmem((2, 2, half, width), low),
        out_near=own_low,
        out_mine=vmem((chunks, half, width // 2), low),
        out_keep=vmem((chunks, half, width // 2), wide),
        out_far=vmem((chunks, half, width // 2), low),
        columns=vmem((2, quarter, rows), low),
        col_send=vmem((2, chunks, quarter, half), low),
        w_kv=vmem((4 * inner, width), low),
        k2_peer=vmem((enc_rows // 2, inner), low),
        v2_peer=vmem((enc_rows // 2, inner), low),
        pair=vmem((rows, 2 * inner), low),
        pair_peer=vmem((rows // 2, 2 * inner), low),
        tail_send=vmem((chunks, *TILE), low),
        tail_far=vmem((2, chunks, *TILE), low),
        out_tail_send=vmem((chunks, *TILE), low),
        out_tail_far=vmem((chunks, *TILE), low),
        inner_send=vmem((chunks, 8, half), wide),
        inner_far=vmem((chunks, 8, half), wide),
        pre=vmem((CHUNK_SLOTS * seq, hidden), wide),
        bias=vmem((heads * seq, seq), wide),
        table=vmem((heads * seq, seq), wide),
        small=vmem((8, width), wide),
        small_land=vmem((levels + 2, 8, width), wide),
        load_sem=dma((3 + len(weights),)),
        enc_sem=dma((2,)),
        near_sem=dma((2, 5, chunks)),
        far_sem=dma((2, 5, chunks)),
        share_sem=dma((2, 5, chunks)),
        out_near_sem=dma((2, chunks)),
        out_far_sem=dma((2, 2, chunks)),
        tail_sem=dma((2, 5, chunks)),
        col_sem=dma((2, 2, chunks)),
        enc_near_sem=dma((2, 2)),
        peer_sem=dma((2, 1)),
        kv_sem=dma((2, 1)),
        inner_sem=dma((2, chunks)),
        dp_sem=dma((2, 4, 2, levels)),
        small_sem=dma((2, levels + 2)),
        credit_sem=pltpu.SemaphoreType.REGULAR((2, 2, levels)),
    )
    if in_kernel:
        scratch.update(
            term=vmem((2, 2, dp_count, piece, width // 2), low),
            held=vmem((8, piece, inner), wide),
            held_wide=vmem((2, 2, piece, width // 2), wide),
            grad_sem=dma((12,)),
        )
        for level in range(levels):
            count = 1 << (levels - 1 - level)
            scratch["land%d" % level] = vmem((2, 2, count, piece, width // 2), low)
            if level + 1 < levels:
                scratch["hold%d" % level] = vmem((2, 2, count, piece, width // 2), low)
    else:
        scratch.update(term=vmem((2, width, width), low))
    cfg = SimpleNamespace(
        seq=seq,
        enc_len=enc_len,
        slots=slots,
        width=width,
        heads=heads,
        levels=levels,
        in_kernel=in_kernel,
        piece=piece,
    )
    results = pl.pallas_call(
        functools.partial(layer_kernel, cfg, tuple(ins) + tuple(outs) + tuple(scratch)),
        out_shape=tuple(o[0] for o in outs.values()),
        in_specs=[i[1] for i in ins.values()],
        out_specs=tuple(o[1] for o in outs.values()),
        scratch_shapes=list(scratch.values()),
        compiler_params=pltpu.CompilerParams(
            collective_id=1, has_side_effects=True, vmem_limit_bytes=65000 * 2**10
        ),
    )(*[i[0] for i in ins.values()])
    moved = [i for i, name in enumerate(outs) if name not in ("small_out", "raw_grads")]
    buckets_row = buckets[None]
    kinds = bias_table.shape[0]
    finals = pl.pallas_call(
        functools.partial(finish_kernel, len(moved), heads, seq),
        out_shape=(
            *(shape(results[i].shape, results[i].dtype) for i in moved),
            *(shape((width,), wide) for _ in range(3)),
            shape((heads, kinds), wide),
        ),
        in_specs=[HBM] * len(moved) + [VM, VM],
        out_specs=(HBM,) * len(moved) + (VM,) * 4,
        scratch_shapes=[
            *(vmem(results[i].shape, results[i].dtype) for i in moved),
            dma((4 * len(moved),)),
        ],
    )(*[results[i] for i in moved], results[3], buckets_row)
    if in_kernel:
        grads = finals[3 : len(moved)]
    else:
        raw = results[4]
        parts = [raw[3][:, i * inner : (i + 1) * inner] for i in range(4)]
        parts += [raw[2][:, i * inner : (i + 1) * inner] for i in range(4)]
        grads = [
            lax.psum_scatter(part.astype(wide), "dp", scatter_dimension=0, tiled=True)
            for part in (*parts, raw[1], raw[0])
        ]
    gains = finals[len(moved) : len(moved) + 3]
    return (finals[0].T, finals[1].T, finals[2], *gains, finals[-1].T, *grads)


def solution(mesh):
    columns = P(None, "tensor")
    both = P("dp", "tensor")
    placed = (
        (P("dp", None), P("dp", None), P("dp"), P("dp"), P(), P(), P(), P())
        + (columns,) * 11
        + (P("dp", None),)
    )
    return jax.shard_map(
        per_device,
        mesh=mesh,
        in_specs=placed,
        out_specs=(both, both, P(("dp", "tensor"), None), P(), P(), P(), columns) + (both,) * 10,
        check_vma=False,
    )
```
